512 devices in a mesh: group: 32 (over x_lo, z, core), tensor: 16 (over y, x_hi).
Axes of the slice: x: 4 (x_hi: 2, x_lo: 2; x = x_hi * 2 + x_lo), y: 8, z: 8, core: 2. Of those that a mesh axis runs over, the one named last changes fastest.
Arguments:
- hidden_x: bfloat16 [64, 8, 8192], P('group', None, 'tensor'), may hold values from -6 to 6
- base_weight: bfloat16 [2048, 8192], P(None, 'tensor'), may hold values from -0.0625 to 0.0625
- delta_codes: bfloat16 [2048, 8192], P('group', 'tensor'), may hold values from -4 to 4
- delta_scales: bfloat16 [2048, 64], P('group', 'tensor'), may hold values from 0.0019989014 to 0.019897461
- owner_map: int32 [32], replicated, may hold values from 0 to 31, each once
- kv_cache: bfloat16 [64, 4096, 2048], P('group', 'tensor'), may hold values from -6 to 6
- queries: bfloat16 [64, 8, 8192], P('group'), may hold values from -180 to 180
- lengths: int32 [64], P('group'), may hold values from 1024 to 4096, as said below
Outputs:
- new_kv: bfloat16 [64, 8, 2048], P('group', None, 'tensor')
- attended: bfloat16 [64, 8, 8192], P('group', None, 'tensor')
The draws below stay inside these ranges and needn't reach their ends.
Inputs may be any that keep to these rules, and one draw needn't show every extreme that they name: `owner_map`: a permutation of the shard indices. Row r's entries are its first lengths[r] cache positions; some row is full.
All inputs are finite; a program needn't handle non-finite values.
Results may differ from the reference program's by a relative error of at most 0.009.
Values may be sent and summed in bfloat16 or wider, within the bound.
A program may use at most 64 MiB of HBM per device.

```python
import math
import jax
import jax.numpy as jnp
from jax import lax

D = 8192
H = 64
KVH = 8
HD = 128
BLK = 128
STEPS = 8
CACHE_DEV = 256
CACHE = 4096
ROWS_ALL = 64
OUT = 2048
N_GROUP = 32
N_TENSOR = 16


def anchor_keys(key):
    anchor = jnp.clip(jax.random.normal(jax.random.fold_in(key, 77), (ROWS_ALL, KVH * HD), jnp.float32), -6.0, 6.0)
    anchor = anchor.at[:, 0].set(6.0)
    return anchor.at[:, 1].set(-6.0)


def draw_kv_cache(key, part):
    anchor = anchor_keys(key)
    key = jax.random.fold_in(key, 11)
    base = jnp.clip(jax.random.normal(key, (ROWS_ALL, CACHE, 2 * KVH * HD), jnp.float32), -6.0, 6.0)
    base = base.at[:, 0, :KVH * HD].set(anchor)
    return base.astype(jnp.bfloat16)


def draw_queries(key, part):
    key = jax.random.fold_in(key, 23)
    fresh = jnp.clip(jax.random.normal(key, (ROWS_ALL, STEPS, H * HD), jnp.float32), -6.0, 6.0)
    return fresh.astype(jnp.bfloat16)


def draw_lengths(key, part):
    key = jax.random.fold_in(key, 5)
    values = jax.random.randint(key, (ROWS_ALL,), CACHE // 4, CACHE + 1)
    full_row = jax.random.randint(jax.random.fold_in(key, 6), (), 0, ROWS_ALL)
    values = jnp.where(jnp.arange(ROWS_ALL) == full_row, CACHE, values)
    return values.astype(jnp.int32)


def shard_levels(rng, dims, pieces, smallest, largest):
    def one(axis_at, shards_of):
        draws = jax.random.uniform(jax.random.fold_in(jax.random.fold_in(rng, 6), axis_at), (shards_of,), jnp.float32, smallest / len(pieces), largest / len(pieces))
        return jnp.repeat(jnp.exp(draws), dims[axis_at] // shards_of).reshape((-1,) + (1,) * (len(dims) - axis_at - 1))

    level = one(*pieces[0])
    for cut in pieces[1:]:
        level = level * one(*cut)
    return level


def gaussian(key, shape, spread, reach, shards=(), kind=jnp.bfloat16):
    entries = jax.random.normal(key, shape, jnp.float32) * spread
    if len(shards) > 0:
        entries = shard_levels(key, shape, shards, -0.22, 0.18) * entries
    return jnp.clip(entries, min=-reach, max=reach).astype(kind)


def setup_inputs(seed: int = 0) -> dict:
    keys = jax.random.split(jax.random.key(seed), 9)
    return {
        "hidden_x": gaussian(keys[0], (ROWS_ALL, STEPS, D), 1.0, 6.0, ((0, 32), (2, 16))),
        "base_weight": gaussian(keys[1], (OUT, D), D ** -0.5, 0.0625, ((1, 16),)),
        "delta_codes": gaussian(keys[2], (OUT, D), 1.0, 4.0, ((0, 32), (1, 16))),
        "delta_scales": jnp.clip(jnp.exp(math.log(0.019897461) - 2.2979944 * jax.random.uniform(keys[3], (OUT, D // BLK), jnp.float32) ** shard_levels(keys[3], (OUT, D // BLK), ((0, 32), (1, 16)), -0.2, 0.2)), 0.0019989014, 0.019897461).astype(jnp.bfloat16),
        "owner_map": jax.random.permutation(keys[4], N_GROUP).astype(jnp.int32),
        "kv_cache": draw_kv_cache(jax.random.fold_in(keys[8], 71), 0),
        "queries": draw_queries(jax.random.fold_in(keys[8], 71), 0),
        "lengths": draw_lengths(jax.random.fold_in(keys[8], 71), 0),
    }


NEGATIVE = -1e30


def attend_row(query_row, cache_row, length_row, new_row):
    score_scale = HD ** -0.5
    kv_width = KVH * HD
    per_group = H // KVH
    grouped_query = query_row.astype(jnp.float32).reshape(STEPS, KVH, per_group, HD)
    cache_keys = cache_row[:, :kv_width].astype(jnp.float32).reshape(N_TENSOR, CACHE_DEV, KVH, HD)
    cache_values = cache_row[:, kv_width:].astype(jnp.float32).reshape(N_TENSOR, CACHE_DEV, KVH, HD)
    scores = jnp.einsum("skgd,nckd->skgnc", grouped_query, cache_keys) * score_scale
    positions = jnp.arange(CACHE, dtype=jnp.int32).reshape(N_TENSOR, CACHE_DEV)
    usable = (positions < length_row)[None, None, None, :, :]
    block_peak = jnp.max(jnp.where(usable, scores, NEGATIVE), axis=-1)
    weights = jnp.where(usable, jnp.exp(scores - block_peak[..., None]), 0.0)
    weight_total = jnp.sum(weights, axis=-1)
    rounded = lax.optimization_barrier(weights.astype(jnp.bfloat16)).astype(jnp.float32)
    weighted = jnp.einsum("skgnc,nckd->skgnd", rounded, cache_values)
    cache_peak = jnp.max(block_peak, axis=-1)
    rescale = jnp.exp(block_peak - cache_peak[..., None])
    cache_total = jnp.sum(weight_total * rescale, axis=-1)
    cache_sum = jnp.sum(weighted * rescale[..., None], axis=-2)
    stored_new = lax.optimization_barrier(new_row).astype(jnp.float32)
    new_keys = stored_new[:, :kv_width].reshape(STEPS, KVH, HD)
    new_values = stored_new[:, kv_width:].reshape(STEPS, KVH, HD)
    near_scores = jnp.einsum("skgd,tkd->skgt", grouped_query, new_keys) * score_scale
    causal = (jnp.arange(STEPS)[:, None] >= jnp.arange(STEPS)[None, :])[:, None, None, :]
    near_peak = jnp.max(jnp.where(causal, near_scores, NEGATIVE), axis=-1)
    near_weights = jnp.where(causal, jnp.exp(near_scores - near_peak[..., None]), 0.0)
    near_total = jnp.sum(near_weights, axis=-1)
    near_rounded = lax.optimization_barrier(near_weights.astype(jnp.bfloat16)).astype(jnp.float32)
    near_sum = jnp.einsum("skgt,tkd->skgd", near_rounded, new_values)
    joined_peak = jnp.maximum(cache_peak, near_peak)
    cache_scale = jnp.exp(cache_peak - joined_peak)
    near_scale = jnp.exp(near_peak - joined_peak)
    numerator = cache_sum * cache_scale[..., None] + near_sum * near_scale[..., None]
    denominator = cache_total * cache_scale + near_total * near_scale
    return (numerator / denominator[..., None]).astype(jnp.bfloat16).reshape(STEPS, H * HD)


def reference(hidden_x, base_weight, delta_codes, delta_scales, owner_map, kv_cache, queries, lengths):
    kv_width = KVH * HD
    out_width = 2 * kv_width
    owner_block = out_width // N_GROUP
    code_values = delta_codes.astype(jnp.float32).reshape(out_width, D // BLK, BLK)
    dequantized = (code_values * delta_scales.astype(jnp.float32)[:, :, None]).reshape(out_width, D).astype(jnp.bfloat16)
    stored = dequantized.reshape(N_GROUP, owner_block, D)
    ordered = jnp.zeros_like(stored).at[owner_map].set(stored).reshape(out_width, D)
    token_rows = hidden_x.reshape(ROWS_ALL * STEPS, D)
    projected = jnp.dot(token_rows, base_weight.T, preferred_element_type=jnp.float32) + jnp.dot(token_rows, ordered.T, preferred_element_type=jnp.float32)
    new_kv = projected.astype(jnp.bfloat16).reshape(ROWS_ALL, STEPS, out_width)

    def one_row(items):
        return attend_row(items[0], items[1], items[2], items[3])

    attended = lax.map(one_row, (queries, kv_cache, lengths, new_kv))
    return new_kv, attended
```

```python
import functools

import jax
import jax.numpy as jnp
from jax import lax
from jax.experimental import pallas as pl
from jax.experimental.pallas import tpu as pltpu
from jax.sharding import PartitionSpec as P

HD = 128
NEGATIVE = -1e30
MESH = pl.DeviceIdType.MESH
F32 = jnp.float32
BF16 = jnp.bfloat16


def nt_dot(a, b):
    return lax.dot_general(a, b, (((1,), (1,)), ((), ())), preferred_element_type=F32)


def kernel(
    NG,
    NT,
    hid_hbm,
    base_hbm,
    codes_hbm,
    scales_ref,
    owner_ref,
    cache_hbm,
    query_hbm,
    lengths_ref,
    new_ref,
    att_ref,
    hid,
    base,
    codes,
    cache,
    query,
    weight,
    place,
    back_send,
    back,
    proj_send,
    proj,
    part_send,
    part,
    lse_cols,
    lse_send,
    lse,
    pair_send,
    pair,
    load_sem,
    hid_send_sem,
    hid_sem,
    weight_send_sem,
    weight_sem,
    back_send_sem,
    back_sem,
    proj_send_sem,
    proj_sem,
    part_send_sem,
    part_sem,
    lse_send_sem,
    lse_sem,
    pair_send_sem,
    pair_sem,
):
    NZ = NG // 4
    KVH = NT // 2
    POS = cache.shape[0] // 2
    KVW = KVH * HD
    scale = HD ** (-0.5)
    me_g = lax.axis_index("group")
    me_t = lax.axis_index("tensor")
    core = lax.rem(me_g, 2)
    me_z = lax.rem(me_g // 2, NZ)
    x_lo = me_g // (2 * NZ)
    me_m = x_lo * 2 + core

    def group_of(m, z):
        return (m // 2) * (2 * NZ) + z * 2 + lax.rem(m, 2)

    def z_peer(i):
        return lax.rem(me_z + i, NZ)

    def m_peer(i):
        return lax.rem(me_m + i, 4)

    def t_peer(i):
        return lax.rem(me_t + i, NT)

    barrier = pltpu.get_barrier_semaphore()

    def greet_z(i, c):
        pl.semaphore_signal(
            barrier, inc=1, device_id=(group_of(me_m, z_peer(i)), me_t), device_id_type=MESH
        )
        return c

    def greet_m(i, c):
        pl.semaphore_signal(
            barrier, inc=1, device_id=(group_of(m_peer(i), me_z), me_t), device_id_type=MESH
        )
        return c

    def greet_t(i, c):
        pl.semaphore_signal(barrier, inc=1, device_id=(me_g, t_peer(i)), device_id_type=MESH)
        return c

    lax.fori_loop(1, NZ, greet_z, 0)
    lax.fori_loop(1, 4, greet_m, 0)
    lax.fori_loop(1, NT, greet_t, 0)

    loads = [
        pltpu.make_async_copy(codes_hbm, codes, load_sem.at[0]),
        pltpu.make_async_copy(hid_hbm, hid.at[me_z], load_sem.at[1]),
        pltpu.make_async_copy(query_hbm, query, load_sem.at[2]),
        pltpu.make_async_copy(cache_hbm.at[pl.ds(0, POS)], cache.at[pl.ds(0, POS)], load_sem.at[3]),
        pltpu.make_async_copy(
            cache_hbm.at[pl.ds(POS, POS)], cache.at[pl.ds(POS, POS)], load_sem.at[4]
        ),
        pltpu.make_async_copy(base_hbm, base, load_sem.at[5]),
    ]
    for load in loads:
        load.start()

    row = lax.broadcasted_iota(jnp.int32, (64, 64), 0)
    col = lax.broadcasted_iota(jnp.int32, (64, 64), 1)
    unit = (row == col).astype(BF16)
    scale_cols = nt_dot(unit, scales_ref[...])
    loads[0].wait()
    blocks = codes.shape[1] // 128
    own_weight = jnp.concatenate(
        [
            codes[:, j * 128 : (j + 1) * 128].astype(F32) * scale_cols[:, j : j + 1]
            for j in range(blocks)
        ],
        axis=1,
    ).astype(BF16)
    weight[me_m] = own_weight
    loads[1].wait()

    pl.semaphore_wait(barrier, (NZ - 1) + 3 + (NT - 1))

    def hid_copy(i):
        return pltpu.make_async_remote_copy(
            src_ref=hid.at[me_z],
            dst_ref=hid.at[me_z],
            send_sem=hid_send_sem.at[i],
            recv_sem=hid_sem.at[me_z],
            device_id=(group_of(me_m, z_peer(i)), me_t),
            device_id_type=MESH,
        )

    def weight_copy(i):
        return pltpu.make_async_remote_copy(
            src_ref=weight.at[me_m],
            dst_ref=weight.at[me_m],
            send_sem=weight_send_sem.at[i],
            recv_sem=weight_sem.at[me_m],
            device_id=(group_of(m_peer(i), me_z), me_t),
            device_id_type=MESH,
        )

    def start_hid(i, c):
        hid_copy(i).start()
        return c

    def start_weight(i, c):
        weight_copy(i).start()
        return c

    lax.fori_loop(1, NZ, start_hid, 0)
    lax.fori_loop(1, 4, start_weight, 0)

    def find(b, c):
        spot = jnp.int32(0)
        for g in range(NG):
            at = ((g // 2) % NZ) * 4 + (g // (2 * NZ)) * 2 + g % 2
            spot = jnp.where(owner_ref[g] == b, jnp.int32(at), spot)
        place[b] = spot
        return c

    lax.fori_loop(0, NG, find, 0)

    for load in loads[2:5]:
        load.wait()
    lse_cols[...] = jnp.zeros_like(lse_cols)
    lane = lax.broadcasted_iota(jnp.int32, (32, 128), 1)
    position = me_t * POS + lax.broadcasted_iota(jnp.int32, (64, POS), 1)

    def part_copy(dest, i):
        return pltpu.make_async_remote_copy(
            src_ref=part_send.at[dest],
            dst_ref=part.at[me_t],
            send_sem=part_send_sem.at[dest],
            recv_sem=part_sem.at[me_t],
            device_id=(me_g, dest),
            device_id_type=MESH,
        )

    def cached(i, c):
        k = lax.rem(me_t // 2 + 1 + i, KVH)
        q_both = query[:, pl.ds(pl.multiple_of(k * 1024, 1024), 1024)].astype(F32)
        for r in range(2):
            q = jnp.concatenate(
                [q_both[r * 8 : (r + 1) * 8, h * HD : (h + 1) * HD] for h in range(8)], axis=0
            ).astype(BF16)
            keys = cache[r * POS : (r + 1) * POS, pl.ds(pl.multiple_of(k * HD, HD), HD)]
            values = cache[r * POS : (r + 1) * POS, pl.ds(pl.multiple_of(KVW + k * HD, HD), HD)]
            scores = nt_dot(q, keys) * scale
            usable = position < lengths_ref[r]
            peak = jnp.max(jnp.where(usable, scores, NEGATIVE), axis=1, keepdims=True)
            weights = jnp.where(usable, jnp.exp(scores - peak), 0.0)
            total = jnp.sum(weights, axis=1, keepdims=True)
            weighted = jnp.dot(weights.astype(BF16), values, preferred_element_type=F32)
            some = total > 0.0
            safe = jnp.where(some, total, 1.0)
            mean = (weighted / safe).astype(BF16)
            log_sum = jnp.where(some, peak + jnp.log(safe), NEGATIVE)
            for half in range(2):
                dest = 2 * k + half
                part_send[dest, r * 32 : (r + 1) * 32] = mean[half * 32 : (half + 1) * 32]
                lse_cols[0:32] = jnp.where(
                    lane == dest * 8 + r, log_sum[half * 32 : (half + 1) * 32], lse_cols[0:32]
                )
        for half in range(2):
            dest = 2 * k + half

            @pl.when(dest != me_t)
            def _():
                part_copy(dest, i).start()

            @pl.when(dest == me_t)
            def _():
                part[me_t] = part_send[dest]

        return c

    lax.fori_loop(0, KVH, cached, 0)

    lse_send[...] = lse_cols[...].T[: NT * 8].reshape(lse_send.shape)

    def lse_copy(i):
        dest = t_peer(i)
        return pltpu.make_async_remote_copy(
            src_ref=lse_send.at[dest],
            dst_ref=lse.at[me_t],
            send_sem=lse_send_sem.at[i],
            recv_sem=lse_sem.at[me_t],
            device_id=(me_g, dest),
            device_id_type=MESH,
        )

    def start_lse(i, c):
        lse_copy(i).start()
        return c

    lax.fori_loop(1, NT, start_lse, 0)
    lse[me_t] = lse_send[me_t]

    def wait_hid(i, c):
        z = z_peer(i)
        pltpu.make_async_remote_copy(
            src_ref=hid.at[z],
            dst_ref=hid.at[z],
            send_sem=hid_send_sem.at[i],
            recv_sem=hid_sem.at[z],
            device_id=(group_of(me_m, z), me_t),
            device_id_type=MESH,
        ).wait_recv()
        return c

    def wait_weight(i, c):
        m = m_peer(i)
        pltpu.make_async_remote_copy(
            src_ref=weight.at[m],
            dst_ref=weight.at[m],
            send_sem=weight_send_sem.at[i],
            recv_sem=weight_sem.at[m],
            device_id=(group_of(m, me_z), me_t),
            device_id_type=MESH,
        ).wait_recv()
        return c

    lax.fori_loop(1, NZ, wait_hid, 0)
    lax.fori_loop(1, 4, wait_weight, 0)
    width = hid.shape[2]
    product = nt_dot(
        hid[...].reshape(NZ * 16, width), weight[...].reshape(4 * 64, width)
    ).reshape(NZ, 2, 8, 256)
    low = lax.broadcasted_iota(jnp.int32, (NZ, 8, 128), 2) < 64
    back_both = back_send
    for j in range(2):
        first = product[:, 0, :, j * 128 : (j + 1) * 128]
        second = product[:, 1, :, j * 128 : (j + 1) * 128]
        even = jnp.where(low, first, pltpu.roll(second, 64, 2))
        odd = jnp.where(low, pltpu.roll(first, 64, 2), second)
        back_both[:, 2 * j] = even
        back_both[:, 2 * j + 1] = odd

    def back_copy(i):
        z = z_peer(i)
        return pltpu.make_async_remote_copy(
            src_ref=back_send.at[z],
            dst_ref=back.at[pl.ds(me_z * 4, 4)],
            send_sem=back_send_sem.at[i],
            recv_sem=back_sem.at[me_z],
            device_id=(group_of(me_m, z), me_t),
            device_id_type=MESH,
        )

    def start_back(i, c):
        back_copy(i).start()
        return c

    lax.fori_loop(1, NZ, start_back, 0)
    back[pl.ds(me_z * 4, 4)] = back_send[me_z]

    loads[5].wait()
    own_rows = hid[me_z]

    def base_tile(j, c):
        rows = base[pl.ds(pl.multiple_of(j * 256, 256), 256), :]
        tile = nt_dot(own_rows, rows)
        proj_send[2 * j] = tile[:, :128]
        proj_send[2 * j + 1] = tile[:, 128:]
        return c

    lax.fori_loop(0, NT // 2, base_tile, 0)

    def wait_back(i, c):
        z = z_peer(i)
        pltpu.make_async_remote_copy(
            src_ref=back_send.at[z],
            dst_ref=back.at[pl.ds(z * 4, 4)],
            send_sem=back_send_sem.at[i],
            recv_sem=back_sem.at[z],
            device_id=(group_of(me_m, z), me_t),
            device_id_type=MESH,
        ).wait_recv()
        return c

    lax.fori_loop(1, NZ, wait_back, 0)
    low8 = lax.broadcasted_iota(jnp.int32, (8, 128), 1) < 64

    def proj_copy(i):
        dest = t_peer(i)
        return pltpu.make_async_remote_copy(
            src_ref=proj_send.at[dest],
            dst_ref=proj.at[me_t],
            send_sem=proj_send_sem.at[i],
            recv_sem=proj_sem.at[me_t],
            device_id=(me_g, dest),
            device_id_type=MESH,
        )

    def whole(dest):
        a = back[place[2 * dest]]
        b = back[place[2 * dest + 1]]
        first = jnp.where(low8, a, pltpu.roll(b, 64, 1))
        second = jnp.where(low8, pltpu.roll(a, 64, 1), b)
        return proj_send[dest] + jnp.concatenate([first, second], axis=0)

    def start_proj(i, c):
        dest = t_peer(i)
        proj_send[dest] = whole(dest)
        proj_copy(i).start()
        return c

    lax.fori_loop(1, NT, start_proj, 0)
    proj[me_t] = whole(me_t)

    def wait_part(i, c):
        u = t_peer(i)
        pltpu.make_async_remote_copy(
            src_ref=lse_send.at[u],
            dst_ref=lse.at[u],
            send_sem=lse_send_sem.at[i],
            recv_sem=lse_sem.at[u],
            device_id=(me_g, u),
            device_id_type=MESH,
        ).wait_recv()
        pltpu.make_async_remote_copy(
            src_ref=part_send.at[u],
            dst_ref=part.at[u],
            send_sem=part_send_sem.at[u],
            recv_sem=part_sem.at[u],
            device_id=(me_g, u),
            device_id_type=MESH,
        ).wait_recv()
        return c

    lax.fori_loop(1, NT, wait_part, 0)
    logs = lse[...]
    top = jnp.max(logs, axis=0)
    grown = jnp.exp(logs - top[None])
    sub = lax.broadcasted_iota(jnp.int32, (8, 128), 0)
    top_down = jnp.concatenate([top[0:2], top[0:2], top[0:4]], axis=0)
    with_top = jnp.where(sub < 2, grown[0], top_down)
    factors = jnp.concatenate([with_top[None], grown[1:]], axis=0).reshape(NT * 8, 128)
    if NT * 8 < 128:
        factors = jnp.concatenate([factors, jnp.zeros((128 - NT * 8, 128), F32)], axis=0)
    factors = factors.T[0:32]
    sums, totals, peaks = [], [], []
    for r in range(2):
        acc = jnp.zeros((32, HD), F32)
        total = jnp.zeros((32, 1), F32)
        for u in range(NT):
            factor = factors[:, u * 8 + r : u * 8 + r + 1]
            acc = acc + factor * part[u, r * 32 : (r + 1) * 32].astype(F32)
            total = total + factor
        sums.append(acc)
        totals.append(total)
        peaks.append(factors[:, 2 + r : 3 + r])
    cache_sum = jnp.concatenate(sums, axis=0)
    cache_total = jnp.concatenate(totals, axis=0)
    cache_peak = jnp.concatenate(peaks, axis=0)
    q_both = query[:, pl.ds(pl.multiple_of(me_t * 512, 512), 512)].astype(F32)
    q_own = jnp.concatenate(
        [
            q_both[r * 8 : (r + 1) * 8, h * HD : (h + 1) * HD]
            for r in range(2)
            for h in range(4)
        ],
        axis=0,
    ).astype(BF16)

    def wait_proj(i, c):
        u = t_peer(i)
        pltpu.make_async_remote_copy(
            src_ref=proj_send.at[u],
            dst_ref=proj.at[u],
            send_sem=proj_send_sem.at[i],
            recv_sem=proj_sem.at[u],
            device_id=(me_g, u),
            device_id_type=MESH,
        ).wait_recv()
        return c

    lax.fori_loop(1, NT, wait_proj, 0)
    fresh = jnp.sum(proj[...], axis=0).astype(BF16)
    pair_send[...] = fresh
    new_ref[...] = fresh
    is_value = me_t // KVH
    head = lax.rem(me_t, KVH)

    def pair_copy(half):
        return pltpu.make_async_remote_copy(
            src_ref=pair_send,
            dst_ref=pair.at[is_value],
            send_sem=pair_send_sem.at[half],
            recv_sem=pair_sem.at[is_value],
            device_id=(me_g, 2 * head + half),
            device_id_type=MESH,
        )

    for half in range(2):

        @pl.when(2 * head + half != me_t)
        def _():
            pair_copy(half).start()

        @pl.when(2 * head + half == me_t)
        def _():
            pair[is_value] = fresh

    for kind in range(2):
        source = kind * KVH + me_t // 2

        @pl.when(source != me_t)
        def _():
            pltpu.make_async_remote_copy(
                src_ref=pair_send,
                dst_ref=pair.at[kind],
                send_sem=pair_send_sem.at[kind],
                recv_sem=pair_sem.at[kind],
                device_id=(me_g, source),
                device_id_type=MESH,
            ).wait_recv()

    near = nt_dot(q_own, pair[0]) * scale
    at = lax.broadcasted_iota(jnp.int32, (64, 16), 0)
    to = lax.broadcasted_iota(jnp.int32, (64, 16), 1)
    causal = (at // 32 == to // 8) & (lax.rem(at, 8) >= lax.rem(to, 8))
    near_peak = jnp.max(jnp.where(causal, near, NEGATIVE), axis=1, keepdims=True)
    near_weights = jnp.where(causal, jnp.exp(near - near_peak), 0.0)
    near_total = jnp.sum(near_weights, axis=1, keepdims=True)
    near_sum = jnp.dot(near_weights.astype(BF16), pair[1], preferred_element_type=F32)
    joined = jnp.maximum(cache_peak, near_peak)
    cache_scale = jnp.exp(cache_peak - joined)
    near_scale = jnp.exp(near_peak - joined)
    numerator = cache_sum * cache_scale + near_sum * near_scale
    denominator = cache_total * cache_scale + near_total * near_scale
    result = numerator / denominator
    att_ref[...] = jnp.concatenate(
        [
            jnp.concatenate(
                [result[r * 32 + h * 8 : r * 32 + h * 8 + 8] for h in range(4)], axis=1
            )
            for r in range(2)
        ],
        axis=0,
    ).astype(BF16)

    def sent_z(i, c):
        hid_copy(i).wait_send()
        back_copy(i).wait_send()
        return c

    def sent_m(i, c):
        weight_copy(i).wait_send()
        return c

    def sent_t(i, c):
        lse_copy(i).wait_send()
        part_copy(t_peer(i), i).wait_send()
        proj_copy(i).wait_send()
        return c

    lax.fori_loop(1, NZ, sent_z, 0)
    lax.fori_loop(1, 4, sent_m, 0)
    lax.fori_loop(1, NT, sent_t, 0)
    for half in range(2):

        @pl.when(2 * head + half != me_t)
        def _():
            pair_copy(half).wait_send()


def on_device(
    hidden_x, base_weight, delta_codes, delta_scales, owner_map, kv_cache, queries, lengths
):
    NG = lax.axis_size("group")
    NT = lax.axis_size("tensor")
    NZ = NG // 4
    rows, steps, width = hidden_x.shape
    tokens = rows * steps
    positions = kv_cache.shape[1]
    any_space = pl.BlockSpec(memory_space=pltpu.HBM)
    vmem = pl.BlockSpec(memory_space=pltpu.VMEM)
    smem = pl.BlockSpec(memory_space=pltpu.SMEM)
    dma = pltpu.SemaphoreType.DMA
    new_kv, attended = pl.pallas_call(
        functools.partial(kernel, NG, NT),
        out_shape=(
            jax.ShapeDtypeStruct((tokens, 128), BF16),
            jax.ShapeDtypeStruct((tokens, 512), BF16),
        ),
        in_specs=[any_space, any_space, any_space, vmem, smem, any_space, any_space, smem],
        out_specs=(vmem, vmem),
        scratch_shapes=[
            pltpu.VMEM((NZ, tokens, width), BF16),
            pltpu.VMEM(base_weight.shape, BF16),
            pltpu.VMEM(delta_codes.shape, BF16),
            pltpu.VMEM((rows * positions, kv_cache.shape[2]), BF16),
            pltpu.VMEM((tokens, queries.shape[2]), BF16),
            pltpu.VMEM((4, 64, width), BF16),
            pltpu.SMEM((NG,), jnp.int32),
            pltpu.VMEM((NZ, 4, 8, 128), F32),
            pltpu.VMEM((NZ * 4, 8, 128), F32),
            pltpu.VMEM((NT, tokens, 128), F32),
            pltpu.VMEM((NT, tokens, 128), F32),
            pltpu.VMEM((NT, 64, HD), BF16),
            pltpu.VMEM((NT, 64, HD), BF16),
            pltpu.VMEM((128, 128), F32),
            pltpu.VMEM((NT, 8, 128), F32),
            pltpu.VMEM((NT, 8, 128), F32),
            pltpu.VMEM((tokens, 128), BF16),
            pltpu.VMEM((2, tokens, 128), BF16),
            dma((6,)),
            dma((NZ,)),
            dma((NZ,)),
            dma((4,)),
            dma((4,)),
            dma((NZ,)),
            dma((NZ,)),
            dma((NT,)),
            dma((NT,)),
            dma((NT,)),
            dma((NT,)),
            dma((NT,)),
            dma((NT,)),
            dma((2,)),
            dma((2,)),
        ],
        compiler_params=pltpu.CompilerParams(
            collective_id=0, has_side_effects=True, vmem_limit_bytes=60 * 1024 * 1024
        ),
    )(
        hidden_x.reshape(tokens, width),
        base_weight,
        delta_codes,
        delta_scales.T,
        owner_map,
        kv_cache.reshape(rows * positions, kv_cache.shape[2]),
        queries.reshape(tokens, queries.shape[2]),
        lengths,
    )
    return new_kv.reshape(rows, steps, 128), attended.reshape(rows, steps, 512)


def solution(mesh):
    in_specs = (
        P("group", None, "tensor"),
        P(None, "tensor"),
        P("group", "tensor"),
        P("group", "tensor"),
        P(),
        P("group", "tensor", None),
        P("group", None, None),
        P("group"),
    )
    out_specs = (P("group", None, "tensor"), P("group", None, "tensor"))
    return jax.shard_map(
        on_device, mesh=mesh, in_specs=in_specs, out_specs=out_specs, check_vma=False
    )
```

```python
import functools

import jax
import jax.numpy as jnp
from jax import lax
from jax.experimental import pallas as pl
from jax.experimental.pallas import tpu as pltpu
from jax.sharding import PartitionSpec as P

HD = 128
NEGATIVE = -1e30
LOG2_E = 1.4426950408889634
MESH = pl.DeviceIdType.MESH
F32 = jnp.float32
BF16 = jnp.bfloat16


def nt_dot(a, b):
    return lax.dot_general(a, b, (((1,), (1,)), ((), ())), preferred_element_type=F32)


def kernel(
    NG,
    NT,
    hid_hbm,
    base_hbm,
    codes_hbm,
    scales_ref,
    owner_ref,
    cache_hbm,
    query_hbm,
    lengths_ref,
    fresh_ref,
    cached_ref,
    own_ref,
    hid,
    base,
    codes,
    cache,
    query,
    weight,
    place,
    back_send,
    back,
    base_proj,
    proj_send,
    proj,
    part_send,
    part,
    lse_cols,
    load_sem,
    hid_send_sem,
    hid_sem,
    weight_send_sem,
    weight_sem,
    back_send_sem,
    back_sem,
    proj_send_sem,
    proj_sem,
    part_send_sem,
    part_sem,
    ready_z,
    ready_t,
    ready_m,
):
    NZ = NG // 4
    NY = NT // 2
    KVH = NT // 2
    POS = cache.shape[0] // 2
    KVW = KVH * HD
    width = hid.shape[2]
    scale = HD ** (-0.5) * LOG2_E
    me_g = lax.axis_index("group")
    me_t = lax.axis_index("tensor")
    core = lax.rem(me_g, 2)
    me_z = lax.rem(me_g // 2, NZ)
    me_m = me_g // (2 * NZ) * 2 + core
    me_y = me_t // 2
    me_x = lax.rem(me_t, 2)

    def group_of(m, z):
        return (m // 2) * (2 * NZ) + z * 2 + lax.rem(m, 2)

    def near_peer(n):
        step = n // 2 + 1
        return lax.rem(me_z + jnp.where(lax.rem(n, 2) == 0, step, NZ - step), NZ)

    me_q = me_m + 1 - 2 * core

    def m_at(q):
        return q + 1 - 2 * lax.rem(q, 2)

    def t_peer(i):
        return lax.rem(me_t + i, NT)

    def order_of(t):
        y = t // 2
        near = jnp.where(y > NY // 2, 2 * (NY - y), jnp.maximum(2 * y - 1, 0))
        return near * 2 + lax.rem(t, 2)

    order = order_of(me_t)
    barrier = pltpu.get_barrier_semaphore()

    def greet_m(q, c):
        pl.semaphore_signal(
            barrier, inc=1, device_id=(group_of(m_at(q), me_z), me_t), device_id_type=MESH
        )
        return c

    def greet_z(z, c):
        pl.semaphore_signal(
            barrier, inc=1, device_id=(group_of(me_m, z), me_t), device_id_type=MESH
        )
        return c

    def greet_t(i, c):
        @pl.when(order_of(t_peer(i)) > order)
        def _():
            pl.semaphore_signal(
                barrier, inc=1, device_id=(me_g, t_peer(i)), device_id_type=MESH
            )

        return c

    def answer_z(z, c):
        pl.semaphore_signal(
            ready_z.at[me_z], inc=1, device_id=(group_of(me_m, z), me_t), device_id_type=MESH
        )
        return c

    def answer_m(q, c):
        pl.semaphore_signal(
            ready_m.at[me_q],
            inc=1,
            device_id=(group_of(m_at(q), me_z), me_t),
            device_id_type=MESH,
        )
        return c

    def answer_t(i, c):
        @pl.when(order_of(t_peer(i)) < order)
        def _():
            pl.semaphore_signal(ready_t, inc=1, device_id=(me_g, t_peer(i)), device_id_type=MESH)

        return c

    loads = [
        pltpu.make_async_copy(codes_hbm, codes, load_sem.at[0]),
        pltpu.make_async_copy(hid_hbm, hid.at[me_z], load_sem.at[1]),
        pltpu.make_async_copy(query_hbm, query, load_sem.at[2]),
        pltpu.make_async_copy(cache_hbm, cache, load_sem.at[3]),
        pltpu.make_async_copy(base_hbm, base, load_sem.at[4]),
    ]
    loads[0].start()
    loads[1].start()
    lax.fori_loop(me_q + 1, 4, greet_m, 0)
    lax.fori_loop(me_z + 1, NZ, greet_z, 0)
    lax.fori_loop(1, NT, greet_t, 0)
    for load in loads[2:]:
        load.start()

    unit = (
        lax.broadcasted_iota(jnp.int32, (64, 64), 0) == lax.broadcasted_iota(jnp.int32, (64, 64), 1)
    ).astype(BF16)
    scale_cols = nt_dot(unit, scales_ref[...])
    loads[0].wait()
    weight[me_m] = jnp.concatenate(
        [
            codes[:, j * 128 : (j + 1) * 128].astype(F32) * scale_cols[:, j : j + 1]
            for j in range(width // 128)
        ],
        axis=1,
    ).astype(BF16)
    loads[1].wait()

    def hid_copy(z):
        return pltpu.make_async_remote_copy(
            src_ref=hid.at[me_z],
            dst_ref=hid.at[me_z],
            send_sem=hid_send_sem.at[z],
            recv_sem=hid_sem.at[me_z],
            device_id=(group_of(me_m, z), me_t),
            device_id_type=MESH,
        )

    def wait_hid(z):
        pltpu.make_async_remote_copy(
            src_ref=hid.at[z],
            dst_ref=hid.at[z],
            send_sem=hid_send_sem.at[z],
            recv_sem=hid_sem.at[z],
            device_id=(group_of(me_m, z), me_t),
            device_id_type=MESH,
        ).wait_recv()

    def weight_copy(q):
        return pltpu.make_async_remote_copy(
            src_ref=weight.at[me_m],
            dst_ref=weight.at[me_m],
            send_sem=weight_send_sem.at[q],
            recv_sem=weight_sem.at[me_m],
            device_id=(group_of(m_at(q), me_z), me_t),
            device_id_type=MESH,
        )

    def start_weight_earlier(q, c):
        weight_copy(q).start()
        return c

    def start_weight_later(q, c):
        pl.semaphore_wait(ready_m.at[q], 1)
        weight_copy(q).start()
        return c

    def wait_weight(i, c):
        q = lax.rem(me_q + i, 4)
        m = m_at(q)
        pltpu.make_async_remote_copy(
            src_ref=weight.at[m],
            dst_ref=weight.at[m],
            send_sem=weight_send_sem.at[q],
            recv_sem=weight_sem.at[m],
            device_id=(group_of(m, me_z), me_t),
            device_id_type=MESH,
        ).wait_recv()
        return c

    def start_hid_earlier(n, c):
        @pl.when(near_peer(n) < me_z)
        def _():
            hid_copy(near_peer(n)).start()

        return c

    def start_hid_later(z, c):
        pl.semaphore_wait(ready_z.at[z], 1)
        hid_copy(z).start()
        return c

    @pl.when(me_z + order + me_q > 0)
    def _():
        pl.semaphore_wait(barrier, me_z + order + me_q)

    lax.fori_loop(0, me_q, answer_m, 0)
    lax.fori_loop(0, me_z, answer_z, 0)
    lax.fori_loop(0, me_q, start_weight_earlier, 0)
    lax.fori_loop(1, NT, answer_t, 0)
    lax.fori_loop(0, NZ - 1, start_hid_earlier, 0)
    lax.fori_loop(me_q + 1, 4, start_weight_later, 0)

    def back_copy(z):
        return pltpu.make_async_remote_copy(
            src_ref=back_send.at[z],
            dst_ref=back.at[pl.ds(me_z * 4, 4)],
            send_sem=back_send_sem.at[z],
            recv_sem=back_sem.at[me_z],
            device_id=(group_of(me_m, z), me_t),
            device_id_type=MESH,
        )

    def products(z):
        product = nt_dot(hid[z], weight[...].reshape(4 * 64, width))
        low = lax.broadcasted_iota(jnp.int32, (8, 128), 1) < 64
        for j in range(2):
            first = product[0:8, j * 128 : (j + 1) * 128]
            second = product[8:16, j * 128 : (j + 1) * 128]
            back_send[z, 2 * j] = jnp.where(low, first, pltpu.roll(second, 64, 1))
            back_send[z, 2 * j + 1] = jnp.where(low, pltpu.roll(first, 64, 1), second)

    def serve(z):
        wait_hid(z)
        products(z)
        back_copy(z).start()

    early_first = sorted(range(1, NZ), key=lambda d: min(d, NZ - d) + (d > NZ // 2) * 1.5)

    def serve_peer(n):
        step = jnp.int32(0)
        for place_in_list, d in enumerate(early_first):
            step = jnp.where(n == place_in_list, d, step)
        return lax.rem(me_z + step, NZ)

    def serve_earlier(n, c):
        @pl.when(serve_peer(n) < me_z)
        def _():
            serve(serve_peer(n))

        return c

    def serve_later(n, c):
        z = serve_peer(n)

        @pl.when((z > me_z) & (z < NZ - 1))
        def _():
            serve(z)

        return c

    last = me_z == NZ - 1

    def serve_first():
        lax.fori_loop(1, 4, wait_weight, 0)
        serve(0)

    def find(b):
        spot = jnp.int32(0)
        for g in range(NG):
            at = ((g // 2) % NZ) * 4 + (g // (2 * NZ)) * 2 + g % 2
            spot = jnp.where(owner_ref[g] == b, jnp.int32(at), spot)
        place[b] = spot

    lane = lax.broadcasted_iota(jnp.int32, (32, 128), 1)
    position = me_t * POS + lax.broadcasted_iota(jnp.int32, (64, POS), 1)
    own_rows = hid[me_z]
    for load in loads[2:]:
        load.wait()

    def cached(i, columns):
        for n in range(2):
            k = 2 * i + n
            q_both = query[:, pl.ds(pl.multiple_of(k * 1024, 1024), 1024)].astype(F32)
            for r in range(2):
                q = jnp.concatenate(
                    [q_both[r * 8 : (r + 1) * 8, h * HD : (h + 1) * HD] for h in range(8)], axis=0
                ).astype(BF16)
                keys = cache[r * POS : (r + 1) * POS, pl.ds(pl.multiple_of(k * HD, HD), HD)]
                values = cache[
                    r * POS : (r + 1) * POS, pl.ds(pl.multiple_of(KVW + k * HD, HD), HD)
                ]
                scores = jnp.where(position < lengths_ref[r], nt_dot(q, keys) * scale, NEGATIVE)
                peak = jnp.max(scores, axis=1, keepdims=True)
                weights = jnp.exp2(scores - peak)
                total = jnp.sum(weights, axis=1, keepdims=True)
                weighted = jnp.dot(weights.astype(BF16), values, preferred_element_type=F32)
                mean = (weighted * (1.0 / total)).astype(BF16)
                some = me_t * POS < lengths_ref[r]
                log_sum = jnp.where(some, peak + jnp.log2(total), NEGATIVE)
                for half in range(2):
                    dest = 2 * k + half
                    part_send[dest, r * 32 : (r + 1) * 32] = mean[half * 32 : (half + 1) * 32]
                    columns = jnp.where(
                        lane == dest * 8 + r, log_sum[half * 32 : (half + 1) * 32], columns
                    )
            rows = base[pl.ds(pl.multiple_of(k * 256, 256), 256), :]
            tile = nt_dot(own_rows, rows)
            base_proj[2 * k] = tile[:, :128]
            base_proj[2 * k + 1] = tile[:, 128:]
            for m in range(NG // KVH):
                find(k * (NG // KVH) + m)

        @pl.when(me_z + 1 + i < jnp.minimum(NZ - 1, me_z + KVH // 2))
        def _():
            start_hid_later(me_z + 1 + i, 0)

        @pl.when(last & (i == KVH // 2 - 2))
        def _():
            serve_first()

        return columns

    lse_cols[...] = jnp.zeros_like(lse_cols)
    lse_cols[0:32] = lax.fori_loop(0, KVH // 2, cached, jnp.zeros((32, 128), F32))

    def part_copy(i):
        dest = t_peer(i)
        return pltpu.make_async_remote_copy(
            src_ref=part_send.at[dest],
            dst_ref=part.at[me_t],
            send_sem=part_send_sem.at[i],
            recv_sem=part_sem.at[me_t],
            device_id=(me_g, dest),
            device_id_type=MESH,
        )

    def start_part(i, c):
        part_copy(i).start()
        return c

    def start_parts():
        logs = lse_cols[...].T[: NT * 8].reshape(NT, 8, 128)
        sub = lax.broadcasted_iota(jnp.int32, (NT, 8, 128), 1)
        high = logs.astype(BF16).astype(F32)
        rest = logs - high
        middle = rest.astype(BF16).astype(F32)
        low = rest - middle
        middle = jnp.concatenate([middle[:, 0:2], middle[:, 0:2], middle[:, 0:4]], axis=1)
        low = jnp.concatenate([low[:, 0:4], low[:, 0:2], low[:, 0:2]], axis=1)
        rows = jnp.where(sub < 2, high, jnp.where(sub < 4, middle, low))
        part_send[:, 64:80] = jnp.concatenate([rows, rows], axis=1).astype(BF16)

        @pl.when(order < NT - 1)
        def _():
            pl.semaphore_wait(ready_t, NT - 1 - order)

        lax.fori_loop(1, NT, start_part, 0)
        part[me_t] = part_send[me_t]

    @pl.when(me_z < NZ // 2)
    def _():
        start_parts()

    lax.fori_loop(me_z + KVH // 2, NZ - 1, start_hid_later, 0)

    @pl.when((me_z >= NZ // 2) & (me_z < NZ - 1))
    def _():
        start_hid_later(NZ - 1, 0)

    @pl.when(me_z >= NZ // 2)
    def _():
        start_parts()

    @pl.when(jnp.logical_not(last))
    def _():
        lax.fori_loop(1, 4, wait_weight, 0)

    lax.fori_loop(jnp.where(last, 1, 0), NZ - 1, serve_earlier, 0)

    @pl.when(me_z < NZ // 2)
    def _():
        start_hid_later(NZ - 1, 0)

    lax.fori_loop(0, NZ - 1, serve_later, 0)

    @pl.when(me_z < NZ - 1)
    def _():
        serve(NZ - 1)

    products(me_z)
    back[pl.ds(me_z * 4, 4)] = back_send[me_z]

    def wait_back(n, c):
        z = near_peer(n)
        pltpu.make_async_remote_copy(
            src_ref=back_send.at[z],
            dst_ref=back.at[pl.ds(z * 4, 4)],
            send_sem=back_send_sem.at[z],
            recv_sem=back_sem.at[z],
            device_id=(group_of(me_m, z), me_t),
            device_id_type=MESH,
        ).wait_recv()
        return c

    lax.fori_loop(0, NZ - 1, wait_back, 0)

    low8 = lax.broadcasted_iota(jnp.int32, (8, 128), 1) < 64

    def whole(block):
        a = back[place[2 * block]]
        b = back[place[2 * block + 1]]
        first = jnp.where(low8, a, pltpu.roll(b, 64, 1))
        second = jnp.where(low8, pltpu.roll(a, 64, 1), b)
        return base_proj[block] + jnp.concatenate([first, second], axis=0)

    def proj_copy(dest):
        return pltpu.make_async_remote_copy(
            src_ref=proj_send.at[dest],
            dst_ref=proj.at[me_t],
            send_sem=proj_send_sem.at[dest],
            recv_sem=proj_sem.at[me_t],
            device_id=(me_g, dest),
            device_id_type=MESH,
        )

    def far_y(n):
        step = (n + 1) // 2
        return lax.rem(me_y + NY // 2 + jnp.where(lax.rem(n, 2) == 0, step, NY - step), NY)

    def start_proj(n, c):
        y = far_y(n)
        key = whole(y)
        value = whole(KVH + y).astype(BF16)
        key_high = key.astype(BF16)
        key_low = (key - key_high.astype(F32)).astype(BF16)
        for x in range(2):
            dest = 2 * y + x
            proj_send[dest, 0:16] = key_high
            proj_send[dest, 16:32] = key_low
            proj_send[dest, 32:48] = value
            proj_send[dest, 48:64] = whole(dest).astype(BF16)
        proj_copy(2 * y + 1 - me_x).start()

        @pl.when(y != me_y)
        def _():
            proj_copy(2 * y + me_x).start()

        return c

    lax.fori_loop(0, NY, start_proj, 0)
    proj[me_t] = proj_send[me_t]

    def wait_part(i, c):
        u = t_peer(i)
        pltpu.make_async_remote_copy(
            src_ref=part_send.at[u],
            dst_ref=part.at[u],
            send_sem=part_send_sem.at[i],
            recv_sem=part_sem.at[u],
            device_id=(me_g, u),
            device_id_type=MESH,
        ).wait_recv()
        return c

    lax.fori_loop(1, NT, wait_part, 0)
    logs = part[:, 64:80].astype(F32)[:, 0:8]
    logs = (
        logs
        + jnp.concatenate([logs[:, 2:8], logs[:, 0:2]], axis=1)
        + jnp.concatenate([logs[:, 4:8], logs[:, 0:4]], axis=1)
    )
    top = jnp.max(logs, axis=0)
    grown = jnp.exp2(logs - top[None])
    sub = lax.broadcasted_iota(jnp.int32, (8, 128), 0)
    top_down = jnp.concatenate([top[0:2], top[0:2], top[0:4]], axis=0)
    with_top = jnp.where(sub < 2, grown[0], top_down)
    factors = jnp.concatenate([with_top[None], grown[1:]], axis=0).reshape(NT * 8, 128)
    if NT * 8 < 128:
        factors = jnp.concatenate([factors, jnp.zeros((128 - NT * 8, 128), F32)], axis=0)
    factors = factors.T[0:32]
    sums, totals, peaks = [], [], []
    for r in range(2):
        acc = jnp.zeros((32, HD), F32)
        total = jnp.zeros((32, 1), F32)
        for u in range(NT):
            factor = factors[:, u * 8 + r : u * 8 + r + 1]
            acc = acc + factor * part[u, r * 32 : (r + 1) * 32].astype(F32)
            total = total + factor
        sums.append(acc)
        totals.append(total)
        peaks.append(factors[:, 2 + r : 3 + r])
    cached_ref[:, 0:HD] = jnp.concatenate(sums, axis=0)
    half_lane = lax.broadcasted_iota(jnp.int32, (64, 128), 1) < 64
    cached_ref[:, HD : 2 * HD] = jnp.where(
        half_lane, jnp.concatenate(totals, axis=0), jnp.concatenate(peaks, axis=0)
    )
    q_both = query[:, pl.ds(pl.multiple_of(me_t * 512, 512), 512)].astype(F32)
    own_ref[...] = jnp.concatenate(
        [
            q_both[r * 8 : (r + 1) * 8, h * HD : (h + 1) * HD]
            for r in range(2)
            for h in range(4)
        ],
        axis=0,
    ).astype(BF16)

    def sent_z(n, c):
        hid_copy(near_peer(n)).wait_send()
        back_copy(near_peer(n)).wait_send()
        return c

    def sent_m(i, c):
        weight_copy(lax.rem(me_q + i, 4)).wait_send()
        return c

    def sent_t(i, c):
        part_copy(i).wait_send()
        proj_copy(t_peer(i)).wait_send()
        return c

    lax.fori_loop(0, NZ - 1, sent_z, 0)
    lax.fori_loop(1, 4, sent_m, 0)
    lax.fori_loop(1, NT, sent_t, 0)

    def wait_proj(i, c):
        u = t_peer(i)
        pltpu.make_async_remote_copy(
            src_ref=proj_send.at[u],
            dst_ref=proj.at[u],
            send_sem=proj_send_sem.at[u],
            recv_sem=proj_sem.at[u],
            device_id=(me_g, u),
            device_id_type=MESH,
        ).wait_recv()
        return c

    lax.fori_loop(1, NT, wait_proj, 0)
    summed = jnp.sum(proj[...].astype(F32), axis=0)
    fresh_ref[0] = (summed[0:16] + summed[16:32]).astype(BF16)
    fresh_ref[1] = summed[32:48].astype(BF16)
    fresh_ref[2] = summed[48:64].astype(BF16)


def finish(fresh_ref, cached_ref, own_ref, new_ref, att_ref):
    scale = HD ** (-0.5) * LOG2_E
    new_ref[...] = fresh_ref[2]
    cache_sum = cached_ref[:, 0:HD]
    cache_total = cached_ref[:, HD : HD + 1]
    cache_peak = cached_ref[:, HD + 64 : HD + 65]
    near = nt_dot(own_ref[...], fresh_ref[0]) * scale
    at = lax.broadcasted_iota(jnp.int32, (64, 16), 0)
    to = lax.broadcasted_iota(jnp.int32, (64, 16), 1)
    causal = (at // 32 == to // 8) & (lax.rem(at, 8) >= lax.rem(to, 8))
    near = jnp.where(causal, near, NEGATIVE)
    near_peak = jnp.max(near, axis=1, keepdims=True)
    near_weights = jnp.exp2(near - near_peak)
    near_total = jnp.sum(near_weights, axis=1, keepdims=True)
    near_sum = jnp.dot(near_weights.astype(BF16), fresh_ref[1], preferred_element_type=F32)
    joined = jnp.maximum(cache_peak, near_peak)
    cache_scale = jnp.exp2(cache_peak - joined)
    near_scale = jnp.exp2(near_peak - joined)
    numerator = cache_sum * cache_scale + near_sum * near_scale
    denominator = cache_total * cache_scale + near_total * near_scale
    result = numerator / denominator
    att_ref[...] = jnp.concatenate(
        [
            jnp.concatenate(
                [result[r * 32 + h * 8 : r * 32 + h * 8 + 8] for h in range(4)], axis=1
            )
            for r in range(2)
        ],
        axis=0,
    ).astype(BF16)


def on_device(
    hidden_x, base_weight, delta_codes, delta_scales, owner_map, kv_cache, queries, lengths
):
    NG = lax.axis_size("group")
    NT = lax.axis_size("tensor")
    NZ = NG // 4
    rows, steps, width = hidden_x.shape
    tokens = rows * steps
    positions = kv_cache.shape[1]
    any_space = pl.BlockSpec(memory_space=pl.ANY)
    vmem = pl.BlockSpec(memory_space=pltpu.VMEM)
    smem = pl.BlockSpec(memory_space=pltpu.SMEM)
    dma = pltpu.SemaphoreType.DMA
    fresh, cached, own_query = pl.pallas_call(
        functools.partial(kernel, NG, NT),
        out_shape=(
            jax.ShapeDtypeStruct((3, tokens, 128), BF16),
            jax.ShapeDtypeStruct((64, 256), F32),
            jax.ShapeDtypeStruct((64, 128), BF16),
        ),
        in_specs=[any_space, any_space, any_space, vmem, smem, any_space, any_space, smem],
        out_specs=(vmem, vmem, vmem),
        scratch_shapes=[
            pltpu.VMEM((NZ, tokens, width), BF16),
            pltpu.VMEM(base_weight.shape, BF16),
            pltpu.VMEM(delta_codes.shape, BF16),
            pltpu.VMEM((rows * positions, kv_cache.shape[2]), BF16),
            pltpu.VMEM((tokens, queries.shape[2]), BF16),
            pltpu.VMEM((4, 64, width), BF16),
            pltpu.SMEM((NG,), jnp.int32),
            pltpu.VMEM((NZ, 4, 8, 128), F32),
            pltpu.VMEM((NZ * 4, 8, 128), F32),
            pltpu.VMEM((NT, tokens, 128), F32),
            pltpu.VMEM((NT, 4 * tokens, 128), BF16),
            pltpu.VMEM((NT, 4 * tokens, 128), BF16),
            pltpu.VMEM((NT, 80, HD), BF16),
            pltpu.VMEM((NT, 80, HD), BF16),
            pltpu.VMEM((128, 128), F32),
            dma((5,)),
            dma((NZ,)),
            dma((NZ,)),
            dma((4,)),
            dma((4,)),
            dma((NZ,)),
            dma((NZ,)),
            dma((NT,)),
            dma((NT,)),
            dma((NT,)),
            dma((NT,)),
            pltpu.SemaphoreType.REGULAR((NZ,)),
            pltpu.SemaphoreType.REGULAR,
            pltpu.SemaphoreType.REGULAR((4,)),
        ],
        compiler_params=pltpu.CompilerParams(
            collective_id=0, has_side_effects=True, vmem_limit_bytes=60 * 1024 * 1024
        ),
    )(
        hidden_x.reshape(tokens, width),
        base_weight,
        delta_codes,
        delta_scales.T,
        owner_map,
        kv_cache.reshape(rows * positions, kv_cache.shape[2]),
        queries.reshape(tokens, queries.shape[2]),
        lengths,
    )
    new_kv, attended = pl.pallas_call(
        finish,
        out_shape=(
            jax.ShapeDtypeStruct((tokens, 128), BF16),
            jax.ShapeDtypeStruct((tokens, 512), BF16),
        ),
        in_specs=[vmem, vmem, vmem],
        out_specs=(vmem, vmem),
    )(fresh, cached, own_query)
    return new_kv.reshape(rows, steps, 128), attended.reshape(rows, steps, 512)


def solution(mesh):
    in_specs = (
        P("group", None, "tensor"),
        P(None, "tensor"),
        P("group", "tensor"),
        P("group", "tensor"),
        P(),
        P("group", "tensor", None),
        P("group", None, None),
        P("group"),
    )
    out_specs = (P("group", None, "tensor"), P("group", None, "tensor"))
    return jax.shard_map(
        on_device, mesh=mesh, in_specs=in_specs, out_specs=out_specs, check_vma=False
    )
```

```python
import functools

import jax
import jax.numpy as jnp
from jax import lax
from jax.experimental import pallas as pl
from jax.experimental.pallas import tpu as pltpu
from jax.sharding import PartitionSpec as P

HD = 128
NEGATIVE = -1e30
LOG2_E = 1.4426950408889634
MESH = pl.DeviceIdType.MESH
F32 = jnp.float32
BF16 = jnp.bfloat16


def nt_dot(a, b):
    return lax.dot_general(a, b, (((1,), (1,)), ((), ())), preferred_element_type=F32)


def kernel(
    NG,
    NT,
    hid_hbm,
    base_hbm,
    codes_hbm,
    scales_ref,
    owner_ref,
    cache_hbm,
    query_hbm,
    lengths_ref,
    fresh_ref,
    cached_ref,
    own_ref,
    hid,
    base,
    codes,
    cache,
    query,
    weight,
    place,
    back_send,
    back,
    base_proj,
    proj_send,
    proj,
    part_send,
    part,
    lse_cols,
    load_sem,
    hid_send_sem,
    hid_sem,
    weight_send_sem,
    weight_sem,
    back_send_sem,
    back_sem,
    proj_send_sem,
    proj_sem,
    part_send_sem,
    part_sem,
    ready_z,
    ready_t,
    ready_x,
    ready_m,
):
    NZ = NG // 4
    NY = NT // 2
    KVH = NT // 2
    POS = cache.shape[0] // 2
    KVW = KVH * HD
    width = hid.shape[2]
    scale = HD ** (-0.5) * LOG2_E
    me_g = lax.axis_index("group")
    me_t = lax.axis_index("tensor")
    core = lax.rem(me_g, 2)
    me_z = lax.rem(me_g // 2, NZ)
    me_m = me_g // (2 * NZ) * 2 + core
    me_y = me_t // 2
    me_x = lax.rem(me_t, 2)

    def group_of(m, z):
        return (m // 2) * (2 * NZ) + z * 2 + lax.rem(m, 2)

    def near_peer(n):
        step = n // 2 + 1
        return lax.rem(me_z + jnp.where(lax.rem(n, 2) == 0, step, NZ - step), NZ)

    def t_peer(i):
        return lax.rem(me_t + i, NT)

    me_q = me_m + 1 - 2 * core

    def m_at(q):
        return q + 1 - 2 * lax.rem(q, 2)

    last_y = NY // 2
    at_last_y = me_y == last_y
    herald = at_last_y & (me_x == 0)
    greeted = me_z + me_q + jnp.where(at_last_y, NY - 1 + me_x, 0)
    barrier = pltpu.get_barrier_semaphore()

    def greet_m(q, c):
        pl.semaphore_signal(
            barrier, inc=1, device_id=(group_of(m_at(q), me_z), me_t), device_id_type=MESH
        )
        return c

    def greet_z(z, c):
        pl.semaphore_signal(
            barrier, inc=1, device_id=(group_of(me_m, z), me_t), device_id_type=MESH
        )
        return c

    def answer_z(z, c):
        pl.semaphore_signal(
            ready_z.at[me_z], inc=1, device_id=(group_of(me_m, z), me_t), device_id_type=MESH
        )
        return c

    def answer_m(q, c):
        pl.semaphore_signal(
            ready_m.at[me_q],
            inc=1,
            device_id=(group_of(m_at(q), me_z), me_t),
            device_id_type=MESH,
        )
        return c

    def answer_t(i, c):
        @pl.when(order_of(t_peer(i)) < order)
        def _():
            pl.semaphore_signal(ready_t, inc=1, device_id=(me_g, t_peer(i)), device_id_type=MESH)

        return c

    loads = [
        pltpu.make_async_copy(codes_hbm, codes, load_sem.at[0]),
        pltpu.make_async_copy(hid_hbm, hid.at[me_z], load_sem.at[1]),
        pltpu.make_async_copy(query_hbm, query, load_sem.at[2]),
        pltpu.make_async_copy(cache_hbm, cache, load_sem.at[3]),
        pltpu.make_async_copy(base_hbm, base, load_sem.at[4]),
    ]
    loads[0].start()
    loads[1].start()
    lax.fori_loop(me_q + 1, 4, greet_m, 0)
    lax.fori_loop(me_z + 1, NZ, greet_z, 0)

    @pl.when(jnp.logical_not(at_last_y))
    def _():
        pl.semaphore_signal(
            barrier, inc=1, device_id=(me_g, 2 * last_y + me_x), device_id_type=MESH
        )

    @pl.when(herald)
    def _():
        pl.semaphore_signal(
            barrier, inc=1, device_id=(me_g, 2 * last_y + 1), device_id_type=MESH
        )

    for load in loads[2:]:
        load.start()

    @pl.when(greeted > 0)
    def _():
        pl.semaphore_wait(barrier, greeted)

    lax.fori_loop(0, me_q, answer_m, 0)
    lax.fori_loop(0, me_z, answer_z, 0)

    @pl.when(at_last_y & (me_x == 1))
    def _():
        pl.semaphore_signal(ready_x, inc=1, device_id=(me_g, 2 * last_y), device_id_type=MESH)

    unit = (
        lax.broadcasted_iota(jnp.int32, (64, 64), 0) == lax.broadcasted_iota(jnp.int32, (64, 64), 1)
    ).astype(BF16)
    scale_cols = nt_dot(unit, scales_ref[...])
    loads[0].wait()
    weight[me_m] = jnp.concatenate(
        [
            codes[:, j * 128 : (j + 1) * 128].astype(F32) * scale_cols[:, j : j + 1]
            for j in range(width // 128)
        ],
        axis=1,
    ).astype(BF16)
    loads[1].wait()

    def hid_copy(z):
        return pltpu.make_async_remote_copy(
            src_ref=hid.at[me_z],
            dst_ref=hid.at[me_z],
            send_sem=hid_send_sem.at[z],
            recv_sem=hid_sem.at[me_z],
            device_id=(group_of(me_m, z), me_t),
            device_id_type=MESH,
        )

    def wait_hid(z):
        pltpu.make_async_remote_copy(
            src_ref=hid.at[z],
            dst_ref=hid.at[z],
            send_sem=hid_send_sem.at[z],
            recv_sem=hid_sem.at[z],
            device_id=(group_of(me_m, z), me_t),
            device_id_type=MESH,
        ).wait_recv()

    def weight_copy(q):
        return pltpu.make_async_remote_copy(
            src_ref=weight.at[me_m],
            dst_ref=weight.at[me_m],
            send_sem=weight_send_sem.at[q],
            recv_sem=weight_sem.at[me_m],
            device_id=(group_of(m_at(q), me_z), me_t),
            device_id_type=MESH,
        )

    def start_weight_earlier(q, c):
        weight_copy(q).start()
        return c

    def start_weight_later(q, c):
        pl.semaphore_wait(ready_m.at[q], 1)
        weight_copy(q).start()
        return c

    def wait_weight(i, c):
        q = lax.rem(me_q + i, 4)
        m = m_at(q)
        pltpu.make_async_remote_copy(
            src_ref=weight.at[m],
            dst_ref=weight.at[m],
            send_sem=weight_send_sem.at[q],
            recv_sem=weight_sem.at[m],
            device_id=(group_of(m, me_z), me_t),
            device_id_type=MESH,
        ).wait_recv()
        return c

    def start_hid_earlier(n, c):
        @pl.when(near_peer(n) < me_z)
        def _():
            hid_copy(near_peer(n)).start()

        return c

    def start_hid_later(z, c):
        pl.semaphore_wait(ready_z.at[z], 1)
        hid_copy(z).start()
        return c

    lax.fori_loop(0, me_q, start_weight_earlier, 0)

    lax.fori_loop(0, NZ - 1, start_hid_earlier, 0)
    lax.fori_loop(me_q + 1, 4, start_weight_later, 0)

    def back_copy(z):
        return pltpu.make_async_remote_copy(
            src_ref=back_send.at[z],
            dst_ref=back.at[pl.ds(me_z * 4, 4)],
            send_sem=back_send_sem.at[z],
            recv_sem=back_sem.at[me_z],
            device_id=(group_of(me_m, z), me_t),
            device_id_type=MESH,
        )

    def products(z):
        product = nt_dot(hid[z], weight[...].reshape(4 * 64, width))
        low = lax.broadcasted_iota(jnp.int32, (8, 128), 1) < 64
        for j in range(2):
            first = product[0:8, j * 128 : (j + 1) * 128]
            second = product[8:16, j * 128 : (j + 1) * 128]
            back_send[z, 2 * j] = jnp.where(low, first, pltpu.roll(second, 64, 1))
            back_send[z, 2 * j + 1] = jnp.where(low, pltpu.roll(first, 64, 1), second)

    def serve(z):
        wait_hid(z)
        products(z)
        back_copy(z).start()

    early_first = sorted(range(1, NZ), key=lambda d: min(d, NZ - d) + (d > NZ // 2) * 1.5)

    def serve_peer(n):
        step = jnp.int32(0)
        for place_in_list, d in enumerate(early_first):
            step = jnp.where(n == place_in_list, d, step)
        return lax.rem(me_z + step, NZ)

    def serve_earlier(n, c):
        @pl.when(serve_peer(n) < me_z)
        def _():
            serve(serve_peer(n))

        return c

    def serve_later(n, c):
        z = serve_peer(n)

        @pl.when((z > me_z) & (z < NZ - 1))
        def _():
            serve(z)

        return c

    last = me_z == NZ - 1

    def serve_first():
        lax.fori_loop(1, 4, wait_weight, 0)
        serve(0)

    def find(b):
        spot = jnp.int32(0)
        for g in range(NG):
            at = ((g // 2) % NZ) * 4 + (g // (2 * NZ)) * 2 + g % 2
            spot = jnp.where(owner_ref[g] == b, jnp.int32(at), spot)
        place[b] = spot

    lane = lax.broadcasted_iota(jnp.int32, (32, 128), 1)
    position = me_t * POS + lax.broadcasted_iota(jnp.int32, (64, POS), 1)
    own_rows = hid[me_z]
    for load in loads[2:]:
        load.wait()

    def cached(i, columns):
        for n in range(2):
            k = 2 * i + n
            q_both = query[:, pl.ds(pl.multiple_of(k * 1024, 1024), 1024)].astype(F32)
            for r in range(2):
                q = jnp.concatenate(
                    [q_both[r * 8 : (r + 1) * 8, h * HD : (h + 1) * HD] for h in range(8)], axis=0
                ).astype(BF16)
                keys = cache[r * POS : (r + 1) * POS, pl.ds(pl.multiple_of(k * HD, HD), HD)]
                values = cache[
                    r * POS : (r + 1) * POS, pl.ds(pl.multiple_of(KVW + k * HD, HD), HD)
                ]
                scores = jnp.where(position < lengths_ref[r], nt_dot(q, keys) * scale, NEGATIVE)
                peak = jnp.max(scores, axis=1, keepdims=True)
                weights = jnp.exp2(scores - peak)
                total = jnp.sum(weights, axis=1, keepdims=True)
                weighted = jnp.dot(weights.astype(BF16), values, preferred_element_type=F32)
                mean = (weighted * (1.0 / total)).astype(BF16)
                some = me_t * POS < lengths_ref[r]
                log_sum = jnp.where(some, peak + jnp.log2(total), NEGATIVE)
                for half in range(2):
                    dest = 2 * k + half
                    part_send[dest, r * 32 : (r + 1) * 32] = mean[half * 32 : (half + 1) * 32]
                    columns = jnp.where(
                        lane == dest * 8 + r, log_sum[half * 32 : (half + 1) * 32], columns
                    )
            rows = base[pl.ds(pl.multiple_of(k * 256, 256), 256), :]
            tile = nt_dot(own_rows, rows)
            base_proj[2 * k] = tile[:, :128]
            base_proj[2 * k + 1] = tile[:, 128:]
            for m in range(NG // KVH):
                find(k * (NG // KVH) + m)

        @pl.when(me_z + 1 + i < jnp.minimum(NZ - 1, me_z + KVH // 2))
        def _():
            start_hid_later(me_z + 1 + i, 0)

        @pl.when(last & (i == max(KVH // 2 - 3, 0)))
        def _():
            serve_first()

        return columns

    def tell(i, c):
        pl.semaphore_signal(ready_t, inc=1, device_id=(me_g, t_peer(i)), device_id_type=MESH)
        return c

    @pl.when(herald)
    def _():
        pl.semaphore_wait(ready_x, 1)
        lax.fori_loop(1, NT, tell, 0)

    lse_cols[...] = jnp.zeros_like(lse_cols)
    lse_cols[0:32] = lax.fori_loop(0, KVH // 2, cached, jnp.zeros((32, 128), F32))

    def part_copy(i):
        dest = t_peer(i)
        return pltpu.make_async_remote_copy(
            src_ref=part_send.at[dest],
            dst_ref=part.at[me_t],
            send_sem=part_send_sem.at[i],
            recv_sem=part_sem.at[me_t],
            device_id=(me_g, dest),
            device_id_type=MESH,
        )

    def start_part(i, c):
        part_copy(i).start()
        return c

    def start_parts():
        logs = lse_cols[...].T[: NT * 8].reshape(NT, 8, 128)
        sub = lax.broadcasted_iota(jnp.int32, (NT, 8, 128), 1)
        high = logs.astype(BF16).astype(F32)
        rest = logs - high
        middle = rest.astype(BF16).astype(F32)
        low = rest - middle
        middle = jnp.concatenate([middle[:, 0:2], middle[:, 0:2], middle[:, 0:4]], axis=1)
        low = jnp.concatenate([low[:, 0:4], low[:, 0:2], low[:, 0:2]], axis=1)
        rows = jnp.where(sub < 2, high, jnp.where(sub < 4, middle, low))
        part_send[:, 64:80] = jnp.concatenate([rows, rows], axis=1).astype(BF16)

        @pl.when(jnp.logical_not(herald))
        def _():
            pl.semaphore_wait(ready_t, 1)

        lax.fori_loop(1, NT, start_part, 0)
        part[me_t] = part_send[me_t]

    parts_first = (me_z < NZ // 2) & (jnp.abs(me_y - last_y) < 2)

    @pl.when(parts_first)
    def _():
        start_parts()

    lax.fori_loop(me_z + KVH // 2, NZ - 1, start_hid_later, 0)

    @pl.when((me_z >= NZ // 2) & (me_z < NZ - 1))
    def _():
        start_hid_later(NZ - 1, 0)

    @pl.when(last)
    def _():
        start_parts()

    @pl.when(jnp.logical_not(last))
    def _():
        lax.fori_loop(1, 4, wait_weight, 0)

    lax.fori_loop(jnp.where(last, 1, 0), NZ - 1, serve_earlier, 0)

    @pl.when((me_z >= NZ // 2) & jnp.logical_not(last))
    def _():
        start_parts()

    @pl.when(me_z < NZ // 2)
    def _():
        start_hid_later(NZ - 1, 0)

    @pl.when((me_z < NZ // 2) & jnp.logical_not(parts_first))
    def _():
        start_parts()

    lax.fori_loop(0, NZ - 1, serve_later, 0)

    @pl.when(me_z < NZ - 1)
    def _():
        serve(NZ - 1)

    products(me_z)
    back[pl.ds(me_z * 4, 4)] = back_send[me_z]

    def wait_back(n, c):
        z = near_peer(n)
        pltpu.make_async_remote_copy(
            src_ref=back_send.at[z],
            dst_ref=back.at[pl.ds(z * 4, 4)],
            send_sem=back_send_sem.at[z],
            recv_sem=back_sem.at[z],
            device_id=(group_of(me_m, z), me_t),
            device_id_type=MESH,
        ).wait_recv()
        return c

    lax.fori_loop(0, NZ - 1, wait_back, 0)

    low8 = lax.broadcasted_iota(jnp.int32, (8, 128), 1) < 64

    def whole(block):
        a = back[place[2 * block]]
        b = back[place[2 * block + 1]]
        first = jnp.where(low8, a, pltpu.roll(b, 64, 1))
        second = jnp.where(low8, pltpu.roll(a, 64, 1), b)
        return base_proj[block] + jnp.concatenate([first, second], axis=0)

    def proj_copy(dest):
        return pltpu.make_async_remote_copy(
            src_ref=proj_send.at[dest],
            dst_ref=proj.at[me_t],
            send_sem=proj_send_sem.at[dest],
            recv_sem=proj_sem.at[me_t],
            device_id=(me_g, dest),
            device_id_type=MESH,
        )

    def far_y(n):
        step = (n + 1) // 2
        return lax.rem(me_y + NY // 2 + jnp.where(lax.rem(n, 2) == 0, step, NY - step), NY)

    def start_proj(n, c):
        y = far_y(n)
        key = whole(y)
        value = whole(KVH + y).astype(BF16)
        key_high = key.astype(BF16)
        key_low = (key - key_high.astype(F32)).astype(BF16)
        for x in range(2):
            dest = 2 * y + x
            proj_send[dest, 0:16] = key_high
            proj_send[dest, 16:32] = key_low
            proj_send[dest, 32:48] = value
            proj_send[dest, 48:64] = whole(dest).astype(BF16)
        proj_copy(2 * y + 1 - me_x).start()

        @pl.when(y != me_y)
        def _():
            proj_copy(2 * y + me_x).start()

        return c

    lax.fori_loop(0, NY, start_proj, 0)
    proj[me_t] = proj_send[me_t]

    def wait_part(i, c):
        u = t_peer(i)
        pltpu.make_async_remote_copy(
            src_ref=part_send.at[u],
            dst_ref=part.at[u],
            send_sem=part_send_sem.at[i],
            recv_sem=part_sem.at[u],
            device_id=(me_g, u),
            device_id_type=MESH,
        ).wait_recv()
        return c

    lax.fori_loop(1, NT, wait_part, 0)
    logs = part[:, 64:80].astype(F32)[:, 0:8]
    logs = (
        logs
        + jnp.concatenate([logs[:, 2:8], logs[:, 0:2]], axis=1)
        + jnp.concatenate([logs[:, 4:8], logs[:, 0:4]], axis=1)
    )
    top = jnp.max(logs, axis=0)
    grown = jnp.exp2(logs - top[None])
    sub = lax.broadcasted_iota(jnp.int32, (8, 128), 0)
    top_down = jnp.concatenate([top[0:2], top[0:2], top[0:4]], axis=0)
    with_top = jnp.where(sub < 2, grown[0], top_down)
    factors = jnp.concatenate([with_top[None], grown[1:]], axis=0).reshape(NT * 8, 128)
    if NT * 8 < 128:
        factors = jnp.concatenate([factors, jnp.zeros((128 - NT * 8, 128), F32)], axis=0)
    factors = factors.T[0:32]
    sums, totals, peaks = [], [], []
    for r in range(2):
        acc = jnp.zeros((32, HD), F32)
        total = jnp.zeros((32, 1), F32)
        for u in range(NT):
            factor = factors[:, u * 8 + r : u * 8 + r + 1]
            acc = acc + factor * part[u, r * 32 : (r + 1) * 32].astype(F32)
            total = total + factor
        sums.append(acc)
        totals.append(total)
        peaks.append(factors[:, 2 + r : 3 + r])
    cached_ref[:, 0:HD] = jnp.concatenate(sums, axis=0)
    half_lane = lax.broadcasted_iota(jnp.int32, (64, 128), 1) < 64
    cached_ref[:, HD : 2 * HD] = jnp.where(
        half_lane, jnp.concatenate(totals, axis=0), jnp.concatenate(peaks, axis=0)
    )
    q_both = query[:, pl.ds(pl.multiple_of(me_t * 512, 512), 512)].astype(F32)
    own_ref[...] = jnp.concatenate(
        [
            q_both[r * 8 : (r + 1) * 8, h * HD : (h + 1) * HD]
            for r in range(2)
            for h in range(4)
        ],
        axis=0,
    ).astype(BF16)

    def sent_z(n, c):
        hid_copy(near_peer(n)).wait_send()
        back_copy(near_peer(n)).wait_send()
        return c

    def sent_m(i, c):
        weight_copy(lax.rem(me_q + i, 4)).wait_send()
        return c

    def sent_t(i, c):
        part_copy(i).wait_send()
        proj_copy(t_peer(i)).wait_send()
        return c

    lax.fori_loop(0, NZ - 1, sent_z, 0)
    lax.fori_loop(1, 4, sent_m, 0)
    lax.fori_loop(1, NT, sent_t, 0)

    def wait_proj(i, c):
        u = t_peer(i)
        pltpu.make_async_remote_copy(
            src_ref=proj_send.at[u],
            dst_ref=proj.at[u],
            send_sem=proj_send_sem.at[u],
            recv_sem=proj_sem.at[u],
            device_id=(me_g, u),
            device_id_type=MESH,
        ).wait_recv()
        return c

    lax.fori_loop(1, NT, wait_proj, 0)
    summed = jnp.sum(proj[...].astype(F32), axis=0)
    fresh_ref[0] = (summed[0:16] + summed[16:32]).astype(BF16)
    fresh_ref[1] = summed[32:48].astype(BF16)
    fresh_ref[2] = summed[48:64].astype(BF16)


def finish(fresh_ref, cached_ref, own_ref, new_ref, att_ref):
    scale = HD ** (-0.5) * LOG2_E
    new_ref[...] = fresh_ref[2]
    cache_sum = cached_ref[:, 0:HD]
    cache_total = cached_ref[:, HD : HD + 1]
    cache_peak = cached_ref[:, HD + 64 : HD + 65]
    near = nt_dot(own_ref[...], fresh_ref[0]) * scale
    at = lax.broadcasted_iota(jnp.int32, (64, 16), 0)
    to = lax.broadcasted_iota(jnp.int32, (64, 16), 1)
    causal = (at // 32 == to // 8) & (lax.rem(at, 8) >= lax.rem(to, 8))
    near = jnp.where(causal, near, NEGATIVE)
    near_peak = jnp.max(near, axis=1, keepdims=True)
    near_weights = jnp.exp2(near - near_peak)
    near_total = jnp.sum(near_weights, axis=1, keepdims=True)
    near_sum = jnp.dot(near_weights.astype(BF16), fresh_ref[1], preferred_element_type=F32)
    joined = jnp.maximum(cache_peak, near_peak)
    cache_scale = jnp.exp2(cache_peak - joined)
    near_scale = jnp.exp2(near_peak - joined)
    numerator = cache_sum * cache_scale + near_sum * near_scale
    denominator = cache_total * cache_scale + near_total * near_scale
    result = numerator / denominator
    att_ref[...] = jnp.concatenate(
        [
            jnp.concatenate(
                [result[r * 32 + h * 8 : r * 32 + h * 8 + 8] for h in range(4)], axis=1
            )
            for r in range(2)
        ],
        axis=0,
    ).astype(BF16)


def on_device(
    hidden_x, base_weight, delta_codes, delta_scales, owner_map, kv_cache, queries, lengths
):
    NG = lax.axis_size("group")
    NT = lax.axis_size("tensor")
    NZ = NG // 4
    rows, steps, width = hidden_x.shape
    tokens = rows * steps
    positions = kv_cache.shape[1]
    any_space = pl.BlockSpec(memory_space=pl.ANY)
    vmem = pl.BlockSpec(memory_space=pltpu.VMEM)
    smem = pl.BlockSpec(memory_space=pltpu.SMEM)
    dma = pltpu.SemaphoreType.DMA

    def in_hbm(x):
        return pltpu.with_memory_space_constraint(x, pltpu.HBM)

    fresh, cached, own_query = pl.pallas_call(
        functools.partial(kernel, NG, NT),
        out_shape=(
            pltpu.VMEM((3, tokens, 128), BF16),
            pltpu.VMEM((64, 256), F32),
            pltpu.VMEM((64, 128), BF16),
        ),
        in_specs=[any_space, any_space, any_space, vmem, smem, any_space, any_space, smem],
        out_specs=(vmem, vmem, vmem),
        scratch_shapes=[
            pltpu.VMEM((NZ, tokens, width), BF16),
            pltpu.VMEM(base_weight.shape, BF16),
            pltpu.VMEM(delta_codes.shape, BF16),
            pltpu.VMEM((rows * positions, kv_cache.shape[2]), BF16),
            pltpu.VMEM((tokens, queries.shape[2]), BF16),
            pltpu.VMEM((4, 64, width), BF16),
            pltpu.SMEM((NG,), jnp.int32),
            pltpu.VMEM((NZ, 4, 8, 128), F32),
            pltpu.VMEM((NZ * 4, 8, 128), F32),
            pltpu.VMEM((NT, tokens, 128), F32),
            pltpu.VMEM((NT, 4 * tokens, 128), BF16),
            pltpu.VMEM((NT, 4 * tokens, 128), BF16),
            pltpu.VMEM((NT, 80, HD), BF16),
            pltpu.VMEM((NT, 80, HD), BF16),
            pltpu.VMEM((128, 128), F32),
            dma((5,)),
            dma((NZ,)),
            dma((NZ,)),
            dma((4,)),
            dma((4,)),
            dma((NZ,)),
            dma((NZ,)),
            dma((NT,)),
            dma((NT,)),
            dma((NT,)),
            dma((NT,)),
            pltpu.SemaphoreType.REGULAR((NZ,)),
            pltpu.SemaphoreType.REGULAR,
            pltpu.SemaphoreType.REGULAR,
            pltpu.SemaphoreType.REGULAR((4,)),
        ],
        compiler_params=pltpu.CompilerParams(
            collective_id=0, has_side_effects=True, vmem_limit_bytes=48 * 1024 * 1024
        ),
    )(
        in_hbm(hidden_x.reshape(tokens, width)),
        in_hbm(base_weight),
        in_hbm(delta_codes),
        in_hbm(delta_scales.T),
        in_hbm(owner_map),
        in_hbm(kv_cache.reshape(rows * positions, kv_cache.shape[2])),
        in_hbm(queries.reshape(tokens, queries.shape[2])),
        in_hbm(lengths),
    )
    new_kv, attended = pl.pallas_call(
        finish,
        out_shape=(
            jax.ShapeDtypeStruct((tokens, 128), BF16),
            jax.ShapeDtypeStruct((tokens, 512), BF16),
        ),
        in_specs=[vmem, vmem, vmem],
        out_specs=(vmem, vmem),
        compiler_params=pltpu.CompilerParams(vmem_limit_bytes=8 * 1024 * 1024),
    )(fresh, cached, own_query)
    return new_kv.reshape(rows, steps, 128), attended.reshape(rows, steps, 512)


def solution(mesh):
    in_specs = (
        P("group", None, "tensor"),
        P(None, "tensor"),
        P("group", "tensor"),
        P("group", "tensor"),
        P(),
        P("group", "tensor", None),
        P("group", None, None),
        P("group"),
    )
    out_specs = (P("group", None, "tensor"), P("group", None, "tensor"))
    return jax.shard_map(
        on_device, mesh=mesh, in_specs=in_specs, out_specs=out_specs, check_vma=False
    )
```

```python
import functools

import jax
import jax.numpy as jnp
from jax import lax
from jax.experimental import pallas as pl
from jax.experimental.pallas import tpu as pltpu
from jax.sharding import PartitionSpec as P

HD = 128
NEGATIVE = -1e30
LOG2_E = 1.4426950408889634
MESH = pl.DeviceIdType.MESH
F32 = jnp.float32
BF16 = jnp.bfloat16


def nt_dot(a, b):
    return lax.dot_general(a, b, (((1,), (1,)), ((), ())), preferred_element_type=F32)


def kernel(
    NG,
    NT,
    hid_hbm,
    base_hbm,
    codes_hbm,
    scales_hbm,
    owner_hbm,
    cache_hbm,
    query_hbm,
    lengths_hbm,
    fresh_ref,
    cached_ref,
    own_ref,
    hid,
    base,
    codes,
    scales_ref,
    owner_ref,
    lengths_ref,
    cache,
    query,
    weight,
    place,
    back_send,
    back,
    base_proj,
    proj_send,
    proj,
    part_send,
    part,
    lse_cols,
    load_sem,
    hid_send_sem,
    hid_sem,
    weight_send_sem,
    weight_sem,
    back_send_sem,
    back_sem,
    proj_send_sem,
    proj_sem,
    part_send_sem,
    part_sem,
    ready_z,
    ready_t,
    ready_x,
    ready_m,
):
    NZ = NG // 4
    NY = NT // 2
    KVH = NT // 2
    POS = cache.shape[0] // 2
    KVW = KVH * HD
    width = hid.shape[2]
    scale = HD ** (-0.5) * LOG2_E
    me_g = lax.axis_index("group")
    me_t = lax.axis_index("tensor")
    core = lax.rem(me_g, 2)
    me_z = lax.rem(me_g // 2, NZ)
    me_m = me_g // (2 * NZ) * 2 + core
    me_y = me_t // 2
    me_x = lax.rem(me_t, 2)

    def group_of(m, z):
        return (m // 2) * (2 * NZ) + z * 2 + lax.rem(m, 2)

    def near_peer(n):
        step = n // 2 + 1
        return lax.rem(me_z + jnp.where(lax.rem(n, 2) == 0, step, NZ - step), NZ)

    def t_peer(i):
        return lax.rem(me_t + i, NT)

    me_q = me_m + 1 - 2 * core

    def m_at(q):
        return q + 1 - 2 * lax.rem(q, 2)

    last_y = NY // 2
    at_last_y = me_y == last_y
    herald = at_last_y & (me_x == 0)
    greeted = me_z + me_q + jnp.where(at_last_y, NY - 1 + me_x, 0)
    barrier = pltpu.get_barrier_semaphore()

    def greet_m(q, c):
        pl.semaphore_signal(
            barrier, inc=1, device_id=(group_of(m_at(q), me_z), me_t), device_id_type=MESH
        )
        return c

    def greet_z(z, c):
        pl.semaphore_signal(
            barrier, inc=1, device_id=(group_of(me_m, z), me_t), device_id_type=MESH
        )
        return c

    def answer_z(z, c):
        pl.semaphore_signal(
            ready_z.at[me_z], inc=1, device_id=(group_of(me_m, z), me_t), device_id_type=MESH
        )
        return c

    def answer_m(q, c):
        pl.semaphore_signal(
            ready_m.at[me_q],
            inc=1,
            device_id=(group_of(m_at(q), me_z), me_t),
            device_id_type=MESH,
        )
        return c

    def answer_t(i, c):
        @pl.when(order_of(t_peer(i)) < order)
        def _():
            pl.semaphore_signal(ready_t, inc=1, device_id=(me_g, t_peer(i)), device_id_type=MESH)

        return c

    loads = [
        pltpu.make_async_copy(codes_hbm, codes, load_sem.at[0]),
        pltpu.make_async_copy(hid_hbm, hid.at[me_z], load_sem.at[1]),
        pltpu.make_async_copy(query_hbm, query, load_sem.at[2]),
        pltpu.make_async_copy(cache_hbm, cache, load_sem.at[3]),
        pltpu.make_async_copy(base_hbm, base, load_sem.at[4]),
        pltpu.make_async_copy(scales_hbm, scales_ref, load_sem.at[5]),
        pltpu.make_async_copy(owner_hbm, owner_ref, load_sem.at[6]),
        pltpu.make_async_copy(lengths_hbm, lengths_ref, load_sem.at[7]),
    ]
    loads[5].start()
    loads[0].start()
    loads[1].start()
    lax.fori_loop(me_q + 1, 4, greet_m, 0)
    lax.fori_loop(me_z + 1, NZ, greet_z, 0)

    @pl.when(jnp.logical_not(at_last_y))
    def _():
        pl.semaphore_signal(
            barrier, inc=1, device_id=(me_g, 2 * last_y + me_x), device_id_type=MESH
        )

    @pl.when(herald)
    def _():
        pl.semaphore_signal(
            barrier, inc=1, device_id=(me_g, 2 * last_y + 1), device_id_type=MESH
        )

    for load in loads[2:5] + loads[6:]:
        load.start()

    @pl.when(greeted > 0)
    def _():
        pl.semaphore_wait(barrier, greeted)

    lax.fori_loop(0, me_q, answer_m, 0)
    lax.fori_loop(0, me_z, answer_z, 0)

    @pl.when(at_last_y & (me_x == 1))
    def _():
        pl.semaphore_signal(ready_x, inc=1, device_id=(me_g, 2 * last_y), device_id_type=MESH)

    unit = (
        lax.broadcasted_iota(jnp.int32, (64, 64), 0) == lax.broadcasted_iota(jnp.int32, (64, 64), 1)
    ).astype(BF16)
    loads[5].wait()
    scale_cols = nt_dot(unit, scales_ref[...])
    loads[0].wait()
    weight[me_m] = jnp.concatenate(
        [
            codes[:, j * 128 : (j + 1) * 128].astype(F32) * scale_cols[:, j : j + 1]
            for j in range(width // 128)
        ],
        axis=1,
    ).astype(BF16)
    loads[1].wait()

    def hid_copy(z):
        return pltpu.make_async_remote_copy(
            src_ref=hid.at[me_z],
            dst_ref=hid.at[me_z],
            send_sem=hid_send_sem.at[z],
            recv_sem=hid_sem.at[me_z],
            device_id=(group_of(me_m, z), me_t),
            device_id_type=MESH,
        )

    def wait_hid(z):
        pltpu.make_async_remote_copy(
            src_ref=hid.at[z],
            dst_ref=hid.at[z],
            send_sem=hid_send_sem.at[z],
            recv_sem=hid_sem.at[z],
            device_id=(group_of(me_m, z), me_t),
            device_id_type=MESH,
        ).wait_recv()

    def weight_copy(q):
        return pltpu.make_async_remote_copy(
            src_ref=weight.at[me_m],
            dst_ref=weight.at[me_m],
            send_sem=weight_send_sem.at[q],
            recv_sem=weight_sem.at[me_m],
            device_id=(group_of(m_at(q), me_z), me_t),
            device_id_type=MESH,
        )

    def start_weight(q):
        @pl.when(q > me_q)
        def _():
            pl.semaphore_wait(ready_m.at[q], 1)

        weight_copy(q).start()

    def wait_weight(i, c):
        q = lax.rem(me_q + i, 4)
        m = m_at(q)
        pltpu.make_async_remote_copy(
            src_ref=weight.at[m],
            dst_ref=weight.at[m],
            send_sem=weight_send_sem.at[q],
            recv_sem=weight_sem.at[m],
            device_id=(group_of(m, me_z), me_t),
            device_id_type=MESH,
        ).wait_recv()
        return c

    def start_hid_earlier(n, c):
        @pl.when(near_peer(n) < me_z)
        def _():
            hid_copy(near_peer(n)).start()

        return c

    def start_hid_later(z, c):
        pl.semaphore_wait(ready_z.at[z], 1)
        hid_copy(z).start()
        return c

    start_weight(lax.rem(me_q + 2, 4))
    start_weight(3 - me_q)
    start_weight(me_q + 1 - 2 * lax.rem(me_q, 2))

    lax.fori_loop(0, NZ - 1, start_hid_earlier, 0)

    def back_copy(z):
        return pltpu.make_async_remote_copy(
            src_ref=back_send.at[z],
            dst_ref=back.at[pl.ds(me_z * 4, 4)],
            send_sem=back_send_sem.at[z],
            recv_sem=back_sem.at[me_z],
            device_id=(group_of(me_m, z), me_t),
            device_id_type=MESH,
        )

    def products(z):
        product = nt_dot(hid[z], weight[...].reshape(4 * 64, width))
        low = lax.broadcasted_iota(jnp.int32, (8, 128), 1) < 64
        for j in range(2):
            first = product[0:8, j * 128 : (j + 1) * 128]
            second = product[8:16, j * 128 : (j + 1) * 128]
            back_send[z, 2 * j] = jnp.where(low, first, pltpu.roll(second, 64, 1))
            back_send[z, 2 * j + 1] = jnp.where(low, pltpu.roll(first, 64, 1), second)

    def serve(z):
        wait_hid(z)
        products(z)
        back_copy(z).start()

    def serve_peer(n):
        return lax.rem(me_z + 1 + n, NZ)

    def serve_earlier(n, c):
        @pl.when(serve_peer(n) < me_z)
        def _():
            serve(serve_peer(n))

        return c

    def serve_later(n, c):
        z = serve_peer(n)

        @pl.when((z > me_z) & (z < NZ - 1))
        def _():
            serve(z)

        return c

    last = me_z == NZ - 1

    between = KVH // 2 - 1

    def find(b):
        spot = jnp.int32(0)
        for g in range(NG):
            at = ((g // 2) % NZ) * 4 + (g // (2 * NZ)) * 2 + g % 2
            spot = jnp.where(owner_ref[g] == b, jnp.int32(at), spot)
        place[b] = spot

    lane = lax.broadcasted_iota(jnp.int32, (32, 128), 1)
    position = me_t * POS + lax.broadcasted_iota(jnp.int32, (64, POS), 1)
    own_rows = hid[me_z]
    for load in loads[2:5] + loads[6:]:
        load.wait()

    def cached(i, columns):
        for n in range(2):
            k = 2 * i + n
            q_both = query[:, pl.ds(pl.multiple_of(k * 1024, 1024), 1024)].astype(F32)
            for r in range(2):
                q = jnp.concatenate(
                    [q_both[r * 8 : (r + 1) * 8, h * HD : (h + 1) * HD] for h in range(8)], axis=0
                ).astype(BF16)
                keys = cache[r * POS : (r + 1) * POS, pl.ds(pl.multiple_of(k * HD, HD), HD)]
                values = cache[
                    r * POS : (r + 1) * POS, pl.ds(pl.multiple_of(KVW + k * HD, HD), HD)
                ]
                scores = jnp.where(position < lengths_ref[r], nt_dot(q, keys) * scale, NEGATIVE)
                peak = jnp.max(scores, axis=1, keepdims=True)
                weights = jnp.exp2(scores - peak)
                total = jnp.sum(weights, axis=1, keepdims=True)
                weighted = jnp.dot(weights.astype(BF16), values, preferred_element_type=F32)
                mean = (weighted * (1.0 / total)).astype(BF16)
                some = me_t * POS < lengths_ref[r]
                log_sum = jnp.where(some, peak + jnp.log2(total), NEGATIVE)
                for half in range(2):
                    dest = 2 * k + half
                    part_send[dest, r * 32 : (r + 1) * 32] = mean[half * 32 : (half + 1) * 32]
                    columns = jnp.where(
                        lane == dest * 8 + r, log_sum[half * 32 : (half + 1) * 32], columns
                    )
            rows = base[pl.ds(pl.multiple_of(k * 256, 256), 256), :]
            tile = nt_dot(own_rows, rows)
            base_proj[2 * k] = tile[:, :128]
            base_proj[2 * k + 1] = tile[:, 128:]
            for m in range(NG // KVH):
                find(k * (NG // KVH) + m)

        @pl.when(me_z + 1 + i < jnp.minimum(NZ - 1, me_z + KVH // 2))
        def _():
            start_hid_later(me_z + 1 + i, 0)

        @pl.when(last & (i == 1))
        def _():
            lax.fori_loop(1, 4, wait_weight, 0)

        @pl.when(last & (i >= 1))
        def _():
            serve(i - 1)

        return columns

    def tell(i, c):
        pl.semaphore_signal(ready_t, inc=1, device_id=(me_g, t_peer(i)), device_id_type=MESH)
        return c

    @pl.when(herald)
    def _():
        pl.semaphore_wait(ready_x, 1)
        lax.fori_loop(1, NT, tell, 0)

    lse_cols[...] = jnp.zeros_like(lse_cols)
    lse_cols[0:32] = lax.fori_loop(0, KVH // 2, cached, jnp.zeros((32, 128), F32))

    def part_copy(i):
        dest = t_peer(i)
        return pltpu.make_async_remote_copy(
            src_ref=part_send.at[dest],
            dst_ref=part.at[me_t],
            send_sem=part_send_sem.at[i],
            recv_sem=part_sem.at[me_t],
            device_id=(me_g, dest),
            device_id_type=MESH,
        )

    def start_part(i, c):
        part_copy(i).start()
        return c

    def start_parts():
        logs = lse_cols[...].T[: NT * 8].reshape(NT, 8, 128)
        sub = lax.broadcasted_iota(jnp.int32, (NT, 8, 128), 1)
        high = logs.astype(BF16).astype(F32)
        rest = logs - high
        middle = rest.astype(BF16).astype(F32)
        low = rest - middle
        middle = jnp.concatenate([middle[:, 0:2], middle[:, 0:2], middle[:, 0:4]], axis=1)
        low = jnp.concatenate([low[:, 0:4], low[:, 0:2], low[:, 0:2]], axis=1)
        rows = jnp.where(sub < 2, high, jnp.where(sub < 4, middle, low))
        part_send[:, 64:80] = jnp.concatenate([rows, rows], axis=1).astype(BF16)

        @pl.when(jnp.logical_not(herald))
        def _():
            pl.semaphore_wait(ready_t, 1)

        lax.fori_loop(1, NT, start_part, 0)
        part[me_t] = part_send[me_t]

    parts_first = (me_z < NZ // 2) & (jnp.abs(me_y - last_y) < 2)

    @pl.when(parts_first)
    def _():
        start_parts()

    lax.fori_loop(me_z + KVH // 2, NZ - 1, start_hid_later, 0)

    @pl.when((me_z >= NZ // 2) & (me_z < NZ - 1))
    def _():
        start_hid_later(NZ - 1, 0)

    @pl.when(jnp.logical_not(last) | (between == 0))
    def _():
        lax.fori_loop(1, 4, wait_weight, 0)

    @pl.when(last)
    def _():
        serve(between)
        start_parts()

    lax.fori_loop(jnp.where(last, between + 1, 0), NZ - 1, serve_earlier, 0)

    @pl.when((me_z >= NZ // 2) & jnp.logical_not(last))
    def _():
        start_parts()

    @pl.when(me_z < NZ // 2)
    def _():
        start_hid_later(NZ - 1, 0)

    @pl.when((me_z < NZ // 2) & jnp.logical_not(parts_first))
    def _():
        start_parts()

    lax.fori_loop(0, NZ - 1, serve_later, 0)

    @pl.when(me_z < NZ - 1)
    def _():
        serve(NZ - 1)

    products(me_z)
    back[pl.ds(me_z * 4, 4)] = back_send[me_z]

    def wait_back(n, c):
        z = near_peer(n)
        pltpu.make_async_remote_copy(
            src_ref=back_send.at[z],
            dst_ref=back.at[pl.ds(z * 4, 4)],
            send_sem=back_send_sem.at[z],
            recv_sem=back_sem.at[z],
            device_id=(group_of(me_m, z), me_t),
            device_id_type=MESH,
        ).wait_recv()
        return c

    lax.fori_loop(0, NZ - 1, wait_back, 0)

    low8 = lax.broadcasted_iota(jnp.int32, (8, 128), 1) < 64

    def whole(block):
        a = back[place[2 * block]]
        b = back[place[2 * block + 1]]
        first = jnp.where(low8, a, pltpu.roll(b, 64, 1))
        second = jnp.where(low8, pltpu.roll(a, 64, 1), b)
        return base_proj[block] + jnp.concatenate([first, second], axis=0)

    def proj_copy(dest):
        return pltpu.make_async_remote_copy(
            src_ref=proj_send.at[dest],
            dst_ref=proj.at[me_t],
            send_sem=proj_send_sem.at[dest],
            recv_sem=proj_sem.at[me_t],
            device_id=(me_g, dest),
            device_id_type=MESH,
        )

    def far_y(n):
        step = (n + 1) // 2
        return lax.rem(me_y + NY // 2 + jnp.where(lax.rem(n, 2) == 0, step, NY - step), NY)

    def start_proj(n, c):
        y = far_y(n)
        key = whole(y)
        value = whole(KVH + y).astype(BF16)
        key_high = key.astype(BF16)
        key_low = (key - key_high.astype(F32)).astype(BF16)
        for x in range(2):
            dest = 2 * y + x
            proj_send[dest, 0:16] = key_high
            proj_send[dest, 16:32] = key_low
            proj_send[dest, 32:48] = value
            proj_send[dest, 48:64] = whole(dest).astype(BF16)
        proj_copy(2 * y + 1 - me_x).start()

        @pl.when(y != me_y)
        def _():
            proj_copy(2 * y + me_x).start()

        return c

    lax.fori_loop(0, NY, start_proj, 0)
    proj[me_t] = proj_send[me_t]

    def wait_part(i, c):
        u = t_peer(i)
        pltpu.make_async_remote_copy(
            src_ref=part_send.at[u],
            dst_ref=part.at[u],
            send_sem=part_send_sem.at[i],
            recv_sem=part_sem.at[u],
            device_id=(me_g, u),
            device_id_type=MESH,
        ).wait_recv()
        return c

    lax.fori_loop(1, NT, wait_part, 0)
    logs = part[:, 64:80].astype(F32)[:, 0:8]
    logs = (
        logs
        + jnp.concatenate([logs[:, 2:8], logs[:, 0:2]], axis=1)
        + jnp.concatenate([logs[:, 4:8], logs[:, 0:4]], axis=1)
    )
    top = jnp.max(logs, axis=0)
    grown = jnp.exp2(logs - top[None])
    sub = lax.broadcasted_iota(jnp.int32, (8, 128), 0)
    top_down = jnp.concatenate([top[0:2], top[0:2], top[0:4]], axis=0)
    with_top = jnp.where(sub < 2, grown[0], top_down)
    factors = jnp.concatenate([with_top[None], grown[1:]], axis=0).reshape(NT * 8, 128)
    if NT * 8 < 128:
        factors = jnp.concatenate([factors, jnp.zeros((128 - NT * 8, 128), F32)], axis=0)
    factors = factors.T[0:32]
    sums, totals, peaks = [], [], []
    for r in range(2):
        acc = jnp.zeros((32, HD), F32)
        total = jnp.zeros((32, 1), F32)
        for u in range(NT):
            factor = factors[:, u * 8 + r : u * 8 + r + 1]
            acc = acc + factor * part[u, r * 32 : (r + 1) * 32].astype(F32)
            total = total + factor
        sums.append(acc)
        totals.append(total)
        peaks.append(factors[:, 2 + r : 3 + r])
    cached_ref[:, 0:HD] = jnp.concatenate(sums, axis=0)
    half_lane = lax.broadcasted_iota(jnp.int32, (64, 128), 1) < 64
    cached_ref[:, HD : 2 * HD] = jnp.where(
        half_lane, jnp.concatenate(totals, axis=0), jnp.concatenate(peaks, axis=0)
    )
    q_both = query[:, pl.ds(pl.multiple_of(me_t * 512, 512), 512)].astype(F32)
    own_ref[...] = jnp.concatenate(
        [
            q_both[r * 8 : (r + 1) * 8, h * HD : (h + 1) * HD]
            for r in range(2)
            for h in range(4)
        ],
        axis=0,
    ).astype(BF16)

    def sent_z(n, c):
        hid_copy(near_peer(n)).wait_send()
        back_copy(near_peer(n)).wait_send()
        return c

    def sent_m(i, c):
        weight_copy(lax.rem(me_q + i, 4)).wait_send()
        return c

    def sent_t(i, c):
        part_copy(i).wait_send()
        proj_copy(t_peer(i)).wait_send()
        return c

    lax.fori_loop(0, NZ - 1, sent_z, 0)
    lax.fori_loop(1, 4, sent_m, 0)
    lax.fori_loop(1, NT, sent_t, 0)

    def wait_proj(i, c):
        u = t_peer(i)
        pltpu.make_async_remote_copy(
            src_ref=proj_send.at[u],
            dst_ref=proj.at[u],
            send_sem=proj_send_sem.at[u],
            recv_sem=proj_sem.at[u],
            device_id=(me_g, u),
            device_id_type=MESH,
        ).wait_recv()
        return c

    lax.fori_loop(1, NT, wait_proj, 0)
    summed = jnp.sum(proj[...].astype(F32), axis=0)
    fresh_ref[0] = (summed[0:16] + summed[16:32]).astype(BF16)
    fresh_ref[1] = summed[32:48].astype(BF16)
    fresh_ref[2] = summed[48:64].astype(BF16)


def finish(fresh_ref, cached_ref, own_ref, new_ref, att_ref):
    scale = HD ** (-0.5) * LOG2_E
    new_ref[...] = fresh_ref[2]
    cache_sum = cached_ref[:, 0:HD]
    cache_total = cached_ref[:, HD : HD + 1]
    cache_peak = cached_ref[:, HD + 64 : HD + 65]
    near = nt_dot(own_ref[...], fresh_ref[0]) * scale
    at = lax.broadcasted_iota(jnp.int32, (64, 16), 0)
    to = lax.broadcasted_iota(jnp.int32, (64, 16), 1)
    causal = (at // 32 == to // 8) & (lax.rem(at, 8) >= lax.rem(to, 8))
    near = jnp.where(causal, near, NEGATIVE)
    near_peak = jnp.max(near, axis=1, keepdims=True)
    near_weights = jnp.exp2(near - near_peak)
    near_total = jnp.sum(near_weights, axis=1, keepdims=True)
    near_sum = jnp.dot(near_weights.astype(BF16), fresh_ref[1], preferred_element_type=F32)
    joined = jnp.maximum(cache_peak, near_peak)
    cache_scale = jnp.exp2(cache_peak - joined)
    near_scale = jnp.exp2(near_peak - joined)
    numerator = cache_sum * cache_scale + near_sum * near_scale
    denominator = cache_total * cache_scale + near_total * near_scale
    result = numerator / denominator
    att_ref[...] = jnp.concatenate(
        [
            jnp.concatenate(
                [result[r * 32 + h * 8 : r * 32 + h * 8 + 8] for h in range(4)], axis=1
            )
            for r in range(2)
        ],
        axis=0,
    ).astype(BF16)


def on_device(
    hidden_x, base_weight, delta_codes, delta_scales, owner_map, kv_cache, queries, lengths
):
    NG = lax.axis_size("group")
    NT = lax.axis_size("tensor")
    NZ = NG // 4
    rows, steps, width = hidden_x.shape
    tokens = rows * steps
    positions = kv_cache.shape[1]
    any_space = pl.BlockSpec(memory_space=pl.ANY)
    vmem = pl.BlockSpec(memory_space=pltpu.VMEM)
    dma = pltpu.SemaphoreType.DMA

    def in_hbm(x):
        return pltpu.with_memory_space_constraint(x, pltpu.HBM)

    fresh, cached, own_query = pl.pallas_call(
        functools.partial(kernel, NG, NT),
        out_shape=(
            pltpu.VMEM((3, tokens, 128), BF16),
            pltpu.VMEM((64, 256), F32),
            pltpu.VMEM((64, 128), BF16),
        ),
        in_specs=[any_space] * 8,
        out_specs=(vmem, vmem, vmem),
        scratch_shapes=[
            pltpu.VMEM((NZ, tokens, width), BF16),
            pltpu.VMEM(base_weight.shape, BF16),
            pltpu.VMEM(delta_codes.shape, BF16),
            pltpu.VMEM(delta_scales.shape[::-1], BF16),
            pltpu.SMEM(owner_map.shape, jnp.int32),
            pltpu.SMEM(lengths.shape, jnp.int32),
            pltpu.VMEM((rows * positions, kv_cache.shape[2]), BF16),
            pltpu.VMEM((tokens, queries.shape[2]), BF16),
            pltpu.VMEM((4, 64, width), BF16),
            pltpu.SMEM((NG,), jnp.int32),
            pltpu.VMEM((NZ, 4, 8, 128), F32),
            pltpu.VMEM((NZ * 4, 8, 128), F32),
            pltpu.VMEM((NT, tokens, 128), F32),
            pltpu.VMEM((NT, 4 * tokens, 128), BF16),
            pltpu.VMEM((NT, 4 * tokens, 128), BF16),
            pltpu.VMEM((NT, 80, HD), BF16),
            pltpu.VMEM((NT, 80, HD), BF16),
            pltpu.VMEM((128, 128), F32),
            dma((8,)),
            dma((NZ,)),
            dma((NZ,)),
            dma((4,)),
            dma((4,)),
            dma((NZ,)),
            dma((NZ,)),
            dma((NT,)),
            dma((NT,)),
            dma((NT,)),
            dma((NT,)),
            pltpu.SemaphoreType.REGULAR((NZ,)),
            pltpu.SemaphoreType.REGULAR,
            pltpu.SemaphoreType.REGULAR,
            pltpu.SemaphoreType.REGULAR((4,)),
        ],
        compiler_params=pltpu.CompilerParams(
            collective_id=0, has_side_effects=True, vmem_limit_bytes=48 * 1024 * 1024
        ),
    )(
        in_hbm(hidden_x.reshape(tokens, width)),
        in_hbm(base_weight),
        in_hbm(delta_codes),
        in_hbm(delta_scales.T),
        in_hbm(owner_map),
        in_hbm(kv_cache.reshape(rows * positions, kv_cache.shape[2])),
        in_hbm(queries.reshape(tokens, queries.shape[2])),
        in_hbm(lengths),
    )
    new_kv, attended = pl.pallas_call(
        finish,
        out_shape=(
            jax.ShapeDtypeStruct((tokens, 128), BF16),
            jax.ShapeDtypeStruct((tokens, 512), BF16),
        ),
        in_specs=[vmem, vmem, vmem],
        out_specs=(vmem, vmem),
        compiler_params=pltpu.CompilerParams(vmem_limit_bytes=8 * 1024 * 1024),
    )(fresh, cached, own_query)
    return new_kv.reshape(rows, steps, 128), attended.reshape(rows, steps, 512)


def solution(mesh):
    in_specs = (
        P("group", None, "tensor"),
        P(None, "tensor"),
        P("group", "tensor"),
        P("group", "tensor"),
        P(),
        P("group", "tensor", None),
        P("group", None, None),
        P("group"),
    )
    out_specs = (P("group", None, "tensor"), P("group", None, "tensor"))
    return jax.shard_map(
        on_device, mesh=mesh, in_specs=in_specs, out_specs=out_specs, check_vma=False
    )
```

```python
import functools

import jax
import jax.numpy as jnp
from jax import lax
from jax.experimental import pallas as pl
from jax.experimental.pallas import tpu as pltpu
from jax.sharding import PartitionSpec as P

HD = 128
NEGATIVE = -1e30
LOG2_E = 1.4426950408889634
MESH = pl.DeviceIdType.MESH
F32 = jnp.float32
BF16 = jnp.bfloat16


def nt_dot(a, b):
    return lax.dot_general(a, b, (((1,), (1,)), ((), ())), preferred_element_type=F32)


def kernel(
    NG,
    NT,
    hid_hbm,
    base_hbm,
    codes_hbm,
    scales_hbm,
    owner_hbm,
    cache_hbm,
    query_hbm,
    lengths_hbm,
    fresh_ref,
    cached_ref,
    own_ref,
    hid,
    base,
    codes,
    scales_ref,
    owner_ref,
    lengths_ref,
    cache,
    query,
    weight,
    place,
    odd_place,
    back_send,
    back,
    base_proj,
    proj_send,
    proj,
    part_send,
    part,
    lse_cols,
    load_sem,
    hid_send_sem,
    hid_sem,
    relay_send_sem,
    weight_send_sem,
    weight_sem,
    back_send_sem,
    back_sem,
    proj_send_sem,
    proj_sem,
    part_send_sem,
    part_sem,
    ready_z,
    ready_t,
    ready_x,
    ready_m,
):
    NZ = NG // 4
    NY = NT // 2
    KVH = NT // 2
    POS = cache.shape[0] // 2
    KVW = KVH * HD
    width = hid.shape[2]
    scale = HD ** (-0.5) * LOG2_E
    me_g = lax.axis_index("group")
    me_t = lax.axis_index("tensor")
    core = lax.rem(me_g, 2)
    me_z = lax.rem(me_g // 2, NZ)
    me_m = me_g // (2 * NZ) * 2 + core
    me_y = me_t // 2
    me_x = lax.rem(me_t, 2)

    def group_of(m, z):
        return (m // 2) * (2 * NZ) + z * 2 + lax.rem(m, 2)

    def near_peer(n):
        step = n // 2 + 1
        return lax.rem(me_z + jnp.where(lax.rem(n, 2) == 0, step, NZ - step), NZ)

    def t_peer(i):
        return lax.rem(me_t + i, NT)

    me_q = me_m + 1 - 2 * core

    def m_at(q):
        return q + 1 - 2 * lax.rem(q, 2)

    last_y = NY // 2
    at_last_y = me_y == last_y
    herald = at_last_y & (me_x == 0)
    greeted = me_z + me_q + jnp.where(at_last_y, NY - 1 + me_x, 0)
    barrier = pltpu.get_barrier_semaphore()

    def greet_m(q, c):
        pl.semaphore_signal(
            barrier, inc=1, device_id=(group_of(m_at(q), me_z), me_t), device_id_type=MESH
        )
        return c

    def greet_z(z, c):
        pl.semaphore_signal(
            barrier, inc=1, device_id=(group_of(me_m, z), me_t), device_id_type=MESH
        )
        return c

    def answer_z(z, c):
        pl.semaphore_signal(
            ready_z.at[me_z], inc=1, device_id=(group_of(me_m, z), me_t), device_id_type=MESH
        )
        return c

    def answer_m(q, c):
        pl.semaphore_signal(
            ready_m.at[me_q],
            inc=1,
            device_id=(group_of(m_at(q), me_z), me_t),
            device_id_type=MESH,
        )
        return c

    def answer_t(i, c):
        @pl.when(order_of(t_peer(i)) < order)
        def _():
            pl.semaphore_signal(ready_t, inc=1, device_id=(me_g, t_peer(i)), device_id_type=MESH)

        return c

    loads = [
        pltpu.make_async_copy(codes_hbm, codes, load_sem.at[0]),
        pltpu.make_async_copy(hid_hbm, hid.at[me_z], load_sem.at[1]),
        pltpu.make_async_copy(query_hbm, query, load_sem.at[2]),
        pltpu.make_async_copy(cache_hbm, cache, load_sem.at[3]),
        pltpu.make_async_copy(base_hbm, base, load_sem.at[4]),
        pltpu.make_async_copy(scales_hbm, scales_ref, load_sem.at[5]),
        pltpu.make_async_copy(owner_hbm, owner_ref, load_sem.at[6]),
        pltpu.make_async_copy(lengths_hbm, lengths_ref, load_sem.at[7]),
    ]
    loads[5].start()
    loads[0].start()
    loads[1].start()
    lax.fori_loop(me_q + 1, 4, greet_m, 0)
    lax.fori_loop(me_z + 1, NZ, greet_z, 0)

    @pl.when(jnp.logical_not(at_last_y))
    def _():
        pl.semaphore_signal(
            barrier, inc=1, device_id=(me_g, 2 * last_y + me_x), device_id_type=MESH
        )

    @pl.when(herald)
    def _():
        pl.semaphore_signal(
            barrier, inc=1, device_id=(me_g, 2 * last_y + 1), device_id_type=MESH
        )

    for load in loads[2:5] + loads[6:]:
        load.start()

    @pl.when(greeted > 0)
    def _():
        pl.semaphore_wait(barrier, greeted)

    lax.fori_loop(0, me_q, answer_m, 0)
    lax.fori_loop(0, me_z, answer_z, 0)

    @pl.when(at_last_y & (me_x == 1))
    def _():
        pl.semaphore_signal(ready_x, inc=1, device_id=(me_g, 2 * last_y), device_id_type=MESH)

    unit = (
        lax.broadcasted_iota(jnp.int32, (64, 64), 0) == lax.broadcasted_iota(jnp.int32, (64, 64), 1)
    ).astype(BF16)
    loads[5].wait()
    scale_cols = nt_dot(unit, scales_ref[...])
    loads[0].wait()
    weight[me_m] = jnp.concatenate(
        [
            codes[:, j * 128 : (j + 1) * 128].astype(F32) * scale_cols[:, j : j + 1]
            for j in range(width // 128)
        ],
        axis=1,
    ).astype(BF16)
    loads[1].wait()

    def hid_copy(z):
        return pltpu.make_async_remote_copy(
            src_ref=hid.at[me_z],
            dst_ref=hid.at[me_z],
            send_sem=hid_send_sem.at[z],
            recv_sem=hid_sem.at[me_z],
            device_id=(group_of(me_m, z), me_t),
            device_id_type=MESH,
        )

    def wait_hid(z):
        pltpu.make_async_remote_copy(
            src_ref=hid.at[z],
            dst_ref=hid.at[z],
            send_sem=hid_send_sem.at[z],
            recv_sem=hid_sem.at[z],
            device_id=(group_of(me_m, z), me_t),
            device_id_type=MESH,
        ).wait_recv()

    def weight_copy(q):
        return pltpu.make_async_remote_copy(
            src_ref=weight.at[me_m],
            dst_ref=weight.at[me_m],
            send_sem=weight_send_sem.at[q],
            recv_sem=weight_sem.at[me_m],
            device_id=(group_of(m_at(q), me_z), me_t),
            device_id_type=MESH,
        )

    def start_weight(q):
        @pl.when(q > me_q)
        def _():
            pl.semaphore_wait(ready_m.at[q], 1)

        weight_copy(q).start()

    def wait_weight(i, c):
        q = lax.rem(me_q + i, 4)
        m = m_at(q)
        pltpu.make_async_remote_copy(
            src_ref=weight.at[m],
            dst_ref=weight.at[m],
            send_sem=weight_send_sem.at[q],
            recv_sem=weight_sem.at[m],
            device_id=(group_of(m, me_z), me_t),
            device_id_type=MESH,
        ).wait_recv()
        return c

    def start_hid_earlier(n, c):
        @pl.when(near_peer(n) < me_z)
        def _():
            hid_copy(near_peer(n)).start()

        return c

    middle = NZ // 4
    far = 2 * middle
    relays = (me_z >= middle) & (me_z + middle < NZ) & (middle > 0)

    def straight(z):
        return (z != me_z + far) | (middle == 0)

    def start_hid_later(z, c):
        @pl.when(straight(z))
        def _():
            pl.semaphore_wait(ready_z.at[z], 1)
            hid_copy(z).start()

        return c

    relay_step = jnp.where(me_z < far, max(KVH // 2 - 2, middle - 1), KVH // 2 - 1)

    def relay_copy():
        z = jnp.maximum(me_z - middle, 0)
        return pltpu.make_async_remote_copy(
            src_ref=hid.at[z],
            dst_ref=hid.at[z],
            send_sem=relay_send_sem.at[0],
            recv_sem=hid_sem.at[z],
            device_id=(group_of(me_m, lax.rem(me_z + middle, NZ)), me_t),
            device_id_type=MESH,
        )

    def relay():
        wait_hid(me_z - middle)
        relay_copy().start()

    start_weight(lax.rem(me_q + 2, 4))
    start_weight(3 - me_q)
    start_weight(me_q + 1 - 2 * lax.rem(me_q, 2))

    lax.fori_loop(0, NZ - 1, start_hid_earlier, 0)

    def back_copy(z):
        return pltpu.make_async_remote_copy(
            src_ref=back_send.at[z],
            dst_ref=back.at[pl.ds(me_z * 2, 2)],
            send_sem=back_send_sem.at[z],
            recv_sem=back_sem.at[me_z],
            device_id=(group_of(me_m, z), me_t),
            device_id_type=MESH,
        )

    def products(z):
        product = nt_dot(hid[z], weight[...].reshape(4 * 64, width))
        low = lax.broadcasted_iota(jnp.int32, (8, 128), 1) < 64
        for j in range(2):
            first = product[0:8, j * 128 : (j + 1) * 128]
            second = product[8:16, j * 128 : (j + 1) * 128]
            even = jnp.where(low, first, pltpu.roll(second, 64, 1))
            odd = jnp.where(low, pltpu.roll(first, 64, 1), second)
            back_send[z, j] = jnp.concatenate([even, odd], axis=0).astype(BF16)

    def serve(z):
        @pl.when(jnp.logical_not(relays & (z == me_z - middle)))
        def _():
            wait_hid(z)

        products(z)
        back_copy(z).start()

    def serve_peer(n):
        return lax.rem(me_z + 1 + n, NZ)

    def serve_earlier(n, c):
        @pl.when(serve_peer(n) < me_z)
        def _():
            serve(serve_peer(n))

        return c

    def serve_later(n, c):
        z = serve_peer(n)

        @pl.when((z > me_z) & (z < NZ - 1))
        def _():
            serve(z)

        return c

    last = me_z == NZ - 1

    between = KVH // 2 - 1

    def find(b):
        spot = jnp.int32(0)
        for g in range(NG):
            at = (((g // 2) % NZ) * 2 + g // (2 * NZ)) * 2 + g % 2
            spot = jnp.where(owner_ref[g] == b, jnp.int32(at), spot)
        place[b] = lax.div(spot, jnp.int32(2))
        odd_place[b] = lax.rem(spot, jnp.int32(2))

    lane = lax.broadcasted_iota(jnp.int32, (32, 128), 1)
    position = me_t * POS + lax.broadcasted_iota(jnp.int32, (64, POS), 1)
    own_rows = hid[me_z]
    for load in loads[2:5] + loads[6:]:
        load.wait()

    def cached(i, columns):
        for n in range(2):
            k = 2 * i + n
            q_both = query[:, pl.ds(pl.multiple_of(k * 1024, 1024), 1024)].astype(F32)
            for r in range(2):
                q = jnp.concatenate(
                    [q_both[r * 8 : (r + 1) * 8, h * HD : (h + 1) * HD] for h in range(8)], axis=0
                ).astype(BF16)
                keys = cache[r * POS : (r + 1) * POS, pl.ds(pl.multiple_of(k * HD, HD), HD)]
                values = cache[
                    r * POS : (r + 1) * POS, pl.ds(pl.multiple_of(KVW + k * HD, HD), HD)
                ]
                scores = jnp.where(position < lengths_ref[r], nt_dot(q, keys) * scale, NEGATIVE)
                peak = jnp.max(scores, axis=1, keepdims=True)
                weights = jnp.exp2(scores - peak)
                total = jnp.sum(weights, axis=1, keepdims=True)
                weighted = jnp.dot(weights.astype(BF16), values, preferred_element_type=F32)
                mean = (weighted * (1.0 / total)).astype(BF16)
                some = me_t * POS < lengths_ref[r]
                log_sum = jnp.where(some, peak + jnp.log2(total), NEGATIVE)
                for half in range(2):
                    dest = 2 * k + half
                    part_send[dest, r * 32 : (r + 1) * 32] = mean[half * 32 : (half + 1) * 32]
                    columns = jnp.where(
                        lane == dest * 8 + r, log_sum[half * 32 : (half + 1) * 32], columns
                    )
            rows = base[pl.ds(pl.multiple_of(k * 256, 256), 256), :]
            tile = nt_dot(own_rows, rows)
            base_proj[2 * k] = tile[:, :128]
            base_proj[2 * k + 1] = tile[:, 128:]
            for m in range(NG // KVH):
                find(k * (NG // KVH) + m)

        @pl.when(me_z + 1 + i < jnp.minimum(NZ - 1, me_z + KVH // 2))
        def _():
            start_hid_later(me_z + 1 + i, 0)

        @pl.when(relays & (i == relay_step) & (me_z + middle < NZ - 1))
        def _():
            relay()

        @pl.when(last & (i == 1))
        def _():
            lax.fori_loop(1, 4, wait_weight, 0)

        @pl.when(last & (i >= 1))
        def _():
            serve(i - 1)

        return columns

    def tell(i, c):
        pl.semaphore_signal(ready_t, inc=1, device_id=(me_g, t_peer(i)), device_id_type=MESH)
        return c

    @pl.when(herald)
    def _():
        pl.semaphore_wait(ready_x, 1)
        lax.fori_loop(1, NT, tell, 0)

    lse_cols[...] = jnp.zeros_like(lse_cols)
    lse_cols[0:32] = lax.fori_loop(0, KVH // 2, cached, jnp.zeros((32, 128), F32))

    def part_copy(i):
        dest = t_peer(i)
        return pltpu.make_async_remote_copy(
            src_ref=part_send.at[dest],
            dst_ref=part.at[me_t],
            send_sem=part_send_sem.at[i],
            recv_sem=part_sem.at[me_t],
            device_id=(me_g, dest),
            device_id_type=MESH,
        )

    def start_part(i, c):
        part_copy(i).start()
        return c

    def start_parts():
        logs = lse_cols[...].T[: NT * 8].reshape(NT, 8, 128)
        sub = lax.broadcasted_iota(jnp.int32, (NT, 8, 128), 1)
        high = logs.astype(BF16).astype(F32)
        rest = logs - high
        middle = rest.astype(BF16).astype(F32)
        low = rest - middle
        middle = jnp.concatenate([middle[:, 0:2], middle[:, 0:2], middle[:, 0:4]], axis=1)
        low = jnp.concatenate([low[:, 0:4], low[:, 0:2], low[:, 0:2]], axis=1)
        rows = jnp.where(sub < 2, high, jnp.where(sub < 4, middle, low))
        part_send[:, 64:80] = jnp.concatenate([rows, rows], axis=1).astype(BF16)

        @pl.when(jnp.logical_not(herald))
        def _():
            pl.semaphore_wait(ready_t, 1)

        lax.fori_loop(1, NT, start_part, 0)
        part[me_t] = part_send[me_t]

    parts_first = (me_z < NZ // 2) & (jnp.abs(me_y - last_y) < 2)

    @pl.when(parts_first)
    def _():
        start_parts()

    lax.fori_loop(me_z + KVH // 2, NZ - 1, start_hid_later, 0)

    @pl.when((me_z >= NZ // 2) & (me_z < NZ - 1))
    def _():
        start_hid_later(NZ - 1, 0)

    @pl.when(relays & (me_z + middle == NZ - 1))
    def _():
        relay()

    @pl.when(jnp.logical_not(last) | (between == 0))
    def _():
        lax.fori_loop(1, 4, wait_weight, 0)

    @pl.when(last)
    def _():
        serve(between)
        start_parts()

    lax.fori_loop(jnp.where(last, between + 1, 0), NZ - 1, serve_earlier, 0)

    @pl.when((me_z >= NZ // 2) & jnp.logical_not(last))
    def _():
        start_parts()

    @pl.when(me_z < NZ // 2)
    def _():
        start_hid_later(NZ - 1, 0)

    @pl.when((me_z < NZ // 2) & jnp.logical_not(parts_first))
    def _():
        start_parts()

    lax.fori_loop(0, NZ - 1, serve_later, 0)

    @pl.when(me_z < NZ - 1)
    def _():
        serve(NZ - 1)

    products(me_z)
    back[pl.ds(me_z * 2, 2)] = back_send[me_z]

    def wait_back(n, c):
        z = near_peer(n)
        pltpu.make_async_remote_copy(
            src_ref=back_send.at[z],
            dst_ref=back.at[pl.ds(z * 2, 2)],
            send_sem=back_send_sem.at[z],
            recv_sem=back_sem.at[z],
            device_id=(group_of(me_m, z), me_t),
            device_id_type=MESH,
        ).wait_recv()
        return c

    lax.fori_loop(0, NZ - 1, wait_back, 0)

    low8 = lax.broadcasted_iota(jnp.int32, (8, 128), 1) < 64

    def returned(block):
        both = back[place[block]].astype(F32)
        return jnp.where(odd_place[block] == 0, both[0:8], both[8:16])

    def whole(block):
        a = returned(2 * block)
        b = returned(2 * block + 1)
        first = jnp.where(low8, a, pltpu.roll(b, 64, 1))
        second = jnp.where(low8, pltpu.roll(a, 64, 1), b)
        return base_proj[block] + jnp.concatenate([first, second], axis=0)

    def proj_copy(dest):
        return pltpu.make_async_remote_copy(
            src_ref=proj_send.at[dest],
            dst_ref=proj.at[me_t],
            send_sem=proj_send_sem.at[dest],
            recv_sem=proj_sem.at[me_t],
            device_id=(me_g, dest),
            device_id_type=MESH,
        )

    def far_y(n):
        step = (n + 1) // 2
        return lax.rem(me_y + NY // 2 + jnp.where(lax.rem(n, 2) == 0, step, NY - step), NY)

    def start_proj(n, c):
        y = far_y(n)
        key = whole(y)
        value = whole(KVH + y).astype(BF16)
        key_high = key.astype(BF16)
        key_low = (key - key_high.astype(F32)).astype(BF16)
        for x in range(2):
            dest = 2 * y + x
            proj_send[dest, 0:16] = key_high
            proj_send[dest, 16:32] = key_low
            proj_send[dest, 32:48] = value
            proj_send[dest, 48:64] = whole(dest).astype(BF16)
        proj_copy(2 * y + 1 - me_x).start()

        @pl.when(y != me_y)
        def _():
            proj_copy(2 * y + me_x).start()

        return c

    lax.fori_loop(0, NY, start_proj, 0)
    proj[me_t] = proj_send[me_t]

    def wait_part(i, c):
        u = t_peer(i)
        pltpu.make_async_remote_copy(
            src_ref=part_send.at[u],
            dst_ref=part.at[u],
            send_sem=part_send_sem.at[i],
            recv_sem=part_sem.at[u],
            device_id=(me_g, u),
            device_id_type=MESH,
        ).wait_recv()
        return c

    lax.fori_loop(1, NT, wait_part, 0)
    logs = part[:, 64:80].astype(F32)[:, 0:8]
    logs = (
        logs
        + jnp.concatenate([logs[:, 2:8], logs[:, 0:2]], axis=1)
        + jnp.concatenate([logs[:, 4:8], logs[:, 0:4]], axis=1)
    )
    top = jnp.max(logs, axis=0)
    grown = jnp.exp2(logs - top[None])
    sub = lax.broadcasted_iota(jnp.int32, (8, 128), 0)
    top_down = jnp.concatenate([top[0:2], top[0:2], top[0:4]], axis=0)
    with_top = jnp.where(sub < 2, grown[0], top_down)
    factors = jnp.concatenate([with_top[None], grown[1:]], axis=0).reshape(NT * 8, 128)
    if NT * 8 < 128:
        factors = jnp.concatenate([factors, jnp.zeros((128 - NT * 8, 128), F32)], axis=0)
    factors = factors.T[0:32]
    sums, totals, peaks = [], [], []
    for r in range(2):
        acc = jnp.zeros((32, HD), F32)
        total = jnp.zeros((32, 1), F32)
        for u in range(NT):
            factor = factors[:, u * 8 + r : u * 8 + r + 1]
            acc = acc + factor * part[u, r * 32 : (r + 1) * 32].astype(F32)
            total = total + factor
        sums.append(acc)
        totals.append(total)
        peaks.append(factors[:, 2 + r : 3 + r])
    cached_ref[:, 0:HD] = jnp.concatenate(sums, axis=0)
    half_lane = lax.broadcasted_iota(jnp.int32, (64, 128), 1) < 64
    cached_ref[:, HD : 2 * HD] = jnp.where(
        half_lane, jnp.concatenate(totals, axis=0), jnp.concatenate(peaks, axis=0)
    )
    q_both = query[:, pl.ds(pl.multiple_of(me_t * 512, 512), 512)].astype(F32)
    own_ref[...] = jnp.concatenate(
        [
            q_both[r * 8 : (r + 1) * 8, h * HD : (h + 1) * HD]
            for r in range(2)
            for h in range(4)
        ],
        axis=0,
    ).astype(BF16)

    def sent_z(n, c):
        z = near_peer(n)

        @pl.when(straight(z))
        def _():
            hid_copy(z).wait_send()

        @pl.when(jnp.logical_not(straight(z)))
        def _():
            pl.semaphore_wait(ready_z.at[z], 1)

        back_copy(z).wait_send()
        return c

    def sent_m(i, c):
        weight_copy(lax.rem(me_q + i, 4)).wait_send()
        return c

    def sent_t(i, c):
        part_copy(i).wait_send()
        proj_copy(t_peer(i)).wait_send()
        return c

    lax.fori_loop(0, NZ - 1, sent_z, 0)

    @pl.when(relays)
    def _():
        relay_copy().wait_send()

    lax.fori_loop(1, 4, sent_m, 0)
    lax.fori_loop(1, NT, sent_t, 0)

    def wait_proj(i, c):
        u = lax.rem(2 * (last_y + 1) + i, NT)

        @pl.when(u != me_t)
        def _():
            pltpu.make_async_remote_copy(
                src_ref=proj_send.at[u],
                dst_ref=proj.at[u],
                send_sem=proj_send_sem.at[u],
                recv_sem=proj_sem.at[u],
                device_id=(me_g, u),
                device_id_type=MESH,
            ).wait_recv()

        return c

    lax.fori_loop(0, NT, wait_proj, 0)
    summed = jnp.sum(proj[...].astype(F32), axis=0)
    fresh_ref[0] = (summed[0:16] + summed[16:32]).astype(BF16)
    fresh_ref[1] = summed[32:48].astype(BF16)
    fresh_ref[2] = summed[48:64].astype(BF16)


def finish(fresh_ref, cached_ref, own_ref, new_ref, att_ref):
    scale = HD ** (-0.5) * LOG2_E
    new_ref[...] = fresh_ref[2]
    cache_sum = cached_ref[:, 0:HD]
    cache_total = cached_ref[:, HD : HD + 1]
    cache_peak = cached_ref[:, HD + 64 : HD + 65]
    near = nt_dot(own_ref[...], fresh_ref[0]) * scale
    at = lax.broadcasted_iota(jnp.int32, (64, 16), 0)
    to = lax.broadcasted_iota(jnp.int32, (64, 16), 1)
    causal = (at // 32 == to // 8) & (lax.rem(at, 8) >= lax.rem(to, 8))
    near = jnp.where(causal, near, NEGATIVE)
    near_peak = jnp.max(near, axis=1, keepdims=True)
    near_weights = jnp.exp2(near - near_peak)
    near_total = jnp.sum(near_weights, axis=1, keepdims=True)
    near_sum = jnp.dot(near_weights.astype(BF16), fresh_ref[1], preferred_element_type=F32)
    joined = jnp.maximum(cache_peak, near_peak)
    cache_scale = jnp.exp2(cache_peak - joined)
    near_scale = jnp.exp2(near_peak - joined)
    numerator = cache_sum * cache_scale + near_sum * near_scale
    denominator = cache_total * cache_scale + near_total * near_scale
    result = numerator / denominator
    att_ref[...] = jnp.concatenate(
        [
            jnp.concatenate(
                [result[r * 32 + h * 8 : r * 32 + h * 8 + 8] for h in range(4)], axis=1
            )
            for r in range(2)
        ],
        axis=0,
    ).astype(BF16)


def on_device(
    hidden_x, base_weight, delta_codes, delta_scales, owner_map, kv_cache, queries, lengths
):
    NG = lax.axis_size("group")
    NT = lax.axis_size("tensor")
    NZ = NG // 4
    rows, steps, width = hidden_x.shape
    tokens = rows * steps
    positions = kv_cache.shape[1]
    any_space = pl.BlockSpec(memory_space=pl.ANY)
    vmem = pl.BlockSpec(memory_space=pltpu.VMEM)
    dma = pltpu.SemaphoreType.DMA

    def in_hbm(x):
        return pltpu.with_memory_space_constraint(x, pltpu.HBM)

    fresh, cached, own_query = pl.pallas_call(
        functools.partial(kernel, NG, NT),
        out_shape=(
            pltpu.VMEM((3, tokens, 128), BF16),
            pltpu.VMEM((64, 256), F32),
            pltpu.VMEM((64, 128), BF16),
        ),
        in_specs=[any_space] * 8,
        out_specs=(vmem, vmem, vmem),
        scratch_shapes=[
            pltpu.VMEM((NZ, tokens, width), BF16),
            pltpu.VMEM(base_weight.shape, BF16),
            pltpu.VMEM(delta_codes.shape, BF16),
            pltpu.VMEM(delta_scales.shape[::-1], BF16),
            pltpu.SMEM(owner_map.shape, jnp.int32),
            pltpu.SMEM(lengths.shape, jnp.int32),
            pltpu.VMEM((rows * positions, kv_cache.shape[2]), BF16),
            pltpu.VMEM((tokens, queries.shape[2]), BF16),
            pltpu.VMEM((4, 64, width), BF16),
            pltpu.SMEM((NG,), jnp.int32),
            pltpu.SMEM((NG,), jnp.int32),
            pltpu.VMEM((NZ, 2, 16, 128), BF16),
            pltpu.VMEM((NZ * 2, 16, 128), BF16),
            pltpu.VMEM((NT, tokens, 128), F32),
            pltpu.VMEM((NT, 4 * tokens, 128), BF16),
            pltpu.VMEM((NT, 4 * tokens, 128), BF16),
            pltpu.VMEM((NT, 80, HD), BF16),
            pltpu.VMEM((NT, 80, HD), BF16),
            pltpu.VMEM((128, 128), F32),
            dma((8,)),
            dma((NZ,)),
            dma((NZ,)),
            dma((1,)),
            dma((4,)),
            dma((4,)),
            dma((NZ,)),
            dma((NZ,)),
            dma((NT,)),
            dma((NT,)),
            dma((NT,)),
            dma((NT,)),
            pltpu.SemaphoreType.REGULAR((NZ,)),
            pltpu.SemaphoreType.REGULAR,
            pltpu.SemaphoreType.REGULAR,
            pltpu.SemaphoreType.REGULAR((4,)),
        ],
        compiler_params=pltpu.CompilerParams(
            collective_id=0, has_side_effects=True, vmem_limit_bytes=48 * 1024 * 1024
        ),
    )(
        in_hbm(hidden_x.reshape(tokens, width)),
        in_hbm(base_weight),
        in_hbm(delta_codes),
        in_hbm(delta_scales.T),
        in_hbm(owner_map),
        in_hbm(kv_cache.reshape(rows * positions, kv_cache.shape[2])),
        in_hbm(queries.reshape(tokens, queries.shape[2])),
        in_hbm(lengths),
    )
    new_kv, attended = pl.pallas_call(
        finish,
        out_shape=(
            jax.ShapeDtypeStruct((tokens, 128), BF16),
            jax.ShapeDtypeStruct((tokens, 512), BF16),
        ),
        in_specs=[vmem, vmem, vmem],
        out_specs=(vmem, vmem),
        compiler_params=pltpu.CompilerParams(vmem_limit_bytes=8 * 1024 * 1024),
    )(fresh, cached, own_query)
    return new_kv.reshape(rows, steps, 128), attended.reshape(rows, steps, 512)


def solution(mesh):
    in_specs = (
        P("group", None, "tensor"),
        P(None, "tensor"),
        P("group", "tensor"),
        P("group", "tensor"),
        P(),
        P("group", "tensor", None),
        P("group", None, None),
        P("group"),
    )
    out_specs = (P("group", None, "tensor"), P("group", None, "tensor"))
    return jax.shard_map(
        on_device, mesh=mesh, in_specs=in_specs, out_specs=out_specs, check_vma=False
    )
```

```python
import functools

import jax
import jax.numpy as jnp
from jax import lax
from jax.experimental import pallas as pl
from jax.experimental.pallas import tpu as pltpu
from jax.sharding import PartitionSpec as P

HD = 128
NEGATIVE = -1e30
LOG2_E = 1.4426950408889634
MESH = pl.DeviceIdType.MESH
F32 = jnp.float32
BF16 = jnp.bfloat16


def nt_dot(a, b):
    return lax.dot_general(a, b, (((1,), (1,)), ((), ())), preferred_element_type=F32)


def kernel(
    NG,
    NT,
    hid_hbm,
    base_hbm,
    codes_hbm,
    scales_ref,
    owner_hbm,
    cache_hbm,
    query_hbm,
    lengths_hbm,
    fresh_ref,
    cached_ref,
    own_ref,
    hid,
    base,
    codes,
    owner_ref,
    lengths_ref,
    cache,
    query,
    weight,
    place,
    odd_place,
    back_send,
    back,
    base_proj,
    proj_send,
    proj,
    part_send,
    part,
    lse_cols,
    load_sem,
    hid_send_sem,
    hid_sem,
    relay_send_sem,
    weight_send_sem,
    weight_sem,
    back_send_sem,
    back_sem,
    proj_send_sem,
    proj_sem,
    part_send_sem,
    part_sem,
    ready_z,
    ready_t,
    ready_x,
    ready_m,
):
    NZ = NG // 4
    NY = NT // 2
    KVH = NT // 2
    POS = cache.shape[0] // 2
    KVW = KVH * HD
    width = hid.shape[2]
    scale = HD ** (-0.5) * LOG2_E
    me_g = lax.axis_index("group")
    me_t = lax.axis_index("tensor")
    core = lax.rem(me_g, 2)
    me_z = lax.rem(me_g // 2, NZ)
    me_m = me_g // (2 * NZ) * 2 + core
    me_y = me_t // 2
    me_x = lax.rem(me_t, 2)

    def group_of(m, z):
        return (m // 2) * (2 * NZ) + z * 2 + lax.rem(m, 2)

    def near_peer(n):
        step = n // 2 + 1
        return lax.rem(me_z + jnp.where(lax.rem(n, 2) == 0, step, NZ - step), NZ)

    def t_peer(i):
        return lax.rem(me_t + i, NT)

    me_q = me_m + 1 - 2 * core

    def m_at(q):
        return q + 1 - 2 * lax.rem(q, 2)

    last_y = NY // 2
    at_last_y = me_y == last_y
    herald = at_last_y & (me_x == 0)
    greeted = me_z + me_q + jnp.where(at_last_y, NY - 1 + me_x, 0)
    barrier = pltpu.get_barrier_semaphore()

    def greet_m(q, c):
        pl.semaphore_signal(
            barrier, inc=1, device_id=(group_of(m_at(q), me_z), me_t), device_id_type=MESH
        )
        return c

    def greet_z(z, c):
        pl.semaphore_signal(
            barrier, inc=1, device_id=(group_of(me_m, z), me_t), device_id_type=MESH
        )
        return c

    def answer_z(z, c):
        pl.semaphore_signal(
            ready_z.at[me_z], inc=1, device_id=(group_of(me_m, z), me_t), device_id_type=MESH
        )
        return c

    def answer_m(q, c):
        pl.semaphore_signal(
            ready_m.at[me_q],
            inc=1,
            device_id=(group_of(m_at(q), me_z), me_t),
            device_id_type=MESH,
        )
        return c

    def answer_t(i, c):
        @pl.when(order_of(t_peer(i)) < order)
        def _():
            pl.semaphore_signal(ready_t, inc=1, device_id=(me_g, t_peer(i)), device_id_type=MESH)

        return c

    loads = [
        pltpu.make_async_copy(codes_hbm, codes, load_sem.at[0]),
        pltpu.make_async_copy(hid_hbm, hid.at[me_z], load_sem.at[1]),
        pltpu.make_async_copy(query_hbm, query, load_sem.at[2]),
        pltpu.make_async_copy(cache_hbm, cache, load_sem.at[3]),
        pltpu.make_async_copy(base_hbm, base, load_sem.at[4]),
        pltpu.make_async_copy(owner_hbm, owner_ref, load_sem.at[5]),
        pltpu.make_async_copy(lengths_hbm, lengths_ref, load_sem.at[6]),
    ]
    loads[0].start()
    loads[1].start()
    lax.fori_loop(me_q + 1, 4, greet_m, 0)
    lax.fori_loop(me_z + 1, NZ, greet_z, 0)

    @pl.when(jnp.logical_not(at_last_y))
    def _():
        pl.semaphore_signal(
            barrier, inc=1, device_id=(me_g, 2 * last_y + me_x), device_id_type=MESH
        )

    @pl.when(herald)
    def _():
        pl.semaphore_signal(
            barrier, inc=1, device_id=(me_g, 2 * last_y + 1), device_id_type=MESH
        )

    for load in loads[2:]:
        load.start()

    @pl.when(greeted > 0)
    def _():
        pl.semaphore_wait(barrier, greeted)

    lax.fori_loop(0, me_q, answer_m, 0)
    lax.fori_loop(0, me_z, answer_z, 0)

    @pl.when(at_last_y & (me_x == 1))
    def _():
        pl.semaphore_signal(ready_x, inc=1, device_id=(me_g, 2 * last_y), device_id_type=MESH)

    unit = (
        lax.broadcasted_iota(jnp.int32, (64, 64), 0) == lax.broadcasted_iota(jnp.int32, (64, 64), 1)
    ).astype(BF16)
    scale_cols = nt_dot(unit, scales_ref[...])
    loads[0].wait()
    weight[me_m] = jnp.concatenate(
        [
            codes[:, j * 128 : (j + 1) * 128].astype(F32) * scale_cols[:, j : j + 1]
            for j in range(width // 128)
        ],
        axis=1,
    ).astype(BF16)
    loads[1].wait()

    def hid_copy(z):
        return pltpu.make_async_remote_copy(
            src_ref=hid.at[me_z],
            dst_ref=hid.at[me_z],
            send_sem=hid_send_sem.at[z],
            recv_sem=hid_sem.at[me_z],
            device_id=(group_of(me_m, z), me_t),
            device_id_type=MESH,
        )

    def wait_hid(z):
        pltpu.make_async_remote_copy(
            src_ref=hid.at[z],
            dst_ref=hid.at[z],
            send_sem=hid_send_sem.at[z],
            recv_sem=hid_sem.at[z],
            device_id=(group_of(me_m, z), me_t),
            device_id_type=MESH,
        ).wait_recv()

    def weight_copy(q):
        return pltpu.make_async_remote_copy(
            src_ref=weight.at[me_m],
            dst_ref=weight.at[me_m],
            send_sem=weight_send_sem.at[q],
            recv_sem=weight_sem.at[me_m],
            device_id=(group_of(m_at(q), me_z), me_t),
            device_id_type=MESH,
        )

    def start_weight(q):
        @pl.when(q > me_q)
        def _():
            pl.semaphore_wait(ready_m.at[q], 1)

        weight_copy(q).start()

    def wait_weight(i, c):
        q = lax.rem(me_q + i, 4)
        m = m_at(q)
        pltpu.make_async_remote_copy(
            src_ref=weight.at[m],
            dst_ref=weight.at[m],
            send_sem=weight_send_sem.at[q],
            recv_sem=weight_sem.at[m],
            device_id=(group_of(m, me_z), me_t),
            device_id_type=MESH,
        ).wait_recv()
        return c

    def start_hid_earlier(n, c):
        @pl.when(near_peer(n) < me_z)
        def _():
            hid_copy(near_peer(n)).start()

        return c

    middle = NZ // 4
    far = 2 * middle
    relays = (me_z >= middle) & (me_z + middle < NZ) & (middle > 0)

    def straight(z):
        return (z != me_z + far) | (middle == 0)

    def start_hid_later(z, c):
        @pl.when(straight(z))
        def _():
            pl.semaphore_wait(ready_z.at[z], 1)
            hid_copy(z).start()

        return c

    relay_step = jnp.where(me_z < far, max(KVH // 2 - 2, middle - 1), KVH // 2 - 1)

    def relay_copy():
        z = jnp.maximum(me_z - middle, 0)
        return pltpu.make_async_remote_copy(
            src_ref=hid.at[z],
            dst_ref=hid.at[z],
            send_sem=relay_send_sem.at[0],
            recv_sem=hid_sem.at[z],
            device_id=(group_of(me_m, lax.rem(me_z + middle, NZ)), me_t),
            device_id_type=MESH,
        )

    def relay():
        wait_hid(me_z - middle)
        relay_copy().start()

    start_weight(lax.rem(me_q + 2, 4))
    start_weight(3 - me_q)
    start_weight(me_q + 1 - 2 * lax.rem(me_q, 2))

    lax.fori_loop(0, NZ - 1, start_hid_earlier, 0)

    def back_copy(z):
        return pltpu.make_async_remote_copy(
            src_ref=back_send.at[z],
            dst_ref=back.at[pl.ds(me_z * 2, 2)],
            send_sem=back_send_sem.at[z],
            recv_sem=back_sem.at[me_z],
            device_id=(group_of(me_m, z), me_t),
            device_id_type=MESH,
        )

    def products(z):
        product = nt_dot(hid[z], weight[...].reshape(4 * 64, width))
        low = lax.broadcasted_iota(jnp.int32, (8, 128), 1) < 64
        for j in range(2):
            first = product[0:8, j * 128 : (j + 1) * 128]
            second = product[8:16, j * 128 : (j + 1) * 128]
            even = jnp.where(low, first, pltpu.roll(second, 64, 1))
            odd = jnp.where(low, pltpu.roll(first, 64, 1), second)
            back_send[z, j] = jnp.concatenate([even, odd], axis=0).astype(BF16)

    def serve(z):
        @pl.when(jnp.logical_not(relays & (z == me_z - middle)))
        def _():
            wait_hid(z)

        products(z)
        back_copy(z).start()

    def serve_peer(n):
        return lax.rem(me_z + 1 + n, NZ)

    def serve_earlier(n, c):
        @pl.when(serve_peer(n) < me_z)
        def _():
            serve(serve_peer(n))

        return c

    def serve_later(n, c):
        z = serve_peer(n)

        @pl.when((z > me_z) & (z < NZ - 1))
        def _():
            serve(z)

        return c

    last = me_z == NZ - 1

    between = KVH // 2 - 1

    def find(b):
        spot = jnp.int32(0)
        for g in range(NG):
            at = (((g // 2) % NZ) * 2 + g // (2 * NZ)) * 2 + g % 2
            spot = jnp.where(owner_ref[g] == b, jnp.int32(at), spot)
        place[b] = lax.div(spot, jnp.int32(2))
        odd_place[b] = lax.rem(spot, jnp.int32(2))

    lane = lax.broadcasted_iota(jnp.int32, (32, 128), 1)
    position = me_t * POS + lax.broadcasted_iota(jnp.int32, (64, POS), 1)
    own_rows = hid[me_z]
    for load in loads[2:]:
        load.wait()

    def cached(i, columns):
        for n in range(2):
            k = 2 * i + n
            q_both = query[:, pl.ds(pl.multiple_of(k * 1024, 1024), 1024)].astype(F32)
            for r in range(2):
                q = jnp.concatenate(
                    [q_both[r * 8 : (r + 1) * 8, h * HD : (h + 1) * HD] for h in range(8)], axis=0
                ).astype(BF16)
                keys = cache[r * POS : (r + 1) * POS, pl.ds(pl.multiple_of(k * HD, HD), HD)]
                values = cache[
                    r * POS : (r + 1) * POS, pl.ds(pl.multiple_of(KVW + k * HD, HD), HD)
                ]
                scores = jnp.where(position < lengths_ref[r], nt_dot(q, keys) * scale, NEGATIVE)
                peak = jnp.max(scores, axis=1, keepdims=True)
                weights = jnp.exp2(scores - peak)
                total = jnp.sum(weights, axis=1, keepdims=True)
                weighted = jnp.dot(weights.astype(BF16), values, preferred_element_type=F32)
                mean = (weighted * (1.0 / total)).astype(BF16)
                some = me_t * POS < lengths_ref[r]
                log_sum = jnp.where(some, peak + jnp.log2(total), NEGATIVE)
                for half in range(2):
                    dest = 2 * k + half
                    part_send[dest, r * 32 : (r + 1) * 32] = mean[half * 32 : (half + 1) * 32]
                    columns = jnp.where(
                        lane == dest * 8 + r, log_sum[half * 32 : (half + 1) * 32], columns
                    )
            rows = base[pl.ds(pl.multiple_of(k * 256, 256), 256), :]
            tile = nt_dot(own_rows, rows)
            base_proj[2 * k] = tile[:, :128]
            base_proj[2 * k + 1] = tile[:, 128:]
            for m in range(NG // KVH):
                find(k * (NG // KVH) + m)

        @pl.when(me_z + 1 + i < jnp.minimum(NZ - 1, me_z + KVH // 2))
        def _():
            start_hid_later(me_z + 1 + i, 0)

        @pl.when(relays & (i == relay_step) & (me_z + middle < NZ - 1))
        def _():
            relay()

        @pl.when(last & (i == 1))
        def _():
            lax.fori_loop(1, 4, wait_weight, 0)

        @pl.when(last & (i >= 1))
        def _():
            serve(i - 1)

        return columns

    def tell(i, c):
        pl.semaphore_signal(ready_t, inc=1, device_id=(me_g, t_peer(i)), device_id_type=MESH)
        return c

    @pl.when(herald)
    def _():
        pl.semaphore_wait(ready_x, 1)
        lax.fori_loop(1, NT, tell, 0)

    lse_cols[...] = jnp.zeros_like(lse_cols)
    lse_cols[0:32] = lax.fori_loop(0, KVH // 2, cached, jnp.zeros((32, 128), F32))

    def part_copy(i):
        dest = t_peer(i)
        return pltpu.make_async_remote_copy(
            src_ref=part_send.at[dest],
            dst_ref=part.at[me_t],
            send_sem=part_send_sem.at[i],
            recv_sem=part_sem.at[me_t],
            device_id=(me_g, dest),
            device_id_type=MESH,
        )

    def start_part(i, c):
        part_copy(i).start()
        return c

    def start_parts():
        logs = lse_cols[...].T[: NT * 8].reshape(NT, 8, 128)
        sub = lax.broadcasted_iota(jnp.int32, (NT, 8, 128), 1)
        high = logs.astype(BF16).astype(F32)
        rest = logs - high
        middle = rest.astype(BF16).astype(F32)
        low = rest - middle
        middle = jnp.concatenate([middle[:, 0:2], middle[:, 0:2], middle[:, 0:4]], axis=1)
        low = jnp.concatenate([low[:, 0:4], low[:, 0:2], low[:, 0:2]], axis=1)
        rows = jnp.where(sub < 2, high, jnp.where(sub < 4, middle, low))
        part_send[:, 64:80] = jnp.concatenate([rows, rows], axis=1).astype(BF16)

        @pl.when(jnp.logical_not(herald))
        def _():
            pl.semaphore_wait(ready_t, 1)

        lax.fori_loop(1, NT, start_part, 0)
        part[me_t] = part_send[me_t]

    parts_first = (me_z < NZ // 2) & (jnp.abs(me_y - last_y) < 2)

    @pl.when(parts_first)
    def _():
        start_parts()

    lax.fori_loop(me_z + KVH // 2, NZ - 1, start_hid_later, 0)

    @pl.when((me_z >= NZ // 2) & (me_z < NZ - 1))
    def _():
        start_hid_later(NZ - 1, 0)

    @pl.when(relays & (me_z + middle == NZ - 1))
    def _():
        relay()

    @pl.when(jnp.logical_not(last) | (between == 0))
    def _():
        lax.fori_loop(1, 4, wait_weight, 0)

    @pl.when(last)
    def _():
        serve(between)
        start_parts()

    lax.fori_loop(jnp.where(last, between + 1, 0), NZ - 1, serve_earlier, 0)

    @pl.when((me_z >= NZ // 2) & jnp.logical_not(last))
    def _():
        start_parts()

    @pl.when(me_z < NZ // 2)
    def _():
        start_hid_later(NZ - 1, 0)

    @pl.when((me_z < NZ // 2) & jnp.logical_not(parts_first))
    def _():
        start_parts()

    lax.fori_loop(0, NZ - 1, serve_later, 0)

    @pl.when(me_z < NZ - 1)
    def _():
        serve(NZ - 1)

    products(me_z)
    back[pl.ds(me_z * 2, 2)] = back_send[me_z]

    def wait_back(n, c):
        z = near_peer(n)
        pltpu.make_async_remote_copy(
            src_ref=back_send.at[z],
            dst_ref=back.at[pl.ds(z * 2, 2)],
            send_sem=back_send_sem.at[z],
            recv_sem=back_sem.at[z],
            device_id=(group_of(me_m, z), me_t),
            device_id_type=MESH,
        ).wait_recv()
        return c

    lax.fori_loop(0, NZ - 1, wait_back, 0)

    low8 = lax.broadcasted_iota(jnp.int32, (8, 128), 1) < 64

    def returned(block):
        both = back[place[block]].astype(F32)
        return jnp.where(odd_place[block] == 0, both[0:8], both[8:16])

    def whole(block):
        a = returned(2 * block)
        b = returned(2 * block + 1)
        first = jnp.where(low8, a, pltpu.roll(b, 64, 1))
        second = jnp.where(low8, pltpu.roll(a, 64, 1), b)
        return base_proj[block] + jnp.concatenate([first, second], axis=0)

    def proj_copy(dest):
        return pltpu.make_async_remote_copy(
            src_ref=proj_send.at[dest],
            dst_ref=proj.at[me_t],
            send_sem=proj_send_sem.at[dest],
            recv_sem=proj_sem.at[me_t],
            device_id=(me_g, dest),
            device_id_type=MESH,
        )

    def far_y(n):
        step = (n + 1) // 2
        return lax.rem(me_y + NY // 2 + jnp.where(lax.rem(n, 2) == 0, step, NY - step), NY)

    def start_proj(n, c):
        y = far_y(n)
        key = whole(y)
        value = whole(KVH + y).astype(BF16)
        key_high = key.astype(BF16)
        key_low = (key - key_high.astype(F32)).astype(BF16)
        for x in range(2):
            dest = 2 * y + x
            proj_send[dest, 0:16] = key_high
            proj_send[dest, 16:32] = key_low
            proj_send[dest, 32:48] = value
            proj_send[dest, 48:64] = whole(dest).astype(BF16)
        proj_copy(2 * y + 1 - me_x).start()

        @pl.when(y != me_y)
        def _():
            proj_copy(2 * y + me_x).start()

        return c

    lax.fori_loop(0, NY, start_proj, 0)
    proj[me_t] = proj_send[me_t]

    def wait_part(i, c):
        u = t_peer(i)
        pltpu.make_async_remote_copy(
            src_ref=part_send.at[u],
            dst_ref=part.at[u],
            send_sem=part_send_sem.at[i],
            recv_sem=part_sem.at[u],
            device_id=(me_g, u),
            device_id_type=MESH,
        ).wait_recv()
        return c

    lax.fori_loop(1, NT, wait_part, 0)
    logs = part[:, 64:80].astype(F32)[:, 0:8]
    logs = (
        logs
        + jnp.concatenate([logs[:, 2:8], logs[:, 0:2]], axis=1)
        + jnp.concatenate([logs[:, 4:8], logs[:, 0:4]], axis=1)
    )
    top = jnp.max(logs, axis=0)
    grown = jnp.exp2(logs - top[None])
    sub = lax.broadcasted_iota(jnp.int32, (8, 128), 0)
    top_down = jnp.concatenate([top[0:2], top[0:2], top[0:4]], axis=0)
    with_top = jnp.where(sub < 2, grown[0], top_down)
    factors = jnp.concatenate([with_top[None], grown[1:]], axis=0).reshape(NT * 8, 128)
    if NT * 8 < 128:
        factors = jnp.concatenate([factors, jnp.zeros((128 - NT * 8, 128), F32)], axis=0)
    factors = factors.T[0:32]
    sums, totals, peaks = [], [], []
    for r in range(2):
        acc = jnp.zeros((32, HD), F32)
        total = jnp.zeros((32, 1), F32)
        for u in range(NT):
            factor = factors[:, u * 8 + r : u * 8 + r + 1]
            acc = acc + factor * part[u, r * 32 : (r + 1) * 32].astype(F32)
            total = total + factor
        sums.append(acc)
        totals.append(total)
        peaks.append(factors[:, 2 + r : 3 + r])
    cached_ref[:, 0:HD] = jnp.concatenate(sums, axis=0)
    half_lane = lax.broadcasted_iota(jnp.int32, (64, 128), 1) < 64
    cached_ref[:, HD : 2 * HD] = jnp.where(
        half_lane, jnp.concatenate(totals, axis=0), jnp.concatenate(peaks, axis=0)
    )
    q_both = query[:, pl.ds(pl.multiple_of(me_t * 512, 512), 512)].astype(F32)
    own_ref[...] = jnp.concatenate(
        [
            q_both[r * 8 : (r + 1) * 8, h * HD : (h + 1) * HD]
            for r in range(2)
            for h in range(4)
        ],
        axis=0,
    ).astype(BF16)

    def sent_z(n, c):
        z = near_peer(n)

        @pl.when(straight(z))
        def _():
            hid_copy(z).wait_send()

        @pl.when(jnp.logical_not(straight(z)))
        def _():
            pl.semaphore_wait(ready_z.at[z], 1)

        back_copy(z).wait_send()
        return c

    def sent_m(i, c):
        weight_copy(lax.rem(me_q + i, 4)).wait_send()
        return c

    def sent_t(i, c):
        part_copy(i).wait_send()
        proj_copy(t_peer(i)).wait_send()
        return c

    lax.fori_loop(0, NZ - 1, sent_z, 0)

    @pl.when(relays)
    def _():
        relay_copy().wait_send()

    lax.fori_loop(1, 4, sent_m, 0)
    lax.fori_loop(1, NT, sent_t, 0)

    def wait_proj(i, c):
        u = lax.rem(2 * (last_y + 1) + i, NT)

        @pl.when(u != me_t)
        def _():
            pltpu.make_async_remote_copy(
                src_ref=proj_send.at[u],
                dst_ref=proj.at[u],
                send_sem=proj_send_sem.at[u],
                recv_sem=proj_sem.at[u],
                device_id=(me_g, u),
                device_id_type=MESH,
            ).wait_recv()

        return c

    lax.fori_loop(0, NT, wait_proj, 0)
    summed = jnp.sum(proj[...].astype(F32), axis=0)
    fresh_ref[0] = (summed[0:16] + summed[16:32]).astype(BF16)
    fresh_ref[1] = summed[32:48].astype(BF16)
    fresh_ref[2] = summed[48:64].astype(BF16)


def finish(fresh_ref, cached_ref, own_ref, new_ref, att_ref):
    scale = HD ** (-0.5) * LOG2_E
    new_ref[...] = fresh_ref[2]
    cache_sum = cached_ref[:, 0:HD]
    cache_total = cached_ref[:, HD : HD + 1]
    cache_peak = cached_ref[:, HD + 64 : HD + 65]
    near = nt_dot(own_ref[...], fresh_ref[0]) * scale
    at = lax.broadcasted_iota(jnp.int32, (64, 16), 0)
    to = lax.broadcasted_iota(jnp.int32, (64, 16), 1)
    causal = (at // 32 == to // 8) & (lax.rem(at, 8) >= lax.rem(to, 8))
    near = jnp.where(causal, near, NEGATIVE)
    near_peak = jnp.max(near, axis=1, keepdims=True)
    near_weights = jnp.exp2(near - near_peak)
    near_total = jnp.sum(near_weights, axis=1, keepdims=True)
    near_sum = jnp.dot(near_weights.astype(BF16), fresh_ref[1], preferred_element_type=F32)
    joined = jnp.maximum(cache_peak, near_peak)
    cache_scale = jnp.exp2(cache_peak - joined)
    near_scale = jnp.exp2(near_peak - joined)
    numerator = cache_sum * cache_scale + near_sum * near_scale
    denominator = cache_total * cache_scale + near_total * near_scale
    result = numerator / denominator
    att_ref[...] = jnp.concatenate(
        [
            jnp.concatenate(
                [result[r * 32 + h * 8 : r * 32 + h * 8 + 8] for h in range(4)], axis=1
            )
            for r in range(2)
        ],
        axis=0,
    ).astype(BF16)


def on_device(
    hidden_x, base_weight, delta_codes, delta_scales, owner_map, kv_cache, queries, lengths
):
    NG = lax.axis_size("group")
    NT = lax.axis_size("tensor")
    NZ = NG // 4
    rows, steps, width = hidden_x.shape
    tokens = rows * steps
    positions = kv_cache.shape[1]
    any_space = pl.BlockSpec(memory_space=pl.ANY)
    vmem = pl.BlockSpec(memory_space=pltpu.VMEM)
    dma = pltpu.SemaphoreType.DMA

    def in_hbm(x):
        return pltpu.with_memory_space_constraint(x, pltpu.HBM)

    fresh, cached, own_query = pl.pallas_call(
        functools.partial(kernel, NG, NT),
        out_shape=(
            pltpu.VMEM((3, tokens, 128), BF16),
            pltpu.VMEM((64, 256), F32),
            pltpu.VMEM((64, 128), BF16),
        ),
        in_specs=[any_space] * 3 + [vmem] + [any_space] * 4,
        out_specs=(vmem, vmem, vmem),
        scratch_shapes=[
            pltpu.VMEM((NZ, tokens, width), BF16),
            pltpu.VMEM(base_weight.shape, BF16),
            pltpu.VMEM(delta_codes.shape, BF16),
            pltpu.SMEM(owner_map.shape, jnp.int32),
            pltpu.SMEM(lengths.shape, jnp.int32),
            pltpu.VMEM((rows * positions, kv_cache.shape[2]), BF16),
            pltpu.VMEM((tokens, queries.shape[2]), BF16),
            pltpu.VMEM((4, 64, width), BF16),
            pltpu.SMEM((NG,), jnp.int32),
            pltpu.SMEM((NG,), jnp.int32),
            pltpu.VMEM((NZ, 2, 16, 128), BF16),
            pltpu.VMEM((NZ * 2, 16, 128), BF16),
            pltpu.VMEM((NT, tokens, 128), F32),
            pltpu.VMEM((NT, 4 * tokens, 128), BF16),
            pltpu.VMEM((NT, 4 * tokens, 128), BF16),
            pltpu.VMEM((NT, 80, HD), BF16),
            pltpu.VMEM((NT, 80, HD), BF16),
            pltpu.VMEM((128, 128), F32),
            dma((7,)),
            dma((NZ,)),
            dma((NZ,)),
            dma((1,)),
            dma((4,)),
            dma((4,)),
            dma((NZ,)),
            dma((NZ,)),
            dma((NT,)),
            dma((NT,)),
            dma((NT,)),
            dma((NT,)),
            pltpu.SemaphoreType.REGULAR((NZ,)),
            pltpu.SemaphoreType.REGULAR,
            pltpu.SemaphoreType.REGULAR,
            pltpu.SemaphoreType.REGULAR((4,)),
        ],
        compiler_params=pltpu.CompilerParams(
            collective_id=0, has_side_effects=True, vmem_limit_bytes=48 * 1024 * 1024
        ),
    )(
        in_hbm(hidden_x.reshape(tokens, width)),
        in_hbm(base_weight),
        in_hbm(delta_codes),
        in_hbm(delta_scales.T),
        in_hbm(owner_map),
        in_hbm(kv_cache.reshape(rows * positions, kv_cache.shape[2])),
        in_hbm(queries.reshape(tokens, queries.shape[2])),
        in_hbm(lengths),
    )
    new_kv, attended = pl.pallas_call(
        finish,
        out_shape=(
            jax.ShapeDtypeStruct((tokens, 128), BF16),
            jax.ShapeDtypeStruct((tokens, 512), BF16),
        ),
        in_specs=[vmem, vmem, vmem],
        out_specs=(vmem, vmem),
        compiler_params=pltpu.CompilerParams(vmem_limit_bytes=8 * 1024 * 1024),
    )(fresh, cached, own_query)
    return new_kv.reshape(rows, steps, 128), attended.reshape(rows, steps, 512)


def solution(mesh):
    in_specs = (
        P("group", None, "tensor"),
        P(None, "tensor"),
        P("group", "tensor"),
        P("group", "tensor"),
        P(),
        P("group", "tensor", None),
        P("group", None, None),
        P("group"),
    )
    out_specs = (P("group", None, "tensor"), P("group", None, "tensor"))
    return jax.shard_map(
        on_device, mesh=mesh, in_specs=in_specs, out_specs=out_specs, check_vma=False
    )
```

```python
import functools

import jax
import jax.numpy as jnp
from jax import lax
from jax.experimental import pallas as pl
from jax.experimental.pallas import tpu as pltpu
from jax.sharding import PartitionSpec as P

HD = 128
NEGATIVE = -1e30
LOG2_E = 1.4426950408889634
MESH = pl.DeviceIdType.MESH
F32 = jnp.float32
BF16 = jnp.bfloat16


def nt_dot(a, b):
    return lax.dot_general(a, b, (((1,), (1,)), ((), ())), preferred_element_type=F32)


def kernel(
    NG,
    NT,
    hid_hbm,
    base_hbm,
    codes_hbm,
    scales_hbm,
    owner_hbm,
    cache_hbm,
    query_hbm,
    lengths_hbm,
    fresh_ref,
    cached_ref,
    own_ref,
    hid,
    base,
    codes,
    scales_ref,
    owner_ref,
    lengths_ref,
    cache,
    query,
    weight,
    place,
    odd_place,
    back_send,
    back,
    base_proj,
    proj_send,
    proj,
    part_send,
    part,
    lse_cols,
    load_sem,
    hid_send_sem,
    hid_sem,
    relay_send_sem,
    weight_send_sem,
    weight_sem,
    back_send_sem,
    back_sem,
    proj_send_sem,
    proj_sem,
    part_send_sem,
    part_sem,
    ready_z,
    ready_t,
    ready_x,
    ready_m,
):
    NZ = NG // 4
    NY = NT // 2
    KVH = NT // 2
    POS = cache.shape[0] // 2
    KVW = KVH * HD
    width = hid.shape[2]
    scale = HD ** (-0.5) * LOG2_E
    me_g = lax.axis_index("group")
    me_t = lax.axis_index("tensor")
    core = lax.rem(me_g, 2)
    me_z = lax.rem(me_g // 2, NZ)
    me_m = me_g // (2 * NZ) * 2 + core
    me_y = me_t // 2
    me_x = lax.rem(me_t, 2)

    def group_of(m, z):
        return (m // 2) * (2 * NZ) + z * 2 + lax.rem(m, 2)

    def near_peer(n):
        step = n // 2 + 1
        return lax.rem(me_z + jnp.where(lax.rem(n, 2) == 0, step, NZ - step), NZ)

    def t_peer(i):
        return lax.rem(me_t + i, NT)

    me_q = me_m + 1 - 2 * core

    def m_at(q):
        return q + 1 - 2 * lax.rem(q, 2)

    last_y = NY // 2
    at_last_y = me_y == last_y
    herald = at_last_y & (me_x == 0)
    greeted = me_z + me_q + jnp.where(at_last_y, NY - 1 + me_x, 0)
    barrier = pltpu.get_barrier_semaphore()

    def greet_m(q, c):
        pl.semaphore_signal(
            barrier, inc=1, device_id=(group_of(m_at(q), me_z), me_t), device_id_type=MESH
        )
        return c

    def greet_z(z, c):
        pl.semaphore_signal(
            barrier, inc=1, device_id=(group_of(me_m, z), me_t), device_id_type=MESH
        )
        return c

    def answer_z(z, c):
        pl.semaphore_signal(
            ready_z.at[me_z], inc=1, device_id=(group_of(me_m, z), me_t), device_id_type=MESH
        )
        return c

    def answer_m(q, c):
        pl.semaphore_signal(
            ready_m.at[me_q],
            inc=1,
            device_id=(group_of(m_at(q), me_z), me_t),
            device_id_type=MESH,
        )
        return c

    def answer_t(i, c):
        @pl.when(order_of(t_peer(i)) < order)
        def _():
            pl.semaphore_signal(ready_t, inc=1, device_id=(me_g, t_peer(i)), device_id_type=MESH)

        return c

    loads = [
        pltpu.make_async_copy(codes_hbm, codes, load_sem.at[0]),
        pltpu.make_async_copy(hid_hbm, hid.at[me_z], load_sem.at[1]),
        pltpu.make_async_copy(query_hbm, query, load_sem.at[2]),
        pltpu.make_async_copy(cache_hbm, cache, load_sem.at[3]),
        pltpu.make_async_copy(base_hbm, base, load_sem.at[4]),
        pltpu.make_async_copy(scales_hbm, scales_ref, load_sem.at[5]),
        pltpu.make_async_copy(owner_hbm, owner_ref, load_sem.at[6]),
        pltpu.make_async_copy(lengths_hbm, lengths_ref, load_sem.at[7]),
    ]
    loads[5].start()
    loads[0].start()
    loads[1].start()
    lax.fori_loop(me_q + 1, 4, greet_m, 0)
    lax.fori_loop(me_z + 1, NZ, greet_z, 0)

    @pl.when(jnp.logical_not(at_last_y))
    def _():
        pl.semaphore_signal(
            barrier, inc=1, device_id=(me_g, 2 * last_y + me_x), device_id_type=MESH
        )

    @pl.when(herald)
    def _():
        pl.semaphore_signal(
            barrier, inc=1, device_id=(me_g, 2 * last_y + 1), device_id_type=MESH
        )

    for load in loads[2:5] + loads[6:]:
        load.start()

    @pl.when(greeted > 0)
    def _():
        pl.semaphore_wait(barrier, greeted)

    lax.fori_loop(0, me_z, answer_z, 0)
    lax.fori_loop(0, me_q, answer_m, 0)

    @pl.when(at_last_y & (me_x == 1))
    def _():
        pl.semaphore_signal(ready_x, inc=1, device_id=(me_g, 2 * last_y), device_id_type=MESH)

    unit = (
        lax.broadcasted_iota(jnp.int32, (64, 64), 0) == lax.broadcasted_iota(jnp.int32, (64, 64), 1)
    ).astype(BF16)
    loads[5].wait()
    scale_cols = nt_dot(unit, scales_ref[...])
    loads[0].wait()
    weight[me_m] = jnp.concatenate(
        [
            codes[:, j * 128 : (j + 1) * 128].astype(F32) * scale_cols[:, j : j + 1]
            for j in range(width // 128)
        ],
        axis=1,
    ).astype(BF16)
    loads[1].wait()

    def hid_copy(z):
        return pltpu.make_async_remote_copy(
            src_ref=hid.at[me_z],
            dst_ref=hid.at[me_z],
            send_sem=hid_send_sem.at[z],
            recv_sem=hid_sem.at[me_z],
            device_id=(group_of(me_m, z), me_t),
            device_id_type=MESH,
        )

    def wait_hid(z):
        pltpu.make_async_remote_copy(
            src_ref=hid.at[z],
            dst_ref=hid.at[z],
            send_sem=hid_send_sem.at[z],
            recv_sem=hid_sem.at[z],
            device_id=(group_of(me_m, z), me_t),
            device_id_type=MESH,
        ).wait_recv()

    def weight_copy(q):
        return pltpu.make_async_remote_copy(
            src_ref=weight.at[me_m],
            dst_ref=weight.at[me_m],
            send_sem=weight_send_sem.at[q],
            recv_sem=weight_sem.at[me_m],
            device_id=(group_of(m_at(q), me_z), me_t),
            device_id_type=MESH,
        )

    def start_weight(q):
        @pl.when(q > me_q)
        def _():
            pl.semaphore_wait(ready_m.at[q], 1)

        weight_copy(q).start()

    def wait_weight(i, c):
        q = lax.rem(me_q + i, 4)
        m = m_at(q)
        pltpu.make_async_remote_copy(
            src_ref=weight.at[m],
            dst_ref=weight.at[m],
            send_sem=weight_send_sem.at[q],
            recv_sem=weight_sem.at[m],
            device_id=(group_of(m, me_z), me_t),
            device_id_type=MESH,
        ).wait_recv()
        return c

    def start_hid_earlier(n, c):
        @pl.when(near_peer(n) < me_z)
        def _():
            hid_copy(near_peer(n)).start()

        return c

    middle = NZ // 4
    far = 2 * middle
    relays = (me_z >= middle) & (me_z + middle < NZ) & (middle > 0)

    def straight(z):
        return (z != me_z + far) | (middle == 0)

    def start_hid_later(z, c):
        @pl.when(straight(z))
        def _():
            pl.semaphore_wait(ready_z.at[z], 1)
            hid_copy(z).start()

        return c

    relay_step = jnp.where(me_z == middle, middle - 1, jnp.where(me_z < far, max(KVH // 2 - 2, middle - 1), KVH // 2 - 1))

    def relay_copy():
        z = jnp.maximum(me_z - middle, 0)
        return pltpu.make_async_remote_copy(
            src_ref=hid.at[z],
            dst_ref=hid.at[z],
            send_sem=relay_send_sem.at[0],
            recv_sem=hid_sem.at[z],
            device_id=(group_of(me_m, lax.rem(me_z + middle, NZ)), me_t),
            device_id_type=MESH,
        )

    def relay():
        wait_hid(me_z - middle)
        relay_copy().start()

    start_weight(lax.rem(me_q + 2, 4))
    start_weight(3 - me_q)
    start_weight(me_q + 1 - 2 * lax.rem(me_q, 2))

    lax.fori_loop(0, NZ - 1, start_hid_earlier, 0)

    def back_copy(z):
        return pltpu.make_async_remote_copy(
            src_ref=back_send.at[z],
            dst_ref=back.at[pl.ds(me_z * 2, 2)],
            send_sem=back_send_sem.at[z],
            recv_sem=back_sem.at[me_z],
            device_id=(group_of(me_m, z), me_t),
            device_id_type=MESH,
        )

    def products(z):
        product = nt_dot(hid[z], weight[...].reshape(4 * 64, width))
        low = lax.broadcasted_iota(jnp.int32, (8, 128), 1) < 64
        for j in range(2):
            first = product[0:8, j * 128 : (j + 1) * 128]
            second = product[8:16, j * 128 : (j + 1) * 128]
            even = jnp.where(low, first, pltpu.roll(second, 64, 1))
            odd = jnp.where(low, pltpu.roll(first, 64, 1), second)
            back_send[z, j] = jnp.concatenate([even, odd], axis=0).astype(BF16)

    def serve(z):
        @pl.when(jnp.logical_not(relays & (z == me_z - middle)))
        def _():
            wait_hid(z)

        products(z)
        back_copy(z).start()

    def serve_peer(n):
        return lax.rem(me_z + 1 + n, NZ)

    def serve_earlier(n, c):
        @pl.when(serve_peer(n) < me_z)
        def _():
            serve(serve_peer(n))

        return c

    def serve_later(n, c):
        z = serve_peer(n)

        @pl.when((z > me_z) & (z < NZ - 1))
        def _():
            serve(z)

        return c

    last = me_z == NZ - 1

    between = KVH // 2 - 1

    def find(b):
        spot = jnp.int32(0)
        for g in range(NG):
            at = (((g // 2) % NZ) * 2 + g // (2 * NZ)) * 2 + g % 2
            spot = jnp.where(owner_ref[g] == b, jnp.int32(at), spot)
        place[b] = lax.div(spot, jnp.int32(2))
        odd_place[b] = lax.rem(spot, jnp.int32(2))

    lane = lax.broadcasted_iota(jnp.int32, (32, 128), 1)
    position = me_t * POS + lax.broadcasted_iota(jnp.int32, (64, POS), 1)
    own_rows = hid[me_z]
    for load in loads[2:5] + loads[6:]:
        load.wait()

    def cached(i, columns):
        for n in range(2):
            k = 2 * i + n
            q_both = query[:, pl.ds(pl.multiple_of(k * 1024, 1024), 1024)].astype(F32)
            for r in range(2):
                q = jnp.concatenate(
                    [q_both[r * 8 : (r + 1) * 8, h * HD : (h + 1) * HD] for h in range(8)], axis=0
                ).astype(BF16)
                keys = cache[r * POS : (r + 1) * POS, pl.ds(pl.multiple_of(k * HD, HD), HD)]
                values = cache[
                    r * POS : (r + 1) * POS, pl.ds(pl.multiple_of(KVW + k * HD, HD), HD)
                ]
                scores = jnp.where(position < lengths_ref[r], nt_dot(q, keys) * scale, NEGATIVE)
                peak = jnp.max(scores, axis=1, keepdims=True)
                weights = jnp.exp2(scores - peak)
                total = jnp.sum(weights, axis=1, keepdims=True)
                weighted = jnp.dot(weights.astype(BF16), values, preferred_element_type=F32)
                mean = (weighted * (1.0 / total)).astype(BF16)
                some = me_t * POS < lengths_ref[r]
                log_sum = jnp.where(some, peak + jnp.log2(total), NEGATIVE)
                for half in range(2):
                    dest = 2 * k + half
                    part_send[dest, r * 32 : (r + 1) * 32] = mean[half * 32 : (half + 1) * 32]
                    columns = jnp.where(
                        lane == dest * 8 + r, log_sum[half * 32 : (half + 1) * 32], columns
                    )
            rows = base[pl.ds(pl.multiple_of(k * 256, 256), 256), :]
            tile = nt_dot(own_rows, rows)
            base_proj[2 * k] = tile[:, :128]
            base_proj[2 * k + 1] = tile[:, 128:]
            for m in range(NG // KVH):
                find(k * (NG // KVH) + m)

        @pl.when(me_z + 1 + i < jnp.minimum(NZ - 1, me_z + KVH // 2))
        def _():
            start_hid_later(me_z + 1 + i, 0)

        @pl.when(relays & (i == relay_step) & (me_z + middle < NZ - 1))
        def _():
            relay()

        @pl.when(last & (i == 1))
        def _():
            lax.fori_loop(1, 4, wait_weight, 0)

        @pl.when(last & (i >= 1))
        def _():
            serve(i - 1)

        return columns

    def tell(i, c):
        pl.semaphore_signal(ready_t, inc=1, device_id=(me_g, t_peer(i)), device_id_type=MESH)
        return c

    @pl.when(herald)
    def _():
        pl.semaphore_wait(ready_x, 1)
        lax.fori_loop(1, NT, tell, 0)

    lse_cols[...] = jnp.zeros_like(lse_cols)
    lse_cols[0:32] = lax.fori_loop(0, KVH // 2, cached, jnp.zeros((32, 128), F32))

    def part_copy(i):
        dest = t_peer(i)
        return pltpu.make_async_remote_copy(
            src_ref=part_send.at[dest],
            dst_ref=part.at[me_t],
            send_sem=part_send_sem.at[i],
            recv_sem=part_sem.at[me_t],
            device_id=(me_g, dest),
            device_id_type=MESH,
        )

    def start_part(i, c):
        part_copy(i).start()
        return c

    def start_parts():
        logs = lse_cols[...].T[: NT * 8].reshape(NT, 8, 128)
        sub = lax.broadcasted_iota(jnp.int32, (NT, 8, 128), 1)
        high = logs.astype(BF16).astype(F32)
        rest = logs - high
        middle = rest.astype(BF16).astype(F32)
        low = rest - middle
        middle = jnp.concatenate([middle[:, 0:2], middle[:, 0:2], middle[:, 0:4]], axis=1)
        low = jnp.concatenate([low[:, 0:4], low[:, 0:2], low[:, 0:2]], axis=1)
        rows = jnp.where(sub < 2, high, jnp.where(sub < 4, middle, low))
        part_send[:, 64:80] = jnp.concatenate([rows, rows], axis=1).astype(BF16)

        @pl.when(jnp.logical_not(herald))
        def _():
            pl.semaphore_wait(ready_t, 1)

        lax.fori_loop(1, NT, start_part, 0)
        part[me_t] = part_send[me_t]

    parts_first = (me_z < NZ // 2) & (jnp.abs(me_y - last_y) < 2)

    @pl.when(parts_first)
    def _():
        start_parts()

    lax.fori_loop(me_z + KVH // 2, NZ - 1, start_hid_later, 0)

    @pl.when((me_z >= NZ // 2) & (me_z < NZ - 1))
    def _():
        start_hid_later(NZ - 1, 0)

    @pl.when(relays & (me_z + middle == NZ - 1))
    def _():
        relay()

    @pl.when(jnp.logical_not(last) | (between == 0))
    def _():
        lax.fori_loop(1, 4, wait_weight, 0)

    @pl.when(last)
    def _():
        serve(between)
        start_parts()

    lax.fori_loop(jnp.where(last, between + 1, 0), NZ - 1, serve_earlier, 0)

    @pl.when((me_z >= NZ // 2) & jnp.logical_not(last))
    def _():
        start_parts()

    @pl.when(me_z < NZ // 2)
    def _():
        start_hid_later(NZ - 1, 0)

    @pl.when((me_z < NZ // 2) & jnp.logical_not(parts_first))
    def _():
        start_parts()

    lax.fori_loop(0, NZ - 1, serve_later, 0)

    @pl.when(me_z < NZ - 1)
    def _():
        serve(NZ - 1)

    products(me_z)
    back[pl.ds(me_z * 2, 2)] = back_send[me_z]

    def wait_back(n, c):
        z = near_peer(n)
        pltpu.make_async_remote_copy(
            src_ref=back_send.at[z],
            dst_ref=back.at[pl.ds(z * 2, 2)],
            send_sem=back_send_sem.at[z],
            recv_sem=back_sem.at[z],
            device_id=(group_of(me_m, z), me_t),
            device_id_type=MESH,
        ).wait_recv()
        return c

    lax.fori_loop(0, NZ - 1, wait_back, 0)

    low8 = lax.broadcasted_iota(jnp.int32, (8, 128), 1) < 64

    def returned(block):
        both = back[place[block]].astype(F32)
        return jnp.where(odd_place[block] == 0, both[0:8], both[8:16])

    def whole(block):
        a = returned(2 * block)
        b = returned(2 * block + 1)
        first = jnp.where(low8, a, pltpu.roll(b, 64, 1))
        second = jnp.where(low8, pltpu.roll(a, 64, 1), b)
        return base_proj[block] + jnp.concatenate([first, second], axis=0)

    def proj_copy(dest):
        return pltpu.make_async_remote_copy(
            src_ref=proj_send.at[dest],
            dst_ref=proj.at[me_t],
            send_sem=proj_send_sem.at[dest],
            recv_sem=proj_sem.at[me_t],
            device_id=(me_g, dest),
            device_id_type=MESH,
        )

    def far_y(n):
        step = (n + 1) // 2
        return lax.rem(me_y + NY // 2 + jnp.where(lax.rem(n, 2) == 0, step, NY - step), NY)

    def start_proj(n, c):
        y = far_y(n)
        key = whole(y)
        value = whole(KVH + y).astype(BF16)
        key_high = key.astype(BF16)
        key_low = (key - key_high.astype(F32)).astype(BF16)
        for x in range(2):
            dest = 2 * y + x
            proj_send[dest, 0:16] = key_high
            proj_send[dest, 16:32] = key_low
            proj_send[dest, 32:48] = value
            proj_send[dest, 48:64] = whole(dest).astype(BF16)
        proj_copy(2 * y + 1 - me_x).start()

        @pl.when(y != me_y)
        def _():
            proj_copy(2 * y + me_x).start()

        return c

    lax.fori_loop(0, NY, start_proj, 0)
    proj[me_t] = proj_send[me_t]

    def wait_part(i, c):
        u = t_peer(i)
        pltpu.make_async_remote_copy(
            src_ref=part_send.at[u],
            dst_ref=part.at[u],
            send_sem=part_send_sem.at[i],
            recv_sem=part_sem.at[u],
            device_id=(me_g, u),
            device_id_type=MESH,
        ).wait_recv()
        return c

    lax.fori_loop(1, NT, wait_part, 0)
    logs = part[:, 64:80].astype(F32)[:, 0:8]
    logs = (
        logs
        + jnp.concatenate([logs[:, 2:8], logs[:, 0:2]], axis=1)
        + jnp.concatenate([logs[:, 4:8], logs[:, 0:4]], axis=1)
    )
    top = jnp.max(logs, axis=0)
    grown = jnp.exp2(logs - top[None])
    sub = lax.broadcasted_iota(jnp.int32, (8, 128), 0)
    top_down = jnp.concatenate([top[0:2], top[0:2], top[0:4]], axis=0)
    with_top = jnp.where(sub < 2, grown[0], top_down)
    factors = jnp.concatenate([with_top[None], grown[1:]], axis=0).reshape(NT * 8, 128)
    if NT * 8 < 128:
        factors = jnp.concatenate([factors, jnp.zeros((128 - NT * 8, 128), F32)], axis=0)
    factors = factors.T[0:32]
    sums, totals, peaks = [], [], []
    for r in range(2):
        acc = jnp.zeros((32, HD), F32)
        total = jnp.zeros((32, 1), F32)
        for u in range(NT):
            factor = factors[:, u * 8 + r : u * 8 + r + 1]
            acc = acc + factor * part[u, r * 32 : (r + 1) * 32].astype(F32)
            total = total + factor
        sums.append(acc)
        totals.append(total)
        peaks.append(factors[:, 2 + r : 3 + r])
    cached_ref[:, 0:HD] = jnp.concatenate(sums, axis=0)
    half_lane = lax.broadcasted_iota(jnp.int32, (64, 128), 1) < 64
    cached_ref[:, HD : 2 * HD] = jnp.where(
        half_lane, jnp.concatenate(totals, axis=0), jnp.concatenate(peaks, axis=0)
    )
    q_both = query[:, pl.ds(pl.multiple_of(me_t * 512, 512), 512)].astype(F32)
    own_ref[...] = jnp.concatenate(
        [
            q_both[r * 8 : (r + 1) * 8, h * HD : (h + 1) * HD]
            for r in range(2)
            for h in range(4)
        ],
        axis=0,
    ).astype(BF16)

    def sent_z(n, c):
        z = near_peer(n)

        @pl.when(straight(z))
        def _():
            hid_copy(z).wait_send()

        @pl.when(jnp.logical_not(straight(z)))
        def _():
            pl.semaphore_wait(ready_z.at[z], 1)

        back_copy(z).wait_send()
        return c

    def sent_m(i, c):
        weight_copy(lax.rem(me_q + i, 4)).wait_send()
        return c

    def sent_t(i, c):
        part_copy(i).wait_send()
        proj_copy(t_peer(i)).wait_send()
        return c

    lax.fori_loop(0, NZ - 1, sent_z, 0)

    @pl.when(relays)
    def _():
        relay_copy().wait_send()

    lax.fori_loop(1, 4, sent_m, 0)
    lax.fori_loop(1, NT, sent_t, 0)

    def wait_proj(i, c):
        u = lax.rem(2 * (last_y + 1) + i, NT)

        @pl.when(u != me_t)
        def _():
            pltpu.make_async_remote_copy(
                src_ref=proj_send.at[u],
                dst_ref=proj.at[u],
                send_sem=proj_send_sem.at[u],
                recv_sem=proj_sem.at[u],
                device_id=(me_g, u),
                device_id_type=MESH,
            ).wait_recv()

        return c

    lax.fori_loop(0, NT, wait_proj, 0)
    summed = jnp.sum(proj[...].astype(F32), axis=0)
    fresh_ref[0] = (summed[0:16] + summed[16:32]).astype(BF16)
    fresh_ref[1] = summed[32:48].astype(BF16)
    fresh_ref[2] = summed[48:64].astype(BF16)


def finish(fresh_ref, cached_ref, own_ref, new_ref, att_ref):
    scale = HD ** (-0.5) * LOG2_E
    new_ref[...] = fresh_ref[2]
    cache_sum = cached_ref[:, 0:HD]
    cache_total = cached_ref[:, HD : HD + 1]
    cache_peak = cached_ref[:, HD + 64 : HD + 65]
    near = nt_dot(own_ref[...], fresh_ref[0]) * scale
    at = lax.broadcasted_iota(jnp.int32, (64, 16), 0)
    to = lax.broadcasted_iota(jnp.int32, (64, 16), 1)
    causal = (at // 32 == to // 8) & (lax.rem(at, 8) >= lax.rem(to, 8))
    near = jnp.where(causal, near, NEGATIVE)
    near_peak = jnp.max(near, axis=1, keepdims=True)
    near_weights = jnp.exp2(near - near_peak)
    near_total = jnp.sum(near_weights, axis=1, keepdims=True)
    near_sum = jnp.dot(near_weights.astype(BF16), fresh_ref[1], preferred_element_type=F32)
    joined = jnp.maximum(cache_peak, near_peak)
    cache_scale = jnp.exp2(cache_peak - joined)
    near_scale = jnp.exp2(near_peak - joined)
    numerator = cache_sum * cache_scale + near_sum * near_scale
    denominator = cache_total * cache_scale + near_total * near_scale
    result = numerator / denominator
    att_ref[...] = jnp.concatenate(
        [
            jnp.concatenate(
                [result[r * 32 + h * 8 : r * 32 + h * 8 + 8] for h in range(4)], axis=1
            )
            for r in range(2)
        ],
        axis=0,
    ).astype(BF16)


def on_device(
    hidden_x, base_weight, delta_codes, delta_scales, owner_map, kv_cache, queries, lengths
):
    NG = lax.axis_size("group")
    NT = lax.axis_size("tensor")
    NZ = NG // 4
    rows, steps, width = hidden_x.shape
    tokens = rows * steps
    positions = kv_cache.shape[1]
    any_space = pl.BlockSpec(memory_space=pl.ANY)
    vmem = pl.BlockSpec(memory_space=pltpu.VMEM)
    dma = pltpu.SemaphoreType.DMA

    def in_hbm(x):
        return pltpu.with_memory_space_constraint(x, pltpu.HBM)

    fresh, cached, own_query = pl.pallas_call(
        functools.partial(kernel, NG, NT),
        out_shape=(
            pltpu.VMEM((3, tokens, 128), BF16),
            pltpu.VMEM((64, 256), F32),
            pltpu.VMEM((64, 128), BF16),
        ),
        in_specs=[any_space] * 8,
        out_specs=(vmem, vmem, vmem),
        scratch_shapes=[
            pltpu.VMEM((NZ, tokens, width), BF16),
            pltpu.VMEM(base_weight.shape, BF16),
            pltpu.VMEM(delta_codes.shape, BF16),
            pltpu.VMEM(delta_scales.shape[::-1], BF16),
            pltpu.SMEM(owner_map.shape, jnp.int32),
            pltpu.SMEM(lengths.shape, jnp.int32),
            pltpu.VMEM((rows * positions, kv_cache.shape[2]), BF16),
            pltpu.VMEM((tokens, queries.shape[2]), BF16),
            pltpu.VMEM((4, 64, width), BF16),
            pltpu.SMEM((NG,), jnp.int32),
            pltpu.SMEM((NG,), jnp.int32),
            pltpu.VMEM((NZ, 2, 16, 128), BF16),
            pltpu.VMEM((NZ * 2, 16, 128), BF16),
            pltpu.VMEM((NT, tokens, 128), F32),
            pltpu.VMEM((NT, 4 * tokens, 128), BF16),
            pltpu.VMEM((NT, 4 * tokens, 128), BF16),
            pltpu.VMEM((NT, 80, HD), BF16),
            pltpu.VMEM((NT, 80, HD), BF16),
            pltpu.VMEM((128, 128), F32),
            dma((8,)),
            dma((NZ,)),
            dma((NZ,)),
            dma((1,)),
            dma((4,)),
            dma((4,)),
            dma((NZ,)),
            dma((NZ,)),
            dma((NT,)),
            dma((NT,)),
            dma((NT,)),
            dma((NT,)),
            pltpu.SemaphoreType.REGULAR((NZ,)),
            pltpu.SemaphoreType.REGULAR,
            pltpu.SemaphoreType.REGULAR,
            pltpu.SemaphoreType.REGULAR((4,)),
        ],
        compiler_params=pltpu.CompilerParams(
            collective_id=0, has_side_effects=True, vmem_limit_bytes=48 * 1024 * 1024
        ),
    )(
        in_hbm(hidden_x.reshape(tokens, width)),
        in_hbm(base_weight),
        in_hbm(delta_codes),
        in_hbm(delta_scales.T),
        in_hbm(owner_map),
        in_hbm(kv_cache.reshape(rows * positions, kv_cache.shape[2])),
        in_hbm(queries.reshape(tokens, queries.shape[2])),
        in_hbm(lengths),
    )
    new_kv, attended = pl.pallas_call(
        finish,
        out_shape=(
            jax.ShapeDtypeStruct((tokens, 128), BF16),
            jax.ShapeDtypeStruct((tokens, 512), BF16),
        ),
        in_specs=[vmem, vmem, vmem],
        out_specs=(vmem, vmem),
        compiler_params=pltpu.CompilerParams(vmem_limit_bytes=8 * 1024 * 1024),
    )(fresh, cached, own_query)
    return new_kv.reshape(rows, steps, 128), attended.reshape(rows, steps, 512)


def solution(mesh):
    in_specs = (
        P("group", None, "tensor"),
        P(None, "tensor"),
        P("group", "tensor"),
        P("group", "tensor"),
        P(),
        P("group", "tensor", None),
        P("group", None, None),
        P("group"),
    )
    out_specs = (P("group", None, "tensor"), P("group", None, "tensor"))
    return jax.shard_map(
        on_device, mesh=mesh, in_specs=in_specs, out_specs=out_specs, check_vma=False
    )
```

```python
import functools

import jax
import jax.numpy as jnp
from jax import lax
from jax.experimental import pallas as pl
from jax.experimental.pallas import tpu as pltpu
from jax.sharding import PartitionSpec as P

HD = 128
NEGATIVE = -1e30
LOG2_E = 1.4426950408889634
MESH = pl.DeviceIdType.MESH
F32 = jnp.float32
BF16 = jnp.bfloat16


def nt_dot(a, b):
    return lax.dot_general(a, b, (((1,), (1,)), ((), ())), preferred_element_type=F32)


def kernel(
    NG,
    NT,
    hid_hbm,
    base_hbm,
    codes_hbm,
    scales_hbm,
    owner_hbm,
    cache_hbm,
    query_hbm,
    lengths_hbm,
    fresh_ref,
    cached_ref,
    own_ref,
    hid,
    base,
    codes,
    scales_ref,
    owner_ref,
    lengths_ref,
    cache,
    query,
    weight,
    place,
    odd_place,
    back_send,
    back,
    base_proj,
    proj_send,
    proj,
    part_send,
    part,
    lse_cols,
    load_sem,
    hid_send_sem,
    hid_sem,
    relay_send_sem,
    weight_send_sem,
    weight_sem,
    back_send_sem,
    back_sem,
    proj_send_sem,
    proj_sem,
    part_send_sem,
    part_sem,
    ready_z,
    ready_t,
    ready_x,
    ready_m,
):
    NZ = NG // 4
    NY = NT // 2
    KVH = NT // 2
    POS = cache.shape[0] // 2
    KVW = KVH * HD
    width = hid.shape[2]
    scale = HD ** (-0.5) * LOG2_E
    me_g = lax.axis_index("group")
    me_t = lax.axis_index("tensor")
    core = lax.rem(me_g, 2)
    me_z = lax.rem(me_g // 2, NZ)
    me_m = me_g // (2 * NZ) * 2 + core
    me_y = me_t // 2
    me_x = lax.rem(me_t, 2)

    def group_of(m, z):
        return (m // 2) * (2 * NZ) + z * 2 + lax.rem(m, 2)

    def near_peer(n):
        step = n // 2 + 1
        return lax.rem(me_z + jnp.where(lax.rem(n, 2) == 0, step, NZ - step), NZ)

    def t_peer(i):
        return lax.rem(me_t + i, NT)

    me_q = me_m + 1 - 2 * core

    def m_at(q):
        return q + 1 - 2 * lax.rem(q, 2)

    last_y = NY // 2
    at_last_y = me_y == last_y
    herald = at_last_y & (me_x == 0)
    greeted = me_z + me_q + jnp.where(at_last_y, NY - 1 + me_x, 0)
    barrier = pltpu.get_barrier_semaphore()

    def greet_m(q, c):
        pl.semaphore_signal(
            barrier, inc=1, device_id=(group_of(m_at(q), me_z), me_t), device_id_type=MESH
        )
        return c

    def greet_z(z, c):
        pl.semaphore_signal(
            barrier, inc=1, device_id=(group_of(me_m, z), me_t), device_id_type=MESH
        )
        return c

    def answer_z(z, c):
        pl.semaphore_signal(
            ready_z.at[me_z], inc=1, device_id=(group_of(me_m, z), me_t), device_id_type=MESH
        )
        return c

    def answer_m(q, c):
        pl.semaphore_signal(
            ready_m.at[me_q],
            inc=1,
            device_id=(group_of(m_at(q), me_z), me_t),
            device_id_type=MESH,
        )
        return c

    def answer_t(i, c):
        @pl.when(order_of(t_peer(i)) < order)
        def _():
            pl.semaphore_signal(ready_t, inc=1, device_id=(me_g, t_peer(i)), device_id_type=MESH)

        return c

    loads = [
        pltpu.make_async_copy(codes_hbm, codes, load_sem.at[0]),
        pltpu.make_async_copy(hid_hbm, hid.at[me_z], load_sem.at[1]),
        pltpu.make_async_copy(query_hbm, query, load_sem.at[2]),
        pltpu.make_async_copy(cache_hbm, cache, load_sem.at[3]),
        pltpu.make_async_copy(base_hbm, base, load_sem.at[4]),
        pltpu.make_async_copy(scales_hbm, scales_ref, load_sem.at[5]),
        pltpu.make_async_copy(owner_hbm, owner_ref, load_sem.at[6]),
        pltpu.make_async_copy(lengths_hbm, lengths_ref, load_sem.at[7]),
    ]
    loads[5].start()
    loads[0].start()
    loads[1].start()
    lax.fori_loop(me_q + 1, 4, greet_m, 0)
    lax.fori_loop(me_z + 1, NZ, greet_z, 0)

    @pl.when(jnp.logical_not(at_last_y))
    def _():
        pl.semaphore_signal(
            barrier, inc=1, device_id=(me_g, 2 * last_y + me_x), device_id_type=MESH
        )

    @pl.when(herald)
    def _():
        pl.semaphore_signal(
            barrier, inc=1, device_id=(me_g, 2 * last_y + 1), device_id_type=MESH
        )

    for load in loads[2:5] + loads[6:]:
        load.start()

    @pl.when(greeted > 0)
    def _():
        pl.semaphore_wait(barrier, greeted)

    lax.fori_loop(0, me_q, answer_m, 0)
    lax.fori_loop(0, me_z, answer_z, 0)

    @pl.when(at_last_y & (me_x == 1))
    def _():
        pl.semaphore_signal(ready_x, inc=1, device_id=(me_g, 2 * last_y), device_id_type=MESH)

    unit = (
        lax.broadcasted_iota(jnp.int32, (64, 64), 0) == lax.broadcasted_iota(jnp.int32, (64, 64), 1)
    ).astype(BF16)
    loads[5].wait()
    scale_cols = nt_dot(unit, scales_ref[...])
    loads[0].wait()
    weight[me_m] = jnp.concatenate(
        [
            codes[:, j * 128 : (j + 1) * 128].astype(F32) * scale_cols[:, j : j + 1]
            for j in range(width // 128)
        ],
        axis=1,
    ).astype(BF16)
    loads[1].wait()

    def hid_copy(z):
        return pltpu.make_async_remote_copy(
            src_ref=hid.at[me_z],
            dst_ref=hid.at[me_z],
            send_sem=hid_send_sem.at[z],
            recv_sem=hid_sem.at[me_z],
            device_id=(group_of(me_m, z), me_t),
            device_id_type=MESH,
        )

    def wait_hid(z):
        pltpu.make_async_remote_copy(
            src_ref=hid.at[z],
            dst_ref=hid.at[z],
            send_sem=hid_send_sem.at[z],
            recv_sem=hid_sem.at[z],
            device_id=(group_of(me_m, z), me_t),
            device_id_type=MESH,
        ).wait_recv()

    def weight_copy(q):
        return pltpu.make_async_remote_copy(
            src_ref=weight.at[me_m],
            dst_ref=weight.at[me_m],
            send_sem=weight_send_sem.at[q],
            recv_sem=weight_sem.at[me_m],
            device_id=(group_of(m_at(q), me_z), me_t),
            device_id_type=MESH,
        )

    def start_weight(q):
        @pl.when(q > me_q)
        def _():
            pl.semaphore_wait(ready_m.at[q], 1)

        weight_copy(q).start()

    def wait_weight(i, c):
        q = lax.rem(me_q + i, 4)
        m = m_at(q)
        pltpu.make_async_remote_copy(
            src_ref=weight.at[m],
            dst_ref=weight.at[m],
            send_sem=weight_send_sem.at[q],
            recv_sem=weight_sem.at[m],
            device_id=(group_of(m, me_z), me_t),
            device_id_type=MESH,
        ).wait_recv()
        return c

    def start_hid_earlier(n, c):
        @pl.when(near_peer(n) < me_z)
        def _():
            hid_copy(near_peer(n)).start()

        return c

    middle = NZ // 4
    far = 2 * middle
    relays = (me_z >= middle) & (me_z + middle < NZ) & (middle > 0)

    def straight(z):
        return (z != me_z + far) | (middle == 0)

    def start_hid_later(z, c):
        @pl.when(straight(z))
        def _():
            pl.semaphore_wait(ready_z.at[z], 1)
            hid_copy(z).start()

        return c

    relay_step = jnp.where(me_z < far, max(KVH // 2 - 2, middle - 1), KVH // 2 - 1)

    def relay_copy():
        z = jnp.maximum(me_z - middle, 0)
        return pltpu.make_async_remote_copy(
            src_ref=hid.at[z],
            dst_ref=hid.at[z],
            send_sem=relay_send_sem.at[0],
            recv_sem=hid_sem.at[z],
            device_id=(group_of(me_m, lax.rem(me_z + middle, NZ)), me_t),
            device_id_type=MESH,
        )

    def relay():
        wait_hid(me_z - middle)
        relay_copy().start()

    start_weight(lax.rem(me_q + 2, 4))
    start_weight(3 - me_q)
    start_weight(me_q + 1 - 2 * lax.rem(me_q, 2))

    lax.fori_loop(0, NZ - 1, start_hid_earlier, 0)

    def back_copy(z):
        return pltpu.make_async_remote_copy(
            src_ref=back_send.at[z],
            dst_ref=back.at[pl.ds(me_z * 2, 2)],
            send_sem=back_send_sem.at[z],
            recv_sem=back_sem.at[me_z],
            device_id=(group_of(me_m, z), me_t),
            device_id_type=MESH,
        )

    def products(z):
        product = nt_dot(hid[z], weight[...].reshape(4 * 64, width))
        low = lax.broadcasted_iota(jnp.int32, (8, 128), 1) < 64
        for j in range(2):
            first = product[0:8, j * 128 : (j + 1) * 128]
            second = product[8:16, j * 128 : (j + 1) * 128]
            even = jnp.where(low, first, pltpu.roll(second, 64, 1))
            odd = jnp.where(low, pltpu.roll(first, 64, 1), second)
            back_send[z, j] = jnp.concatenate([even, odd], axis=0).astype(BF16)

    def serve(z):
        @pl.when(jnp.logical_not(relays & (z == me_z - middle)))
        def _():
            wait_hid(z)

        products(z)
        back_copy(z).start()

    def serve_peer(n):
        return lax.rem(me_z + 1 + n, NZ)

    def serve_earlier(n, c):
        @pl.when(serve_peer(n) < me_z)
        def _():
            serve(serve_peer(n))

        return c

    def serve_later(n, c):
        z = serve_peer(n)

        @pl.when((z > me_z) & (z < NZ - 1))
        def _():
            serve(z)

        return c

    last = me_z == NZ - 1

    between = KVH // 2 - 1

    def find(b):
        spot = jnp.int32(0)
        for g in range(NG):
            at = (((g // 2) % NZ) * 2 + g // (2 * NZ)) * 2 + g % 2
            spot = jnp.where(owner_ref[g] == b, jnp.int32(at), spot)
        place[b] = lax.div(spot, jnp.int32(2))
        odd_place[b] = lax.rem(spot, jnp.int32(2))

    lane = lax.broadcasted_iota(jnp.int32, (32, 128), 1)
    position = me_t * POS + lax.broadcasted_iota(jnp.int32, (64, POS), 1)
    own_rows = hid[me_z]
    for load in loads[2:5] + loads[6:]:
        load.wait()

    def tell(i, c):
        pl.semaphore_signal(ready_t, inc=1, device_id=(me_g, t_peer(i)), device_id_type=MESH)
        return c

    def cached(i, columns):
        for n in range(2):
            k = 2 * i + n
            q_both = query[:, pl.ds(pl.multiple_of(k * 1024, 1024), 1024)].astype(F32)
            for r in range(2):
                q = jnp.concatenate(
                    [q_both[r * 8 : (r + 1) * 8, h * HD : (h + 1) * HD] for h in range(8)], axis=0
                ).astype(BF16)
                keys = cache[r * POS : (r + 1) * POS, pl.ds(pl.multiple_of(k * HD, HD), HD)]
                values = cache[
                    r * POS : (r + 1) * POS, pl.ds(pl.multiple_of(KVW + k * HD, HD), HD)
                ]
                scores = jnp.where(position < lengths_ref[r], nt_dot(q, keys) * scale, NEGATIVE)
                peak = jnp.max(scores, axis=1, keepdims=True)
                weights = jnp.exp2(scores - peak)
                total = jnp.sum(weights, axis=1, keepdims=True)
                weighted = jnp.dot(weights.astype(BF16), values, preferred_element_type=F32)
                mean = (weighted * (1.0 / total)).astype(BF16)
                some = me_t * POS < lengths_ref[r]
                log_sum = jnp.where(some, peak + jnp.log2(total), NEGATIVE)
                for half in range(2):
                    dest = 2 * k + half
                    part_send[dest, r * 32 : (r + 1) * 32] = mean[half * 32 : (half + 1) * 32]
                    columns = jnp.where(
                        lane == dest * 8 + r, log_sum[half * 32 : (half + 1) * 32], columns
                    )
            rows = base[pl.ds(pl.multiple_of(k * 256, 256), 256), :]
            tile = nt_dot(own_rows, rows)
            base_proj[2 * k] = tile[:, :128]
            base_proj[2 * k + 1] = tile[:, 128:]
            for m in range(NG // KVH):
                find(k * (NG // KVH) + m)

        @pl.when(me_z + 1 + i < jnp.minimum(NZ - 1, me_z + KVH // 2))
        def _():
            start_hid_later(me_z + 1 + i, 0)

        @pl.when(herald & (i == 0))
        def _():
            pl.semaphore_wait(ready_x, 1)
            lax.fori_loop(1, NT, tell, 0)

        @pl.when(relays & (i == relay_step) & (me_z + middle < NZ - 1))
        def _():
            relay()

        @pl.when(last & (i == 1))
        def _():
            lax.fori_loop(1, 4, wait_weight, 0)

        @pl.when(last & (i >= 1))
        def _():
            serve(i - 1)

        return columns

    lse_cols[...] = jnp.zeros_like(lse_cols)
    lse_cols[0:32] = lax.fori_loop(0, KVH // 2, cached, jnp.zeros((32, 128), F32))

    def part_copy(i):
        dest = t_peer(i)
        return pltpu.make_async_remote_copy(
            src_ref=part_send.at[dest],
            dst_ref=part.at[me_t],
            send_sem=part_send_sem.at[i],
            recv_sem=part_sem.at[me_t],
            device_id=(me_g, dest),
            device_id_type=MESH,
        )

    def start_part(i, c):
        part_copy(i).start()
        return c

    def start_parts():
        logs = lse_cols[...].T[: NT * 8].reshape(NT, 8, 128)
        sub = lax.broadcasted_iota(jnp.int32, (NT, 8, 128), 1)
        high = logs.astype(BF16).astype(F32)
        rest = logs - high
        middle = rest.astype(BF16).astype(F32)
        low = rest - middle
        middle = jnp.concatenate([middle[:, 0:2], middle[:, 0:2], middle[:, 0:4]], axis=1)
        low = jnp.concatenate([low[:, 0:4], low[:, 0:2], low[:, 0:2]], axis=1)
        rows = jnp.where(sub < 2, high, jnp.where(sub < 4, middle, low))
        part_send[:, 64:80] = jnp.concatenate([rows, rows], axis=1).astype(BF16)

        @pl.when(jnp.logical_not(herald))
        def _():
            pl.semaphore_wait(ready_t, 1)

        lax.fori_loop(1, NT, start_part, 0)
        part[me_t] = part_send[me_t]

    parts_first = (me_z < NZ // 2) & (jnp.abs(me_y - last_y) < 2)

    @pl.when(parts_first)
    def _():
        start_parts()

    lax.fori_loop(me_z + KVH // 2, NZ - 1, start_hid_later, 0)

    @pl.when((me_z >= NZ // 2) & (me_z < NZ - 1))
    def _():
        start_hid_later(NZ - 1, 0)

    @pl.when(relays & (me_z + middle == NZ - 1))
    def _():
        relay()

    @pl.when(jnp.logical_not(last) | (between == 0))
    def _():
        lax.fori_loop(1, 4, wait_weight, 0)

    @pl.when(last)
    def _():
        serve(between)
        start_parts()

    lax.fori_loop(jnp.where(last, between + 1, 0), NZ - 1, serve_earlier, 0)

    @pl.when((me_z >= NZ // 2) & jnp.logical_not(last))
    def _():
        start_parts()

    @pl.when(me_z < NZ // 2)
    def _():
        start_hid_later(NZ - 1, 0)

    @pl.when((me_z < NZ // 2) & jnp.logical_not(parts_first))
    def _():
        start_parts()

    lax.fori_loop(0, NZ - 1, serve_later, 0)

    @pl.when(me_z < NZ - 1)
    def _():
        serve(NZ - 1)

    products(me_z)
    back[pl.ds(me_z * 2, 2)] = back_send[me_z]

    def wait_back(n, c):
        z = near_peer(n)
        pltpu.make_async_remote_copy(
            src_ref=back_send.at[z],
            dst_ref=back.at[pl.ds(z * 2, 2)],
            send_sem=back_send_sem.at[z],
            recv_sem=back_sem.at[z],
            device_id=(group_of(me_m, z), me_t),
            device_id_type=MESH,
        ).wait_recv()
        return c

    lax.fori_loop(0, NZ - 1, wait_back, 0)

    low8 = lax.broadcasted_iota(jnp.int32, (8, 128), 1) < 64

    def returned(block):
        both = back[place[block]].astype(F32)
        return jnp.where(odd_place[block] == 0, both[0:8], both[8:16])

    def whole(block):
        a = returned(2 * block)
        b = returned(2 * block + 1)
        first = jnp.where(low8, a, pltpu.roll(b, 64, 1))
        second = jnp.where(low8, pltpu.roll(a, 64, 1), b)
        return base_proj[block] + jnp.concatenate([first, second], axis=0)

    def proj_copy(dest):
        return pltpu.make_async_remote_copy(
            src_ref=proj_send.at[dest],
            dst_ref=proj.at[me_t],
            send_sem=proj_send_sem.at[dest],
            recv_sem=proj_sem.at[me_t],
            device_id=(me_g, dest),
            device_id_type=MESH,
        )

    def far_y(n):
        step = (n + 1) // 2
        return lax.rem(me_y + NY // 2 + jnp.where(lax.rem(n, 2) == 0, step, NY - step), NY)

    def start_proj(n, c):
        y = far_y(n)
        key = whole(y)
        value = whole(KVH + y).astype(BF16)
        key_high = key.astype(BF16)
        key_low = (key - key_high.astype(F32)).astype(BF16)
        for x in range(2):
            dest = 2 * y + x
            proj_send[dest, 0:16] = key_high
            proj_send[dest, 16:32] = key_low
            proj_send[dest, 32:48] = value
            proj_send[dest, 48:64] = whole(dest).astype(BF16)
        proj_copy(2 * y + 1 - me_x).start()

        @pl.when(y != me_y)
        def _():
            proj_copy(2 * y + me_x).start()

        return c

    lax.fori_loop(0, NY, start_proj, 0)
    proj[me_t] = proj_send[me_t]

    def wait_part(i, c):
        u = t_peer(i)
        pltpu.make_async_remote_copy(
            src_ref=part_send.at[u],
            dst_ref=part.at[u],
            send_sem=part_send_sem.at[i],
            recv_sem=part_sem.at[u],
            device_id=(me_g, u),
            device_id_type=MESH,
        ).wait_recv()
        return c

    lax.fori_loop(1, NT, wait_part, 0)
    logs = part[:, 64:80].astype(F32)[:, 0:8]
    logs = (
        logs
        + jnp.concatenate([logs[:, 2:8], logs[:, 0:2]], axis=1)
        + jnp.concatenate([logs[:, 4:8], logs[:, 0:4]], axis=1)
    )
    top = jnp.max(logs, axis=0)
    grown = jnp.exp2(logs - top[None])
    sub = lax.broadcasted_iota(jnp.int32, (8, 128), 0)
    top_down = jnp.concatenate([top[0:2], top[0:2], top[0:4]], axis=0)
    with_top = jnp.where(sub < 2, grown[0], top_down)
    factors = jnp.concatenate([with_top[None], grown[1:]], axis=0).reshape(NT * 8, 128)
    if NT * 8 < 128:
        factors = jnp.concatenate([factors, jnp.zeros((128 - NT * 8, 128), F32)], axis=0)
    factors = factors.T[0:32]
    sums, totals, peaks = [], [], []
    for r in range(2):
        acc = jnp.zeros((32, HD), F32)
        total = jnp.zeros((32, 1), F32)
        for u in range(NT):
            factor = factors[:, u * 8 + r : u * 8 + r + 1]
            acc = acc + factor * part[u, r * 32 : (r + 1) * 32].astype(F32)
            total = total + factor
        sums.append(acc)
        totals.append(total)
        peaks.append(factors[:, 2 + r : 3 + r])
    cached_ref[:, 0:HD] = jnp.concatenate(sums, axis=0)
    half_lane = lax.broadcasted_iota(jnp.int32, (64, 128), 1) < 64
    cached_ref[:, HD : 2 * HD] = jnp.where(
        half_lane, jnp.concatenate(totals, axis=0), jnp.concatenate(peaks, axis=0)
    )
    q_both = query[:, pl.ds(pl.multiple_of(me_t * 512, 512), 512)].astype(F32)
    own_ref[...] = jnp.concatenate(
        [
            q_both[r * 8 : (r + 1) * 8, h * HD : (h + 1) * HD]
            for r in range(2)
            for h in range(4)
        ],
        axis=0,
    ).astype(BF16)

    def sent_z(n, c):
        z = near_peer(n)

        @pl.when(straight(z))
        def _():
            hid_copy(z).wait_send()

        @pl.when(jnp.logical_not(straight(z)))
        def _():
            pl.semaphore_wait(ready_z.at[z], 1)

        back_copy(z).wait_send()
        return c

    def sent_m(i, c):
        weight_copy(lax.rem(me_q + i, 4)).wait_send()
        return c

    def sent_t(i, c):
        part_copy(i).wait_send()
        proj_copy(t_peer(i)).wait_send()
        return c

    lax.fori_loop(0, NZ - 1, sent_z, 0)

    @pl.when(relays)
    def _():
        relay_copy().wait_send()

    lax.fori_loop(1, 4, sent_m, 0)
    lax.fori_loop(1, NT, sent_t, 0)

    def wait_proj(i, c):
        u = lax.rem(2 * (last_y + 1) + i, NT)

        @pl.when(u != me_t)
        def _():
            pltpu.make_async_remote_copy(
                src_ref=proj_send.at[u],
                dst_ref=proj.at[u],
                send_sem=proj_send_sem.at[u],
                recv_sem=proj_sem.at[u],
                device_id=(me_g, u),
                device_id_type=MESH,
            ).wait_recv()

        return c

    lax.fori_loop(0, NT, wait_proj, 0)
    summed = jnp.sum(proj[...].astype(F32), axis=0)
    fresh_ref[0] = (summed[0:16] + summed[16:32]).astype(BF16)
    fresh_ref[1] = summed[32:48].astype(BF16)
    fresh_ref[2] = summed[48:64].astype(BF16)


def finish(fresh_ref, cached_ref, own_ref, new_ref, att_ref):
    scale = HD ** (-0.5) * LOG2_E
    new_ref[...] = fresh_ref[2]
    cache_sum = cached_ref[:, 0:HD]
    cache_total = cached_ref[:, HD : HD + 1]
    cache_peak = cached_ref[:, HD + 64 : HD + 65]
    near = nt_dot(own_ref[...], fresh_ref[0]) * scale
    at = lax.broadcasted_iota(jnp.int32, (64, 16), 0)
    to = lax.broadcasted_iota(jnp.int32, (64, 16), 1)
    causal = (at // 32 == to // 8) & (lax.rem(at, 8) >= lax.rem(to, 8))
    near = jnp.where(causal, near, NEGATIVE)
    near_peak = jnp.max(near, axis=1, keepdims=True)
    near_weights = jnp.exp2(near - near_peak)
    near_total = jnp.sum(near_weights, axis=1, keepdims=True)
    near_sum = jnp.dot(near_weights.astype(BF16), fresh_ref[1], preferred_element_type=F32)
    joined = jnp.maximum(cache_peak, near_peak)
    cache_scale = jnp.exp2(cache_peak - joined)
    near_scale = jnp.exp2(near_peak - joined)
    numerator = cache_sum * cache_scale + near_sum * near_scale
    denominator = cache_total * cache_scale + near_total * near_scale
    result = numerator / denominator
    att_ref[...] = jnp.concatenate(
        [
            jnp.concatenate(
                [result[r * 32 + h * 8 : r * 32 + h * 8 + 8] for h in range(4)], axis=1
            )
            for r in range(2)
        ],
        axis=0,
    ).astype(BF16)


def on_device(
    hidden_x, base_weight, delta_codes, delta_scales, owner_map, kv_cache, queries, lengths
):
    NG = lax.axis_size("group")
    NT = lax.axis_size("tensor")
    NZ = NG // 4
    rows, steps, width = hidden_x.shape
    tokens = rows * steps
    positions = kv_cache.shape[1]
    any_space = pl.BlockSpec(memory_space=pl.ANY)
    vmem = pl.BlockSpec(memory_space=pltpu.VMEM)
    dma = pltpu.SemaphoreType.DMA

    def in_hbm(x):
        return pltpu.with_memory_space_constraint(x, pltpu.HBM)

    fresh, cached, own_query = pl.pallas_call(
        functools.partial(kernel, NG, NT),
        out_shape=(
            pltpu.VMEM((3, tokens, 128), BF16),
            pltpu.VMEM((64, 256), F32),
            pltpu.VMEM((64, 128), BF16),
        ),
        in_specs=[any_space] * 8,
        out_specs=(vmem, vmem, vmem),
        scratch_shapes=[
            pltpu.VMEM((NZ, tokens, width), BF16),
            pltpu.VMEM(base_weight.shape, BF16),
            pltpu.VMEM(delta_codes.shape, BF16),
            pltpu.VMEM(delta_scales.shape[::-1], BF16),
            pltpu.SMEM(owner_map.shape, jnp.int32),
            pltpu.SMEM(lengths.shape, jnp.int32),
            pltpu.VMEM((rows * positions, kv_cache.shape[2]), BF16),
            pltpu.VMEM((tokens, queries.shape[2]), BF16),
            pltpu.VMEM((4, 64, width), BF16),
            pltpu.SMEM((NG,), jnp.int32),
            pltpu.SMEM((NG,), jnp.int32),
            pltpu.VMEM((NZ, 2, 16, 128), BF16),
            pltpu.VMEM((NZ * 2, 16, 128), BF16),
            pltpu.VMEM((NT, tokens, 128), F32),
            pltpu.VMEM((NT, 4 * tokens, 128), BF16),
            pltpu.VMEM((NT, 4 * tokens, 128), BF16),
            pltpu.VMEM((NT, 80, HD), BF16),
            pltpu.VMEM((NT, 80, HD), BF16),
            pltpu.VMEM((128, 128), F32),
            dma((8,)),
            dma((NZ,)),
            dma((NZ,)),
            dma((1,)),
            dma((4,)),
            dma((4,)),
            dma((NZ,)),
            dma((NZ,)),
            dma((NT,)),
            dma((NT,)),
            dma((NT,)),
            dma((NT,)),
            pltpu.SemaphoreType.REGULAR((NZ,)),
            pltpu.SemaphoreType.REGULAR,
            pltpu.SemaphoreType.REGULAR,
            pltpu.SemaphoreType.REGULAR((4,)),
        ],
        compiler_params=pltpu.CompilerParams(
            collective_id=0, has_side_effects=True, vmem_limit_bytes=48 * 1024 * 1024
        ),
    )(
        in_hbm(hidden_x.reshape(tokens, width)),
        in_hbm(base_weight),
        in_hbm(delta_codes),
        in_hbm(delta_scales.T),
        in_hbm(owner_map),
        in_hbm(kv_cache.reshape(rows * positions, kv_cache.shape[2])),
        in_hbm(queries.reshape(tokens, queries.shape[2])),
        in_hbm(lengths),
    )
    new_kv, attended = pl.pallas_call(
        finish,
        out_shape=(
            jax.ShapeDtypeStruct((tokens, 128), BF16),
            jax.ShapeDtypeStruct((tokens, 512), BF16),
        ),
        in_specs=[vmem, vmem, vmem],
        out_specs=(vmem, vmem),
        compiler_params=pltpu.CompilerParams(vmem_limit_bytes=8 * 1024 * 1024),
    )(fresh, cached, own_query)
    return new_kv.reshape(rows, steps, 128), attended.reshape(rows, steps, 512)


def solution(mesh):
    in_specs = (
        P("group", None, "tensor"),
        P(None, "tensor"),
        P("group", "tensor"),
        P("group", "tensor"),
        P(),
        P("group", "tensor", None),
        P("group", None, None),
        P("group"),
    )
    out_specs = (P("group", None, "tensor"), P("group", None, "tensor"))
    return jax.shard_map(
        on_device, mesh=mesh, in_specs=in_specs, out_specs=out_specs, check_vma=False
    )
```
